32 devices in a mesh: seq: 16 (over z, y, core), batch: 2 (over x).
Axes of the slice: x: 2, y: 2, z: 4, core: 2. Of those that a mesh axis runs over, the one named last changes fastest.
Arguments:
- inputs: bfloat16 [2, 8192, 1024], P('batch', 'seq'), may hold values from -6 to 6
- lengths: int32 [2], P('batch'), may hold values from 7937 to 8192, as said below
- norm_one_gain: bfloat16 [1024], replicated, may hold values from 0.099609375 to 1.8984375
- w_in: bfloat16 [1024, 3072], P(('seq', 'batch')), may hold values from -0.1875 to 0.1875
- conv_weight: bfloat16 [3, 1024], replicated, may hold values from -3 to 3
- w_out: bfloat16 [1024, 1024], P(('seq', 'batch')), may hold values from -0.1875 to 0.1875
- norm_two_gain: bfloat16 [1024], replicated, may hold values from 0.099609375 to 1.8984375
- w_gate: bfloat16 [1024, 4608], P('seq', 'batch'), may hold values from -0.1875 to 0.1875
- w_up: bfloat16 [1024, 4608], P('seq', 'batch'), may hold values from -0.1875 to 0.1875
- w_down: bfloat16 [4608, 1024], P('batch', 'seq'), may hold values from -0.1875 to 0.1875
- cotangent: bfloat16 [2, 8192, 1024], P('batch', 'seq'), may hold values from -6 to 6
Outputs:
- result: bfloat16 [2, 8192, 1024], P('batch', 'seq')
- grad_inputs: float32 [2, 8192, 1024], P('batch', 'seq')
- grad_norm_one: float32 [1024], replicated
- grad_w_in: float32 [1024, 3072], P(('seq', 'batch'))
- grad_conv: float32 [3, 1024], replicated
- grad_w_out: float32 [1024, 1024], P(('seq', 'batch'))
- grad_norm_two: float32 [1024], replicated
- grad_w_gate: float32 [1024, 4608], P('seq', 'batch')
- grad_w_up: float32 [1024, 4608], P('seq', 'batch')
- grad_w_down: float32 [4608, 1024], P('batch', 'seq')
The draws below stay inside these ranges and needn't reach their ends.
Inputs may be any that keep to these rules, and one draw needn't show every extreme that they name: `lengths`: one sequence has length exactly 8192; every length is above 7936.
All inputs are finite; a program needn't handle non-finite values.
Results may differ from the reference program's by a relative error of at most 0.024.
Values may be sent and summed in bfloat16 or wider, within the bound.
A program may use at most 256 MiB of HBM per device.

```python
import math
import jax
import jax.numpy as jnp
from jax import lax

D = 1024
FF = 4608
KERNEL = 3
TOK_DEV = 512
LENGTH = 8192
BATCH = 2


def draw_lengths(key, part):
    key = jax.random.fold_in(key, 11)
    first_key, second_key = jax.random.split(key)
    shortfall = jax.random.randint(first_key, (BATCH,), 0, TOK_DEV // 2)
    full_row = jax.random.randint(second_key, (), 0, BATCH)
    shortfall = jnp.where(jnp.arange(BATCH) == full_row, 0, shortfall)
    return (LENGTH - shortfall).astype(jnp.int32)


def levels(key, extent, cuts, low, top_value):
    gain = 1.0
    for axis_at, blocks in cuts:
        heights = jax.random.uniform(jax.random.fold_in(jax.random.fold_in(key, 6), axis_at), (blocks,), jnp.float32, low / len(cuts), top_value / len(cuts))
        gain = gain * jnp.repeat(jnp.exp(heights), extent[axis_at] // blocks).reshape((-1,) + (1,) * (len(extent) - 1 - axis_at))
    return gain


def bell_draw(rng, shape, spread, reach, cuts=(), kind=jnp.bfloat16):
    array = jax.random.normal(rng, shape, jnp.float32) * spread
    if len(cuts) > 0:
        array = levels(rng, shape, cuts, -0.22, 0.18) * array
    return jnp.clip(array, min=-reach, max=reach).astype(kind)


def setup_inputs(seed: int = 0) -> dict:
    key_of = jax.random.split(jax.random.key(seed), 12)
    return {
        "inputs": bell_draw(key_of[0], (BATCH, LENGTH, D), 1.0, 6.0, ((0, 2), (1, 16))),
        "lengths": draw_lengths(jax.random.fold_in(key_of[11], 71), 0),
        "norm_one_gain": jnp.clip(1.0 + 0.18 * jax.random.normal(key_of[2], (D,), jnp.float32), 0.099609375, 1.8984375).astype(jnp.bfloat16),
        "w_in": bell_draw(key_of[3], (D, 3 * D), D ** -0.5, 0.1875, ((0, 32),)),
        "conv_weight": bell_draw(key_of[4], (KERNEL, D), 0.6, 3.0),
        "w_out": bell_draw(key_of[5], (D, D), D ** -0.5, 0.1875, ((0, 32),)),
        "norm_two_gain": jnp.clip(1.0 + 0.18 * jax.random.normal(key_of[6], (D,), jnp.float32), 0.099609375, 1.8984375).astype(jnp.bfloat16),
        "w_gate": bell_draw(key_of[7], (D, FF), D ** -0.5, 0.1875, ((0, 16), (1, 2))),
        "w_up": bell_draw(key_of[8], (D, FF), D ** -0.5, 0.1875, ((0, 16), (1, 2))),
        "w_down": bell_draw(key_of[9], (FF, D), (FF // 4) ** -0.5, 0.1875, ((0, 2), (1, 16))),
        "cotangent": bell_draw(key_of[10], (BATCH, LENGTH, D), 1.0, 6.0, ((0, 2), (1, 16))),
    }


@jax.custom_vjp
def low(v):
    return lax.optimization_barrier(v.astype(jnp.bfloat16)).astype(jnp.float32)

@jax.custom_vjp
def low_back(v):
    return v

def low_keep(v):
    return (low(v), None)

def low_pass(kept, grad):
    return (grad,)

def back_keep(v):
    return (v, None)

def back_low(kept, grad):
    return (low(grad),)
low.defvjp(low_keep, low_pass)
low_back.defvjp(back_keep, back_low)
epsilon = 1e-05

def exact_dot(left, right):
    return jnp.dot(left, right, precision=lax.Precision.HIGHEST, preferred_element_type=jnp.float32)

def rms_scaled(values):
    return values * lax.rsqrt(lax.optimization_barrier(jnp.mean(values * values, axis=-1, keepdims=True)) + epsilon)

def blockwise(function, arrays, block_rows):
    shaped = tuple((a.reshape((a.shape[0] // block_rows, block_rows) + a.shape[1:]) for a in arrays))
    mapped = lax.map(jax.checkpoint(lambda pieces: function(*pieces)), shaped)
    return mapped.reshape((arrays[0].shape[0], mapped.shape[-1]))

def forward(inputs, gain_one, w_in, kernel, w_out, gain_two, w_gate, w_up, w_down, valid):
    batch_rows, seq_len, feat_width = inputs.shape
    flat_inputs = inputs.reshape(batch_rows * seq_len, feat_width)
    block_rows = math.gcd(batch_rows * seq_len, 4096)

    def first_part(tok_rows):
        return low_back(exact_dot(low(rms_scaled(tok_rows) * gain_one), w_in))
    projected = blockwise(first_part, (flat_inputs,), block_rows).reshape(batch_rows, seq_len, 3 * feat_width)
    b_part = projected[..., :feat_width]
    c_part = projected[..., feat_width:2 * feat_width]
    v_part = projected[..., 2 * feat_width:]
    product = low(b_part * v_part)
    extended = jnp.pad(product, ((0, 0), (2, 0), (0, 0)))
    conv_out = kernel[0] * extended[:, :seq_len] + kernel[1] * extended[:, 1:seq_len + 1] + kernel[2] * extended[:, 2:]
    gated_mix = low(c_part * conv_out).reshape(batch_rows * seq_len, feat_width)

    def second_part(tok_rows, gated_rows, valid_rows):
        mixer_out = low_back(exact_dot(gated_rows, w_out))
        middle = tok_rows + valid_rows * mixer_out
        normed_two = low(rms_scaled(middle) * gain_two)
        gate_val = low_back(exact_dot(normed_two, w_gate))
        up_val = low_back(exact_dot(normed_two, w_up))
        hidden = low(jax.nn.silu(gate_val) * up_val)
        ffn_out = low_back(exact_dot(hidden, w_down))
        return middle + valid_rows * ffn_out
    result = blockwise(second_part, (flat_inputs, gated_mix, valid), block_rows)
    return result.reshape(batch_rows, seq_len, feat_width)

def reference(inputs, lengths, norm_one_gain, w_in, conv_weight, w_out, norm_two_gain, w_gate, w_up, w_down, cotangent):
    batch_rows, seq_len, feat_width = inputs.shape
    position = jnp.arange(seq_len, dtype=jnp.int32)
    valid = (position[None, :] < lengths[:, None]).astype(jnp.float32).reshape(batch_rows * seq_len, 1)
    params = tuple((a.astype(jnp.float32) for a in (inputs, norm_one_gain, w_in, conv_weight, w_out, norm_two_gain, w_gate, w_up, w_down)))

    def wrapped(*values):
        return forward(*values, valid)
    result, pullback = jax.vjp(wrapped, *params)
    grads = pullback(cotangent.astype(jnp.float32))
    return (result.astype(jnp.bfloat16), grads[0], grads[1], grads[2], grads[3], grads[4], grads[5], grads[6], grads[7], grads[8])
```

```python
import functools

import jax
import jax.numpy as jnp
from jax import lax
from jax.experimental import pallas as pl
from jax.experimental.pallas import tpu as pltpu
from jax.sharding import PartitionSpec as P

epsilon = 1e-05
MESH = pl.DeviceIdType.MESH
F32, BF16 = jnp.float32, jnp.bfloat16
DEPTH = 4
PARTS = (512, 384, 256)


def over_rows(left, right):
    return lax.dot_general(
        left, right, (((0,), (0,)), ((), ())), preferred_element_type=F32
    )


def by_rows(left, right):
    return lax.dot_general(
        left, right, (((1,), (1,)), ((), ())), preferred_element_type=F32
    )


def dot(left, right):
    return jnp.dot(left, right, preferred_element_type=F32)


def rounded_dot(left, right):
    return dot(left, right).astype(BF16).astype(F32)


class Place:
    def __init__(self):
        self.s = lax.axis_index("seq")
        self.x = lax.axis_index("batch")
        self.z = self.s // 4
        self.y = (self.s // 2) % 2
        self.c = self.s % 2
        self.own = {"y": self.y, "c": self.c, "x": self.x}
        self.device = {
            "c": (self.s + 1 - 2 * self.c, self.x),
            "y": (self.s + 2 - 4 * self.y, self.x),
            "x": (self.s, 1 - self.x),
            "up": (self.s + 4, self.x),
            "down": (self.s - 4, self.x),
            "pair": (self.s + 4 - 8 * (self.z % 2), self.x),
            "far": (self.s + 8 - 16 * (self.z // 2), self.x),
        }

    def greet(self, names):
        barrier = pltpu.get_barrier_semaphore()
        ends = {"up": self.z < DEPTH - 1, "down": self.z > 0}

        def signal(name):
            pl.semaphore_signal(
                barrier, inc=1, device_id=self.device[name], device_id_type=MESH
            )

        expected = 0
        for name in names:
            if name in ends:
                pl.when(ends[name])(functools.partial(signal, name))
                expected = expected + ends[name].astype(jnp.int32)
            else:
                signal(name)
                expected = expected + 1
        pl.semaphore_wait(barrier, expected)


class Links:
    def __init__(self, place, send, recv):
        self.place, self.send, self.recv = place, send, recv
        self.used = 0

    def take(self, count):
        first = self.used
        self.used += count
        return first

    def copy(self, source, target, index, name):
        return pltpu.make_async_remote_copy(
            src_ref=source,
            dst_ref=target,
            send_sem=self.send.at[index],
            recv_sem=self.recv.at[index],
            device_id=self.place.device[name],
            device_id_type=MESH,
        )


class Gather:
    def __init__(self, links, view, stages):
        self.links, self.view, self.stages = links, view, stages
        self.place = links.place
        self.rows = {name: links.take(DEPTH) for name in ["up", "down"] + stages}

    def block(self, stage, level, theirs=False):
        where = dict(self.place.own)
        if stage is not None:
            for name in self.stages[:stage]:
                where[name] = slice(None)
            if theirs:
                where[self.stages[stage]] = 1 - where[self.stages[stage]]
        return self.view(level, where["y"], where["c"], where["x"])

    def line(self, name, level):
        ref = self.block(None, level)
        return self.links.copy(ref, ref, self.rows[name] + level, name)

    def staged(self, stage, level, theirs=False):
        name = self.stages[stage]
        ref = self.block(stage, level, theirs)
        return self.links.copy(ref, ref, self.rows[name] + level, name)

    def begin(self):
        z = self.place.z

        @pl.when(z < DEPTH - 1)
        def _():
            self.line("up", z).start()

        @pl.when(z > 0)
        def _():
            self.line("down", z).start()

        self.staged(0, z).start()

    def along(self, distance):
        z = self.place.z

        @pl.when(z >= distance)
        def _():
            level = z - distance
            self.line("up", level).wait_recv()

            @pl.when(z < DEPTH - 1)
            def _():
                self.line("up", level).start()

            self.staged(0, level).start()

        @pl.when(z + distance < DEPTH)
        def _():
            level = z + distance
            self.line("down", level).wait_recv()

            @pl.when(z > 0)
            def _():
                self.line("down", level).start()

            self.staged(0, level).start()

    def across(self, stage, distance):
        z = self.place.z

        def pass_on(level):
            self.staged(stage, level, True).wait_recv()
            if stage + 1 < len(self.stages):
                self.staged(stage + 1, level).start()

        if distance == 0:
            pass_on(z)
            return
        pl.when(z >= distance)(lambda: pass_on(z - distance))
        pl.when(z + distance < DEPTH)(lambda: pass_on(z + distance))

    def steps(self):
        found = []
        count = len(self.stages)
        for time in range(DEPTH + count):
            for stage in range(count, 0, -1):
                if 0 <= time - stage < DEPTH:
                    found.append(functools.partial(self.across, stage - 1, time - stage))
            if 0 < time < DEPTH:
                found.append(functools.partial(self.along, time))
        return found

    def drain(self):
        z = self.place.z
        for level in range(DEPTH):

            @pl.when((z >= level) & (z < DEPTH - 1))
            def _():
                self.line("up", level).wait_send()

            @pl.when((z <= level) & (z > 0))
            def _():
                self.line("down", level).wait_send()

            for stage in range(len(self.stages)):
                self.staged(stage, level).wait_send()


def add_into(target, source):
    target[...] = (target[...].astype(F32) + source[...].astype(F32)).astype(BF16)


class Reduce:
    def __init__(self, links, view, stages, slots, line_slots):
        self.links, self.view, self.stages = links, view, stages
        self.slots, self.line_slots = slots, line_slots
        self.place = links.place
        self.rows = {name: links.take(DEPTH) for name in ["up", "down"] + stages}

    def block(self, stage, level, theirs=False):
        where = dict(self.place.own)
        for name in self.stages[stage + 1 :]:
            where[name] = slice(None)
        if theirs:
            where[self.stages[stage]] = 1 - where[self.stages[stage]]
        return self.view(level, where["y"], where["c"], where["x"])

    def staged(self, stage, level):
        name = self.stages[stage]
        return self.links.copy(
            self.block(stage, level, True),
            self.slots[stage].at[level],
            self.rows[name] + level,
            name,
        )

    def line(self, name, level):
        slot = level if name == "down" else level + 1
        return self.links.copy(
            self.block(len(self.stages) - 1, level),
            self.line_slots.at[slot],
            self.rows[name] + level,
            name,
        )

    def levels(self, distance, action):
        z = self.place.z
        if distance == 0:
            action(z)
            return
        pl.when(z >= distance)(lambda: action(z - distance))
        pl.when(z + distance < DEPTH)(lambda: action(z + distance))

    def begin(self, distance):
        self.levels(distance, lambda level: self.staged(0, level).start())

    def across(self, stage, distance):
        def take(level):
            self.staged(stage, level).wait_recv()
            add_into(self.block(stage, level), self.slots[stage].at[level])
            if stage + 1 < len(self.stages):
                self.staged(stage + 1, level).start()

        self.levels(distance, take)

    def take(self, name, level):
        self.line(name, level).wait_recv()
        slot = level if name == "down" else level + 1
        add_into(
            self.block(len(self.stages) - 1, level), self.line_slots.at[slot]
        )

    def along(self, distance):
        z = self.place.z
        if distance == 0:
            pl.when(z < DEPTH - 1)(lambda: self.take("down", z))
            pl.when(z > 0)(lambda: self.take("up", z))
            return

        @pl.when(z >= distance)
        def _():
            level = z - distance
            pl.when(z < DEPTH - 1)(lambda: self.take("down", level))
            self.line("down", level).start()

        @pl.when(z + distance < DEPTH)
        def _():
            level = z + distance
            pl.when(z > 0)(lambda: self.take("up", level))
            self.line("up", level).start()

    def steps(self):
        found = []
        count = len(self.stages)
        for time in range(DEPTH + count):
            for stage in range(count, -1, -1):
                if 0 <= time - stage < DEPTH:
                    distance = DEPTH - 1 - (time - stage)
                    if stage == count:
                        found.append(functools.partial(self.along, distance))
                    else:
                        found.append(functools.partial(self.across, stage, distance))
        return found

    def drain(self):
        z = self.place.z
        for level in range(DEPTH):

            @pl.when(z > level)
            def _():
                self.line("down", level).wait_send()

            @pl.when(z < level)
            def _():
                self.line("up", level).wait_send()

            for stage in range(len(self.stages)):
                self.staged(stage, level).wait_send()


def gather_kernel(mixer_ref, f0_ref, f1_ref, f2_ref, wm, w0, w1, w2, send, recv):
    place = Place()
    links = Links(place, send, recv)
    half = mixer_ref.shape[1] // 2
    parts = [
        Gather(
            links,
            lambda z, y, c, x: wm.at[z, y, c, x, :, pl.ds(0, half)],
            ["y", "x", "c"],
        ),
        Gather(
            links,
            lambda z, y, c, x: wm.at[z, y, c, x, :, pl.ds(half, half)],
            ["x", "y", "c"],
        ),
    ]
    ffn = []
    for buffer in (w0, w1, w2):
        ffn.append(Gather(links, lambda z, y, c, x, b=buffer: b.at[z, y], ["y"]))
    twins = []
    for source, target in ((f0_ref, w0), (f1_ref, w1), (f2_ref, w2)):
        twins.append(
            links.copy(
                source.at[1 - place.c],
                target.at[place.z, place.y, place.c],
                links.take(1),
                "c",
            )
        )
    place.greet(["c", "y", "x", "up", "down"])
    wm[place.z, place.y, place.c, place.x] = mixer_ref[...]
    for part in parts:
        part.begin()
    for twin in twins:
        twin.start()
    for source, target in ((f0_ref, w0), (f1_ref, w1), (f2_ref, w2)):
        target[place.z, place.y, place.c] = source[place.c]
    first, second = parts[0].steps(), parts[1].steps()
    for step_one, step_two in zip(first, second):
        step_one()
        step_two()
    for twin, part in zip(twins, ffn):
        twin.wait_recv()
        part.begin()
        for step in part.steps():
            step()
    for part in parts + ffn:
        part.drain()
    for twin in twins:
        twin.wait_send()


def gather_all(mixer, ffn):
    columns = mixer.shape[1]
    shapes = [jax.ShapeDtypeStruct((DEPTH, 2, 2, 2, 32, columns), BF16)]
    for block in ffn:
        shapes.append(
            jax.ShapeDtypeStruct((DEPTH, 2, 2, 64, block.shape[2]), BF16)
        )
    vmem = pl.BlockSpec(memory_space=pltpu.VMEM)
    return pl.pallas_call(
        gather_kernel,
        out_shape=shapes,
        in_specs=[vmem] * 4,
        out_specs=[vmem] * 4,
        scratch_shapes=[
            pltpu.SemaphoreType.DMA((96,)),
            pltpu.SemaphoreType.DMA((96,)),
        ],
        compiler_params=pltpu.CompilerParams(
            collective_id=0, has_side_effects=True, vmem_limit_bytes=40 * 2**20
        ),
    )(mixer, *ffn)


def ffn_kernel(
    normed_ref,
    grad_ref,
    w0_ref,
    w1_ref,
    w2_ref,
    out_ref,
    back_ref,
    d0_ref,
    d1_ref,
    d2_ref,
    tokens,
    grads,
    tokens_t,
    grads_t,
    w0,
    w1,
    w2,
    r0,
    r1,
    r2,
    l0,
    l1,
    l2,
    hidden,
    slopes,
    out_sum,
    back_sum,
    out_slots,
    back_slots,
    e0,
    e1,
    e2,
    load_sem,
    send,
    recv,
):
    place = Place()
    links = Links(place, send, recv)
    rows = normed_ref.shape[0]
    weights = (w0, w1, w2)
    loads = [
        pltpu.make_async_copy(source, target, load_sem.at[i])
        for i, (source, target) in enumerate(
            zip((w0_ref, w1_ref, w2_ref), weights)
        )
    ]
    for load in loads:
        load.start()

    def share(buffer):
        first = links.take(3)
        return (
            links.copy(buffer.at[0], buffer.at[1], first, "c"),
            links.copy(buffer.at[0], buffer.at[2], first + 1, "x"),
            links.copy(buffer.at[2], buffer.at[3], first + 2, "c"),
        )

    def give_back(total, slots):
        first = links.take(3)
        return (
            links.copy(total.at[3], slots.at[2], first, "c"),
            links.copy(total.at[2], slots.at[1], first + 1, "x"),
            links.copy(total.at[1], slots.at[0], first + 2, "c"),
        )

    shared = [share(tokens), share(grads)]
    returned = [give_back(back_sum, back_slots), give_back(out_sum, out_slots)]
    reduces = [
        Reduce(links, lambda z, y, c, x, b=w: b.at[z, y], ["y"], [r], l)
        for w, r, l in zip(weights, (r0, r1, r2), (l0, l1, l2))
    ]
    twins = links.take(3)
    place.greet(["c", "y", "x", "up", "down"])
    tokens[0] = normed_ref[...]
    grads[0] = grad_ref[...]
    for group in shared:
        group[1].start()
        group[0].start()
    for group in shared:
        group[1].wait_recv()
        group[2].start()
    for group in shared:
        group[0].wait_recv()
        group[2].wait_recv()
    for load in loads:
        load.wait()

    def flip(i, carry):
        tokens_t[:, pl.ds(pl.multiple_of(i * rows, rows), rows)] = tokens[i].T
        grads_t[:, pl.ds(pl.multiple_of(i * rows, rows), rows)] = grads[i].T
        return carry

    lax.fori_loop(0, 4, flip, 0)
    depth = tokens_t.shape[0]
    for number, (weight, width) in enumerate(zip(weights, PARTS)):

        def block(i, carry, weight=weight, width=width, number=number):
            gate_up = weight[..., : 2 * width].reshape(depth, 2 * width)
            both = dot(tokens[i], gate_up).astype(BF16).astype(F32)
            gate, up = both[:, :width], both[:, width:]
            sigmoid = jax.nn.sigmoid(gate)
            silu = gate * sigmoid
            slope = sigmoid * (1.0 + gate * (1.0 - sigmoid))
            kept = (silu * up).astype(BF16)
            down = weight[..., 2 * width :].reshape(depth, width)
            grad_hidden = dot(grads[i], down)
            grad_gate = (grad_hidden * up * slope).astype(BF16)
            grad_up = (grad_hidden * silu).astype(BF16)
            where = pl.ds(pl.multiple_of(i * rows, rows), rows)
            hidden[where, :width] = kept
            slopes[where, :width] = grad_gate
            slopes[where, width : 2 * width] = grad_up
            out_part = by_rows(kept, down)
            back_part = by_rows(slopes[where, : 2 * width], gate_up)
            if number == 0:
                out_sum[i] = out_part.astype(BF16)
                back_sum[i] = back_part.astype(BF16)
            else:
                out_sum[i] = (out_sum[i].astype(F32) + out_part).astype(BF16)
                back_sum[i] = (back_sum[i].astype(F32) + back_part).astype(BF16)
            return carry

        lax.fori_loop(0, 4, block, 0)
        step = 256
        for start in range(0, 2 * width, step):
            part = dot(tokens_t[...], slopes[:, start : start + step])
            weight[..., start : start + step] = part.astype(BF16).reshape(
                weight.shape[:-1] + (step,)
            )
        for start in range(0, width, step):
            size = min(step, width - start)
            part = dot(grads_t[...], hidden[:, start : start + size])
            weight[..., 2 * width + start : 2 * width + start + size] = part.astype(
                BF16
            ).reshape(weight.shape[:-1] + (size,))
        for distance in (3, 2, 1, 0):
            reduces[number].begin(distance)

    for total, slots, group in zip(
        (back_sum, out_sum), (back_slots, out_slots), returned
    ):
        group[0].start()
        group[2].start()
    for total, slots, group in zip(
        (back_sum, out_sum), (back_slots, out_slots), returned
    ):
        group[0].wait_recv()
        add_into(total.at[2], slots.at[2])
        group[1].start()
    for reduce in reduces:
        for action in reduce.steps():
            action()
    for total, slots, group, target in zip(
        (back_sum, out_sum),
        (back_slots, out_slots),
        returned,
        (back_ref, out_ref),
    ):
        group[1].wait_recv()
        group[2].wait_recv()
        target[...] = (
            total[0].astype(F32) + slots[0].astype(F32) + slots[1].astype(F32)
        )
    exchanges = []
    for number, (weight, edge, target) in enumerate(
        zip(weights, (e0, e1, e2), (d0_ref, d1_ref, d2_ref))
    ):
        edge[...] = weight[place.z, place.y, 1 - place.c]
        exchange = links.copy(
            edge, target.at[place.c], twins + number, "c"
        )
        exchange.start()
        target[place.c] = weight[place.z, place.y, place.c]
        exchanges.append(exchange)
    for exchange in exchanges:
        exchange.wait()
    for reduce in reduces:
        reduce.drain()
    for group in shared + returned:
        for copy in group:
            copy.wait_send()


def ffn_all(normed, grad, weights):
    rows, depth = normed.shape
    vmem = pl.BlockSpec(memory_space=pltpu.VMEM)
    hbm = pl.BlockSpec(memory_space=pl.ANY)
    out_shape = [
        jax.ShapeDtypeStruct((rows, depth), F32),
        jax.ShapeDtypeStruct((rows, depth), F32),
    ] + [jax.ShapeDtypeStruct((2, 64, 3 * w), BF16) for w in PARTS]
    block = (128 // 64, 64)
    scratch = (
        [pltpu.VMEM((4, rows, depth), BF16)] * 2
        + [pltpu.VMEM((depth, 4 * rows), BF16)] * 2
        + [pltpu.VMEM((DEPTH, 2) + block + (3 * w,), BF16) for w in PARTS]
        + [pltpu.VMEM((DEPTH,) + block + (3 * w,), BF16) for w in PARTS]
        + [pltpu.VMEM((DEPTH + 1,) + block + (3 * w,), BF16) for w in PARTS]
        + [
            pltpu.VMEM((4 * rows, PARTS[0]), BF16),
            pltpu.VMEM((4 * rows, 2 * PARTS[0]), BF16),
        ]
        + [pltpu.VMEM((4, rows, depth), BF16)] * 2
        + [pltpu.VMEM((3, rows, depth), BF16)] * 2
        + [pltpu.VMEM((64, 3 * w), BF16) for w in PARTS]
        + [
            pltpu.SemaphoreType.DMA((3,)),
            pltpu.SemaphoreType.DMA((64,)),
            pltpu.SemaphoreType.DMA((64,)),
        ]
    )
    return pl.pallas_call(
        ffn_kernel,
        out_shape=out_shape,
        in_specs=[vmem, vmem, hbm, hbm, hbm],
        out_specs=[vmem] * 5,
        scratch_shapes=scratch,
        compiler_params=pltpu.CompilerParams(
            collective_id=1, has_side_effects=True, vmem_limit_bytes=63 * 2**20
        ),
    )(normed, grad, *weights)


def reduce_kernel(
    grad_ref, small_ref, own_ref, sum_ref, work, c0, c1, a0, a1, b0, b1, z0, z1,
    small, load_sem, send, recv,
):
    place = Place()
    links = Links(place, send, recv)
    load = pltpu.make_async_copy(grad_ref, work, load_sem)
    load.start()
    half = work.shape[-1] // 2
    parts = [
        Reduce(
            links,
            lambda z, y, c, x: work.at[z, y, c, x, :, pl.ds(0, half)],
            ["c", "x", "y"],
            [c0, a0, b0],
            z0,
        ),
        Reduce(
            links,
            lambda z, y, c, x: work.at[z, y, c, x, :, pl.ds(half, half)],
            ["c", "y", "x"],
            [c1, a1, b1],
            z1,
        ),
    ]
    ring = ("c", "x", "y", "pair", "far")
    first = links.take(len(ring))
    place.greet(["c", "y", "x", "up", "down", "far"])
    load.wait()
    for distance in (3, 2, 1, 0):
        for part in parts:
            part.begin(distance)
    small[0] = small_ref[...]
    rounds = [
        links.copy(small.at[i], small.at[len(ring) + 1 + i], first + i, name)
        for i, name in enumerate(ring)
    ]
    steps = list(zip(parts[0].steps(), parts[1].steps()))
    rounds[0].start()
    for number, (one, two) in enumerate(steps):
        one()
        two()
        if number < len(ring):
            rounds[number].wait_recv()
            small[number + 1] = small[number] + small[len(ring) + 1 + number]
            if number + 1 < len(ring):
                rounds[number + 1].start()
    sum_ref[...] = small[len(ring)]
    own_ref[...] = work[place.z, place.y, place.c, place.x].astype(F32)
    for part in parts:
        part.drain()
    for copy in rounds:
        copy.wait_send()


def reduce_all(grad, small):
    columns = grad.shape[-1]
    half = columns // 2
    vmem = pl.BlockSpec(memory_space=pltpu.VMEM)
    hbm = pl.BlockSpec(memory_space=pl.ANY)
    return pl.pallas_call(
        reduce_kernel,
        out_shape=[
            jax.ShapeDtypeStruct((32, columns), F32),
            jax.ShapeDtypeStruct(small.shape, F32),
        ],
        in_specs=[hbm, vmem],
        out_specs=[vmem, vmem],
        scratch_shapes=[pltpu.VMEM(grad.shape, BF16)]
        + [pltpu.VMEM((DEPTH, 2, 2, 32, half), BF16)] * 2
        + [pltpu.VMEM((DEPTH, 2, 32, half), BF16)] * 2
        + [pltpu.VMEM((DEPTH, 32, half), BF16)] * 2
        + [pltpu.VMEM((DEPTH + 1, 32, half), BF16)] * 2
        + [
            pltpu.VMEM((11,) + small.shape, F32),
            pltpu.SemaphoreType.DMA,
            pltpu.SemaphoreType.DMA((64,)),
            pltpu.SemaphoreType.DMA((64,)),
        ],
        compiler_params=pltpu.CompilerParams(
            collective_id=2, has_side_effects=True, vmem_limit_bytes=40 * 2**20
        ),
    )(grad, small)


def shifted(block, axis, distance):
    devices = range(lax.axis_size(axis))
    route = [(i - distance, i) for i in devices if i - distance in devices]
    return lax.ppermute(block, axis, route)


def mixer_forward(inputs, lengths, norm_one_gain, conv_weight, norm_two_gain, in_all, out_all):
    tok_rows, feat_width = inputs.shape[1:]
    kept = {}
    x_float = inputs[0].astype(F32)
    kernel = conv_weight.astype(F32)
    position = lax.axis_index("seq") * tok_rows + lax.iota(jnp.int32, tok_rows)
    valid_mask = (position < lengths[0]).astype(F32)[:, None]
    scale_one = lax.rsqrt(jnp.mean(x_float * x_float, axis=1, keepdims=True) + epsilon)
    hat_one = x_float * scale_one
    normed_one = (hat_one * norm_one_gain.astype(F32)).astype(BF16)
    projected = rounded_dot(normed_one, in_all)
    b_part = projected[:, :feat_width]
    c_part = projected[:, feat_width : 2 * feat_width]
    v_part = projected[:, 2 * feat_width :]
    product = (b_part * v_part).astype(BF16)
    carried = shifted(product[tok_rows - 2 :], "seq", 1)
    extended = jnp.concatenate([carried, product], axis=0).astype(F32)
    conv_out = (
        kernel[0] * extended[:tok_rows]
        + kernel[1] * extended[1 : tok_rows + 1]
        + kernel[2] * extended[2:]
    )
    gated_mix = (c_part * conv_out).astype(BF16)
    mixer_out = rounded_dot(gated_mix, out_all)
    middle = x_float + valid_mask * mixer_out
    scale_two = lax.rsqrt(jnp.mean(middle * middle, axis=1, keepdims=True) + epsilon)
    hat_two = middle * scale_two
    normed_two = (hat_two * norm_two_gain.astype(F32)).astype(BF16)
    kept.update(locals())
    return kept


def mixer_backward(kept, grad_out, normed_part, norm_one_gain, norm_two_gain, in_all, out_all):
    tok_rows, feat_width = grad_out.shape
    kernel = kept["kernel"]
    extended, conv_out = kept["extended"], kept["conv_out"]
    hat_one, hat_two = kept["hat_one"], kept["hat_two"]
    grad_gain_two = jnp.sum(normed_part * hat_two, axis=0)
    scaled_two = normed_part * norm_two_gain.astype(F32)
    grad_middle = grad_out + kept["scale_two"] * (
        scaled_two - hat_two * jnp.mean(scaled_two * hat_two, axis=1, keepdims=True)
    )
    grad_mix = (kept["valid_mask"] * grad_middle).astype(BF16)
    grad_out_w = over_rows(kept["gated_mix"], grad_mix)
    grad_gated = by_rows(grad_mix, out_all)
    grad_c = grad_gated * conv_out
    grad_conv_in = grad_gated * kept["c_part"]
    grad_kernel = jnp.stack(
        [
            jnp.sum(grad_conv_in * extended[:tok_rows], axis=0),
            jnp.sum(grad_conv_in * extended[1 : tok_rows + 1], axis=0),
            jnp.sum(grad_conv_in * extended[2:], axis=0),
        ]
    )
    padded_grad = jnp.pad(grad_conv_in, ((2, 2), (0, 0)))
    grad_extended = (
        kernel[0] * padded_grad[2 : tok_rows + 4]
        + kernel[1] * padded_grad[1 : tok_rows + 3]
        + kernel[2] * padded_grad[: tok_rows + 2]
    )
    returned = shifted(grad_extended[:2], "seq", -1)
    grad_product = grad_extended[2:] + jnp.concatenate(
        [jnp.zeros((tok_rows - 2, feat_width), F32), returned], axis=0
    )
    grad_projected = jnp.concatenate(
        [grad_product * kept["v_part"], grad_c, grad_product * kept["b_part"]], axis=1
    ).astype(BF16)
    grad_in_w = over_rows(kept["normed_one"], grad_projected)
    grad_normed_one = by_rows(grad_projected, in_all)
    grad_gain_one = jnp.sum(grad_normed_one * hat_one, axis=0)
    scaled_one = grad_normed_one * norm_one_gain.astype(F32)
    grad_inputs = grad_middle + kept["scale_one"] * (
        scaled_one - hat_one * jnp.mean(scaled_one * hat_one, axis=1, keepdims=True)
    )
    return grad_inputs, grad_in_w, grad_out_w, grad_gain_one, grad_kernel, grad_gain_two


def in_blocks(
    inputs,
    lengths,
    norm_one_gain,
    w_in,
    conv_weight,
    w_out,
    norm_two_gain,
    w_gate,
    w_up,
    w_down,
    cotangent,
):
    width = inputs.shape[2]
    quarter = w_gate.shape[1] // 2
    down = w_down.T
    starts = [sum(PARTS[:i]) for i in range(len(PARTS))]
    ffn = [
        jnp.stack(
            [
                jnp.concatenate(
                    [
                        w[:, h * quarter + start : h * quarter + start + size]
                        for w in (w_gate, w_up, down)
                    ],
                    axis=1,
                )
                for h in range(2)
            ]
        )
        for start, size in zip(starts, PARTS)
    ]
    mixer, *weights = gather_all(jnp.concatenate([w_in, w_out], axis=1), ffn)
    mixer = mixer.reshape(width, 4 * width)
    in_all, out_all = mixer[:, : 3 * width], mixer[:, 3 * width :]
    kept = mixer_forward(
        inputs, lengths, norm_one_gain, conv_weight, norm_two_gain, in_all, out_all
    )
    grad_out = cotangent[0].astype(F32)
    grad_ffn = (kept["valid_mask"] * grad_out).astype(BF16)
    ffn_sum, normed_part, *ffn_grads = ffn_all(kept["normed_two"], grad_ffn, weights)
    ffn_out = ffn_sum.astype(BF16).astype(F32)
    result = (kept["middle"] + kept["valid_mask"] * ffn_out).astype(BF16)
    grad_inputs, grad_in_w, grad_out_w, gain_one, taps, gain_two = mixer_backward(
        kept, grad_out, normed_part, norm_one_gain, norm_two_gain, in_all, out_all
    )
    small = jnp.concatenate(
        [gain_one[None], taps, gain_two[None], jnp.zeros((3, width), F32)]
    )
    mixer_grad = jnp.concatenate(
        [grad_in_w.astype(BF16), grad_out_w.astype(BF16)], axis=1
    ).reshape(DEPTH, 2, 2, 2, 32, 4 * width)
    own, total = reduce_all(mixer_grad, small)
    sides = []
    for index in range(3):
        pieces = [
            grad[h, :, index * size : (index + 1) * size]
            for h in range(2)
            for grad, size in zip(ffn_grads, PARTS)
        ]
        sides.append(jnp.concatenate(pieces, axis=1).astype(F32))
    return (
        result[None],
        grad_inputs[None],
        total[0],
        own[:, : 3 * width],
        total[1:4],
        own[:, 3 * width :],
        total[4],
        sides[0],
        sides[1],
        sides[2].T,
    )


def anywhere(
    inputs,
    lengths,
    norm_one_gain,
    w_in,
    conv_weight,
    w_out,
    norm_two_gain,
    w_gate,
    w_up,
    w_down,
    cotangent,
):
    both = ("seq", "batch")
    in_all = lax.all_gather(w_in, both, axis=0, tiled=True)
    out_all = lax.all_gather(w_out, both, axis=0, tiled=True)
    gate_use, up_use = (
        lax.all_gather(
            lax.all_gather(w, "seq", axis=0, tiled=True), "batch", axis=1, tiled=True
        )
        for w in (w_gate, w_up)
    )
    down_use = lax.all_gather(
        lax.all_gather(w_down, "seq", axis=1, tiled=True), "batch", axis=0, tiled=True
    )
    kept = mixer_forward(
        inputs, lengths, norm_one_gain, conv_weight, norm_two_gain, in_all, out_all
    )
    rows_norm = kept["normed_two"]
    grad_out = cotangent[0].astype(F32)
    rows_grad = (kept["valid_mask"] * grad_out).astype(BF16)
    gate_val = rounded_dot(rows_norm, gate_use)
    up_val = rounded_dot(rows_norm, up_use)
    hidden = (jax.nn.silu(gate_val) * up_val).astype(BF16)
    ffn_out = rounded_dot(hidden, down_use)
    result = (kept["middle"] + kept["valid_mask"] * ffn_out).astype(BF16)
    grad_down = over_rows(hidden, rows_grad)
    grad_hidden = by_rows(rows_grad, down_use)
    sigmoid_gate = jax.nn.sigmoid(gate_val)
    slope_gate = sigmoid_gate * (1.0 + gate_val * (1.0 - sigmoid_gate))
    grad_gate = (grad_hidden * up_val * slope_gate).astype(BF16)
    grad_up = (grad_hidden * gate_val * sigmoid_gate).astype(BF16)
    grad_gate_w = over_rows(rows_norm, grad_gate)
    grad_up_w = over_rows(rows_norm, grad_up)
    normed_part = by_rows(grad_gate, gate_use) + by_rows(grad_up, up_use)

    def owned(grad, axis):
        half = lax.psum_scatter(
            grad.astype(BF16), "batch", scatter_dimension=axis, tiled=True
        ).astype(F32)
        return lax.psum_scatter(half, "seq", scatter_dimension=1 - axis, tiled=True)

    shards = owned(grad_gate_w, 1), owned(grad_up_w, 1), owned(grad_down, 0)
    grad_inputs, grad_in_w, grad_out_w, gain_one, taps, gain_two = mixer_backward(
        kept, grad_out, normed_part, norm_one_gain, norm_two_gain, in_all, out_all
    )
    shard_in, shard_out = (
        lax.psum_scatter(grad, both, scatter_dimension=0, tiled=True)
        for grad in (grad_in_w, grad_out_w)
    )
    total_one, total_two, total_kernel = lax.psum((gain_one, gain_two, taps), both)
    return (
        result[None],
        grad_inputs[None],
        total_one,
        shard_in,
        total_kernel,
        shard_out,
        total_two,
    ) + shards


def solution(mesh):
    in_specs = (
        P("batch", "seq", None),
        P("batch"),
        P(),
        P(("seq", "batch"), None),
        P(),
        P(("seq", "batch"), None),
        P(),
        P("seq", "batch"),
        P("seq", "batch"),
        P("batch", "seq"),
        P("batch", "seq", None),
    )
    out_specs = (
        P("batch", "seq", None),
        P("batch", "seq", None),
        P(),
        P(("seq", "batch"), None),
        P(),
        P(("seq", "batch"), None),
        P(),
        P("seq", "batch"),
        P("seq", "batch"),
        P("batch", "seq"),
    )
    by_blocks = mesh.shape["seq"] == 4 * DEPTH and mesh.shape["batch"] == 2
    return jax.shard_map(
        in_blocks if by_blocks else anywhere,
        mesh=mesh,
        in_specs=in_specs,
        out_specs=out_specs,
        check_vma=False,
    )
```

```python
import functools

import jax
import jax.numpy as jnp
from jax import lax
from jax.experimental import pallas as pl
from jax.experimental.pallas import tpu as pltpu
from jax.sharding import PartitionSpec as P

epsilon = 1e-05
MESH = pl.DeviceIdType.MESH
F32, BF16 = jnp.float32, jnp.bfloat16
DEPTH = 4
PARTS = (512, 384, 256)


def over_rows(left, right):
    return lax.dot_general(
        left, right, (((0,), (0,)), ((), ())), preferred_element_type=F32
    )


def by_rows(left, right):
    return lax.dot_general(
        left, right, (((1,), (1,)), ((), ())), preferred_element_type=F32
    )


def dot(left, right):
    return jnp.dot(left, right, preferred_element_type=F32)


def rounded_dot(left, right):
    return dot(left, right).astype(BF16).astype(F32)


class Place:
    def __init__(self):
        self.s = lax.axis_index("seq")
        self.x = lax.axis_index("batch")
        self.z = self.s // 4
        self.y = (self.s // 2) % 2
        self.c = self.s % 2
        self.last = lax.axis_size("seq") - 1
        self.own = {"y": self.y, "c": self.c, "x": self.x}
        self.device = {
            "c": (self.s + 1 - 2 * self.c, self.x),
            "y": (self.s + 2 - 4 * self.y, self.x),
            "x": (self.s, 1 - self.x),
            "up": (self.s + 4, self.x),
            "down": (self.s - 4, self.x),
            "next": (self.s + 1, self.x),
            "prev": (self.s - 1, self.x),
            "pair": (self.s + 4 - 8 * (self.z % 2), self.x),
            "far": (self.s + 8 - 16 * (self.z // 2), self.x),
        }

    def greet(self, names):
        barrier = pltpu.get_barrier_semaphore()
        ends = {
            "up": self.z < DEPTH - 1,
            "down": self.z > 0,
            "next": self.s < self.last,
            "prev": self.s > 0,
        }

        def signal(name):
            pl.semaphore_signal(
                barrier, inc=1, device_id=self.device[name], device_id_type=MESH
            )

        expected = 0
        for name in names:
            if name in ends:
                pl.when(ends[name])(functools.partial(signal, name))
                expected = expected + ends[name].astype(jnp.int32)
            else:
                signal(name)
                expected = expected + 1
        pl.semaphore_wait(barrier, expected)


class Links:
    def __init__(self, place, send, recv):
        self.place, self.send, self.recv = place, send, recv
        self.used = 0

    def take(self, count):
        first = self.used
        self.used += count
        assert self.used <= self.send.shape[0]
        return first

    def copy(self, source, target, index, name):
        return pltpu.make_async_remote_copy(
            src_ref=source,
            dst_ref=target,
            send_sem=self.send.at[index],
            recv_sem=self.recv.at[index],
            device_id=self.place.device[name],
            device_id_type=MESH,
        )


def way(direction):
    return (1 - direction) // 2


class Line:
    def take_line(self):
        self.first = self.links.take(2 * DEPTH)

    def hop(self, source, target, direction, level):
        place = self.place
        index = self.first + DEPTH * way(direction) + level
        return pltpu.make_async_remote_copy(
            src_ref=source,
            dst_ref=target,
            send_sem=self.links.send.at[index],
            recv_sem=self.links.recv.at[index],
            device_id=(place.s + 4 * direction, place.x),
            device_id_type=MESH,
        )

    def levels(self, distance, action):
        z = self.place.z
        if distance == 0:
            action(z, None)
            return

        def side(i, carry):
            direction = 1 - 2 * i
            level = z - direction * distance

            @pl.when((level >= 0) & (level < DEPTH))
            def _():
                action(level, direction)

            return carry

        lax.fori_loop(0, 2, side, 0)

    def beyond(self, direction):
        further = self.place.z + direction
        return (further >= 0) & (further < DEPTH)


class Gather(Line):
    def __init__(self, links, view, stages):
        self.links, self.view, self.stages = links, view, stages
        self.place = links.place
        self.take_line()
        self.rows = {name: links.take(DEPTH) for name in stages}

    def block(self, stage, level, theirs=False):
        where = dict(self.place.own)
        if stage is not None:
            for name in self.stages[:stage]:
                where[name] = slice(None)
            if theirs:
                where[self.stages[stage]] = 1 - where[self.stages[stage]]
        return self.view(level, where["y"], where["c"], where["x"])

    def line(self, direction, level):
        ref = self.block(None, level)
        return self.hop(ref, ref, direction, level)

    def staged(self, stage, level, theirs=False):
        name = self.stages[stage]
        ref = self.block(stage, level, theirs)
        return self.links.copy(ref, ref, self.rows[name] + level, name)

    def along(self, distance):
        def hand_on(level, direction):
            if distance:
                self.line(direction, level).wait_recv()

            @pl.when(self.beyond(direction))
            def _():
                self.line(direction, level).start()

        if distance == 0:
            hand_on(self.place.z, 1)
            hand_on(self.place.z, -1)
        else:
            self.levels(distance, hand_on)

    def depart(self, distance):
        self.levels(distance, lambda level, _: self.staged(0, level).start())

    def across(self, stage, distance):
        def pass_on(level, _):
            self.staged(stage, level, True).wait_recv()
            if stage + 1 < len(self.stages):
                self.staged(stage + 1, level).start()

        self.levels(distance, pass_on)

    def drain_line(self):
        z = self.place.z

        def sent(level, carry):
            @pl.when((z >= level) & (z < DEPTH - 1))
            def _():
                self.line(1, level).wait_send()

            @pl.when((z <= level) & (z > 0))
            def _():
                self.line(-1, level).wait_send()

            return carry

        lax.fori_loop(0, DEPTH, sent, 0)

    def drain(self):
        self.drain_line()

        def sent(level, carry):
            for stage in range(len(self.stages)):
                self.staged(stage, level).wait_send()
            return carry

        lax.fori_loop(0, DEPTH, sent, 0)


class PairGather(Gather):
    def __init__(self, links, ref):
        super().__init__(links, lambda z, y, c, x: ref.at[z, y], ["y"])
        self.ref = ref

    def line(self, direction, level):
        ref = self.ref.at[level]
        return self.hop(ref, ref, direction, level)

    def begin(self):
        self.staged(0, self.place.z).start()

    def join(self):
        self.staged(0, self.place.z, True).wait_recv()
        self.along(0)

    def drain(self):
        self.staged(0, self.place.z).wait_send()
        self.drain_line()


def add_into(target, source):
    def add(i, carry):
        target[i] = (target[i].astype(F32) + source[i].astype(F32)).astype(BF16)
        return carry

    if len(target.shape) > 2:
        lax.fori_loop(0, target.shape[0], add, 0)
    else:
        add(Ellipsis, 0)


class Reduce(Line):
    def __init__(self, links, view, stages, slots, line_slots):
        self.links, self.view, self.stages = links, view, stages
        self.slots, self.line_slots = slots, line_slots
        self.place = links.place
        self.take_line()
        self.rows = {name: links.take(DEPTH) for name in stages}

    def block(self, stage, level, theirs=False):
        where = dict(self.place.own)
        for name in self.stages[stage + 1 :]:
            where[name] = slice(None)
        if theirs:
            where[self.stages[stage]] = 1 - where[self.stages[stage]]
        return self.view(level, where["y"], where["c"], where["x"])

    def staged(self, stage, level):
        name = self.stages[stage]
        return self.links.copy(
            self.block(stage, level, True),
            self.slots[stage].at[level],
            self.rows[name] + level,
            name,
        )

    def slot(self, direction, level):
        return self.line_slots.at[level + 1 - way(direction)]

    def line(self, direction, level):
        ref = self.block(len(self.stages) - 1, level)
        return self.hop(ref, self.slot(direction, level), direction, level)

    def begin(self, distance):
        self.levels(distance, lambda level, _: self.staged(0, level).start())

    def across(self, stage, distance):
        def take(level, _):
            self.staged(stage, level).wait_recv()
            add_into(self.block(stage, level), self.slots[stage].at[level])
            if stage + 1 < len(self.stages):
                self.staged(stage + 1, level).start()

        self.levels(distance, take)

    def take(self, direction, level):
        self.line(direction, level).wait_recv()
        add_into(
            self.block(len(self.stages) - 1, level), self.slot(direction, level)
        )

    def along(self, distance):
        if distance == 0:

            def side(i, carry):
                direction = 1 - 2 * i

                @pl.when(self.beyond(-direction))
                def _():
                    self.take(direction, self.place.z)

                return carry

            lax.fori_loop(0, 2, side, 0)
            return

        def send(level, back):
            @pl.when(self.beyond(back))
            def _():
                self.take(-back, level)

            self.line(-back, level).start()

        self.levels(distance, send)

    def drain_line(self):
        z = self.place.z

        def sent(level, carry):
            @pl.when(z > level)
            def _():
                self.line(-1, level).wait_send()

            @pl.when(z < level)
            def _():
                self.line(1, level).wait_send()

            return carry

        lax.fori_loop(0, DEPTH, sent, 0)

    def drain(self):
        self.drain_line()

        def sent(level, carry):
            for stage in range(len(self.stages)):
                self.staged(stage, level).wait_send()
            return carry

        lax.fori_loop(0, DEPTH, sent, 0)

    def steps(self):
        found = []
        count = len(self.stages)
        for time in range(DEPTH + count):
            for stage in range(count, -1, -1):
                if 0 <= time - stage < DEPTH:
                    distance = DEPTH - 1 - (time - stage)
                    if stage == count:
                        found.append(functools.partial(self.along, distance))
                    else:
                        found.append(functools.partial(self.across, stage, distance))
        return found


class PairReduce(Reduce):
    def __init__(self, links, ref, slot, line_slots):
        super().__init__(links, lambda z, y, c, x: ref.at[z, y], ["y"], None, line_slots)
        self.ref, self.last_slot = ref, slot

    def block(self, stage, level, theirs=False):
        return self.ref.at[level]

    def final(self):
        place = self.place
        return self.links.copy(
            self.ref.at[place.z, 1 - place.y], self.last_slot, self.rows["y"], "y"
        )

    def finish(self):
        self.final().wait_recv()
        add_into(self.ref.at[self.place.z, self.place.y], self.last_slot)

    def drain(self):
        self.drain_line()
        self.final().wait_send()


class Plan:
    def __init__(self):
        self.entries = []

    def at(self, time, action, *args):
        self.entries.append((time, len(self.entries), functools.partial(action, *args)))

    def run(self):
        for _, _, action in sorted(self.entries, key=lambda entry: entry[:2]):
            action()


def layer_kernel(
    x_ref,
    grad_ref,
    valid_ref,
    gain_one_ref,
    taps_ref,
    gain_two_ref,
    mixer_ref,
    f0_ref,
    f1_ref,
    f2_ref,
    mixer_out,
    parts_out,
    edge_out,
    middle_out,
    out_ref,
    back_ref,
    d0_ref,
    d1_ref,
    d2_ref,
    wm,
    w0,
    w1,
    w2,
    normed,
    product,
    middle,
    tokens,
    grads,
    r0,
    l0,
    r1,
    l1,
    r2,
    l2,
    hidden,
    slopes,
    out_sum,
    back_sum,
    e0,
    e1,
    e2,
    keep_sem,
    send,
    recv,
):
    place = Place()
    links = Links(place, send, recv)
    plan = Plan()
    rows, depth = x_ref.shape
    weights = (w0, w1, w2)
    half = mixer_ref.shape[1] // 2

    mixers = [
        Gather(
            links,
            lambda z, y, c, x: wm.at[z, y, c, x, :, pl.ds(0, half)],
            ["y", "x", "c"],
        ),
        Gather(
            links,
            lambda z, y, c, x: wm.at[z, y, c, x, :, pl.ds(half, half)],
            ["x", "y", "c"],
        ),
    ]
    gathers = [
        Gather(links, lambda z, y, c, x: w0.at[z, y], ["y"]),
        PairGather(links, w1),
        Gather(links, lambda z, y, c, x: w2.at[z, y], ["y"]),
    ]
    reduces = [
        Reduce(links, lambda z, y, c, x: w0.at[z, y], ["y"], [r0], l0),
        PairReduce(links, w1, r1, l1),
        Reduce(links, lambda z, y, c, x: w2.at[z, y], ["y"], [r2], l2),
    ]
    twins = [
        links.copy(
            source.at[1 - place.c], target.at[place.z, place.y, place.c], links.take(1), "c"
        )
        for source, target in ((f0_ref, w0), (f1_ref, w1), (f2_ref, w2))
    ]

    def share(buffer, start, size):
        first = links.take(3)
        ref = [buffer.at[i, pl.ds(start, size)] for i in range(4)]
        return (
            links.copy(ref[0], ref[1], first, "c"),
            links.copy(ref[0], ref[2], first + 1, "x"),
            links.copy(ref[2], ref[3], first + 2, "c"),
        )

    tile = rows // 2
    shared_grads = share(grads, 0, rows)
    shared_tokens = [share(tokens, tile * i, tile) for i in range(2)]
    edge = links.copy(
        product.at[pl.ds(rows, 8)], product.at[pl.ds(0, 8)], links.take(1), "next"
    )
    slots = [wm.at[pl.ds(0, 2), :, :, :, :, pl.ds(depth * i, depth)] for i in range(4)]
    slots += [wm.at[pl.ds(2, 2), :, :, :, :, pl.ds(depth * i, depth)] for i in range(2)]

    def give_back(total, slots):
        first = links.take(3)
        return (
            links.copy(total.at[3], slots[2], first, "c"),
            links.copy(total.at[2], slots[1], first + 1, "x"),
            links.copy(total.at[1], slots[0], first + 2, "c"),
        )

    returned = [give_back(back_sum, slots[:3]), give_back(out_sum, slots[3:])]
    trades = links.take(3)
    keeps = [
        pltpu.make_async_copy(wm, mixer_out, keep_sem.at[0]),
        pltpu.make_async_copy(slopes.at[pl.ds(0, 3 * rows)], parts_out, keep_sem.at[1]),
        pltpu.make_async_copy(middle, middle_out, keep_sem.at[2]),
        pltpu.make_async_copy(product.at[pl.ds(8, rows)], back_ref, keep_sem.at[3]),
        pltpu.make_async_copy(middle, out_ref, keep_sem.at[4]),
    ]

    def open_all():
        place.greet(["c", "y", "x", "up", "down", "next", "prev"])
        wm[place.z, place.y, place.c, place.x] = mixer_ref[...]
        for part in mixers:
            part.along(0)
            part.depart(0)
        for twin in twins:
            twin.start()
        for source, target in ((f0_ref, w0), (f1_ref, w1), (f2_ref, w2)):
            target[place.z, place.y, place.c] = source[place.c]

    def first_norm():
        x = x_ref[...].astype(F32)
        scale = lax.rsqrt(jnp.mean(x * x, axis=1, keepdims=True) + epsilon)
        normed[...] = (x * scale * gain_one_ref[...].astype(F32)).astype(BF16)
        grads[0] = (grad_ref[...].astype(F32) * valid_ref[...]).astype(BF16)

        @pl.when(place.s == 0)
        def _():
            product[pl.ds(0, 8)] = jnp.zeros((8, depth), F32)

    plan.at(0, open_all)
    plan.at(1, first_norm)
    hop = 4
    for part in mixers:
        for distance in range(DEPTH):
            if distance:
                plan.at(hop * distance, part.along, distance)
                plan.at(hop * distance, part.depart, distance)
            for stage in range(3):
                plan.at(hop * (distance + stage + 1), part.across, stage, distance)

    plan.at(9, lambda: [twin.wait_recv() for twin in twins])
    plan.at(9, gathers[0].along, 0)
    for distance, time in ((1, 18), (2, 27), (3, 38)):
        plan.at(time, gathers[0].along, distance)
    plan.at(27, gathers[1].begin)
    for distance, time in ((0, 27.1), (1, 27.2), (2, 27.3), (3, 38.1)):
        plan.at(time, gathers[0].depart, distance)
    plan.at(38.2, gathers[1].join)
    for distance, time in ((1, 53), (2, 66), (3, 78)):
        plan.at(time, gathers[1].along, distance)
    plan.at(38.3, gathers[2].along, 0)
    plan.at(38.3, gathers[2].depart, 0)
    for distance, time in ((1, 66.1), (2, 78.1), (3, 84)):
        plan.at(time, gathers[2].along, distance)
        plan.at(time, gathers[2].depart, distance)
    for distance in range(DEPTH):
        plan.at(64, gathers[0].across, 0, distance)
        plan.at(115, gathers[2].across, 0, distance)

    def project(index):
        weight = wm[..., depth * index : depth * (index + 1)].reshape(depth, depth)
        slopes[rows * index : rows * (index + 1)] = dot(normed[...], weight).astype(BF16)

    def multiply():
        b_part = slopes[:rows].astype(F32)
        v_part = slopes[2 * rows : 3 * rows].astype(F32)
        product[pl.ds(8, rows)] = (b_part * v_part).astype(BF16).astype(F32)
        pl.when(place.s < place.last)(lambda: edge.start())

    def mix(index):
        start = tile * index
        where = slice(start, start + tile)
        conv = 0.0
        for tap in range(3):
            conv += taps_ref[tap : tap + 1].astype(F32) * product[
                start + 6 + tap : start + 6 + tap + tile
            ]
        c_part = slopes[rows + start : rows + start + tile].astype(F32)
        gated = (c_part * conv).astype(BF16)
        weight = wm[..., 3 * depth :].reshape(depth, depth)
        mixed = dot(gated, weight)
        total = x_ref[where].astype(F32) + valid_ref[where] * mixed
        middle[where] = total
        scale = lax.rsqrt(jnp.mean(total * total, axis=1, keepdims=True) + epsilon)
        tokens[0, where] = (total * scale * gain_two_ref[...].astype(F32)).astype(BF16)

    def send_tokens(index):
        shared_tokens[index][1].start()
        shared_tokens[index][0].start()

    def take_edge():
        pl.when(place.s > 0)(lambda: edge.wait_recv())

    def start_grads():
        shared_grads[1].start()
        shared_grads[0].start()

    def pass_grads():
        shared_grads[1].wait_recv()
        shared_grads[2].start()

    def pass_tokens(index):
        shared_tokens[index][1].wait_recv()
        shared_tokens[index][2].start()

    plan.at(32, start_grads)
    plan.at(39, project, 2)
    plan.at(40, project, 0)
    plan.at(41, multiply)
    plan.at(42, project, 1)
    plan.at(43, lambda: keeps[1].start())
    plan.at(44, mix, 1)
    plan.at(45, lambda: [part.drain() for part in mixers])
    plan.at(46, take_edge)
    plan.at(46.5, lambda: pl.when(place.s < place.last)(lambda: edge.wait_send()))
    plan.at(47, mix, 0)
    plan.at(48, lambda: (keeps[0].start(), keeps[2].start()))
    plan.at(48.5, lambda: keeps[0].wait())
    plan.at(49, send_tokens, 1)
    plan.at(49, send_tokens, 0)
    plan.at(65, pass_grads)
    plan.at(66, lambda: [keep.wait() for keep in keeps[1:3]])

    def block(number, first):
        lax.fori_loop(first, first + 2, functools.partial(one_block, number), 0)

    def one_block(number, i, carry):
        weight, width = weights[number], PARTS[number]
        gate_up = weight[..., : 2 * width].reshape(depth, 2 * width)
        both = dot(tokens[i], gate_up)
        gate, up = both[:, :width], both[:, width:]
        sigmoid = jax.nn.sigmoid(gate)
        silu = gate * sigmoid
        slope = sigmoid + silu * (1.0 - sigmoid)
        kept = (silu * up).astype(BF16)
        down = weight[..., 2 * width :].reshape(depth, width)
        grad_hidden = dot(grads[i], down)
        where = pl.ds(pl.multiple_of(rows * i, rows), rows)
        hidden[where, :width] = kept
        slopes[where, :width] = (grad_hidden * up * slope).astype(BF16)
        slopes[where, width : 2 * width] = (grad_hidden * silu).astype(BF16)
        out_part = by_rows(kept, down)
        back_part = by_rows(slopes[where, : 2 * width], gate_up)
        shape = out_sum.shape[1:]
        if number:
            out_part += out_sum[i].reshape(rows, depth).astype(F32)
            back_part += back_sum[i].reshape(rows, depth).astype(F32)
        out_sum[i] = out_part.astype(BF16).reshape(shape)
        back_sum[i] = back_part.astype(BF16).reshape(shape)
        return carry

    def weigh(number):
        weight, width = weights[number], PARTS[number]
        gathers[number].drain()
        for source, factor, first, size in (
            (tokens, slopes, 0, 2 * width),
            (grads, hidden, 2 * width, width),
        ):
            step = 256 if size % 256 == 0 else size

            def columns(i, carry):
                start = pl.multiple_of(i * step, 128)
                part = over_rows(
                    source[...].reshape(4 * rows, depth), factor[:, pl.ds(start, step)]
                )
                where = pl.ds(pl.multiple_of(first + i * step, 128), step)
                weight[..., where] = part.astype(BF16).reshape(
                    weight.shape[:-1] + (step,)
                )
                return carry

            lax.fori_loop(0, size // step, columns, 0)

    def hear(*copies):
        for copy in copies:
            copy.wait_recv()

    plan.at(67, hear, shared_tokens[1][0], shared_tokens[0][0], shared_grads[0])
    plan.at(68, block, 0, 0)
    plan.at(76, pass_tokens, 1)
    plan.at(76, pass_tokens, 0)
    plan.at(77, hear, shared_grads[2], shared_tokens[1][2], shared_tokens[0][2])
    plan.at(77, block, 0, 2)
    plan.at(85, weigh, 0)
    for distance in (3, 2, 1, 0):
        plan.at(95, reduces[0].begin, distance)
    plan.at(96, block, 1, 0)
    plan.at(103, block, 1, 2)
    plan.at(109.5, weigh, 1)
    plan.at(115, reduces[1].along, 3)
    plan.at(116, block, 2, 2)
    plan.at(121, block, 2, 0)
    plan.at(120.8, returned[0][0].start)
    plan.at(120.9, returned[1][0].start)

    def lift(index):
        group = returned[index]
        group[0].wait_recv()
        total = (back_sum, out_sum)[index]
        add_into(total.at[2], slots[3 * index + 2])
        group[1].start()

    plan.at(120.95, lift, 0)
    plan.at(121.1, lift, 1)
    plan.at(123.5, lambda: [group[2].start() for group in returned])
    plan.at(126, weigh, 2)
    for distance in (3, 2, 1, 0):
        plan.at(131, reduces[2].begin, distance)
    for k, start, unit in ((0, 103, 8.5), (2, 136, 4.3)):
        for index, distance in enumerate((3, 2, 1, 0)):
            plan.at(start + unit * index, reduces[k].across, 0, distance)
            plan.at(start + unit * (index + 1), reduces[k].along, distance)
    for time, distance in ((131, 2), (144, 1), (157, 0)):
        plan.at(time, reduces[1].along, distance)
    plan.at(157.5, lambda: reduces[1].final().start())
    plan.at(165, reduces[1].finish)

    def finish(index):
        total = (back_sum, out_sum)[index]
        target = (product.at[pl.ds(8, rows)], middle)[index]
        hear(returned[index][1], returned[index][2])
        target[...] = (
            total[0].astype(F32)
            + slots[3 * index][...].astype(F32)
            + slots[3 * index + 1][...].astype(F32)
        ).reshape(rows, depth)
        keeps[3 + index].start()

    plan.at(150, finish, 0)
    plan.at(166, finish, 1)

    def trade(number):
        weight, buffer = weights[number], (e0, e1, e2)[number]
        target = (d0_ref, d1_ref, d2_ref)[number]
        buffer[...] = weight[place.z, place.y, 1 - place.c]
        copy = links.copy(buffer, target.at[place.c], trades + number, "c")
        copy.start()
        target[place.c] = weight[place.z, place.y, place.c]
        return copy

    def close():
        for copy in [trade(number) for number in range(3)]:
            copy.wait()
        for reduce in reduces:
            reduce.drain()
        for group in [shared_grads] + shared_tokens + returned:
            for copy in group:
                copy.wait_send()
        for twin in twins:
            twin.wait_send()
        for keep in keeps[3:]:
            keep.wait()
        edge_out[...] = product[pl.ds(0, 8)]

    plan.at(170, close)
    plan.run()


def layer(inputs, grad, valid, gain_one, taps, gain_two, mixer, ffn):
    rows, depth = inputs.shape
    columns = mixer.shape[1]
    vmem = pl.BlockSpec(memory_space=pltpu.VMEM)
    hbm = pl.BlockSpec(memory_space=pl.ANY)
    shape = jax.ShapeDtypeStruct
    out_shape = [
        shape((DEPTH, 2, 2, 2, 32, columns), BF16),
        shape((3 * rows, depth), BF16),
        shape((8, depth), F32),
        shape((rows, depth), F32),
        shape((rows, depth), F32),
        shape((rows, depth), F32),
    ] + [shape((2, 64, 3 * w), BF16) for w in PARTS]
    pair = (2, 64)
    widths = [3 * w for w in PARTS]
    scratch = (
        [pltpu.VMEM((DEPTH, 2, 2, 2, 32, columns), BF16)]
        + [pltpu.VMEM((DEPTH, 2) + pair + (w,), BF16) for w in widths]
        + [
            pltpu.VMEM((rows, depth), BF16),
            pltpu.VMEM((rows + 8, depth), F32),
            pltpu.VMEM((rows, depth), F32),
        ]
        + [pltpu.VMEM((4, rows, depth), BF16)] * 2
        + [
            pltpu.VMEM((DEPTH,) + pair + (widths[0],), BF16),
            pltpu.VMEM((DEPTH + 1,) + pair + (widths[0],), BF16),
            pltpu.VMEM(pair + (widths[1],), BF16),
            pltpu.VMEM((DEPTH + 1, 2) + pair + (widths[1],), BF16),
            pltpu.VMEM((DEPTH,) + pair + (widths[2],), BF16),
            pltpu.VMEM((DEPTH + 1,) + pair + (widths[2],), BF16),
            pltpu.VMEM((4 * rows, PARTS[0]), BF16),
            pltpu.VMEM((4 * rows, 2 * PARTS[0]), BF16),
        ]
        + [pltpu.VMEM((4, 2, 2, 2, 2, rows // 16, depth), BF16)] * 2
        + [pltpu.VMEM((64, w), BF16) for w in widths]
        + [
            pltpu.SemaphoreType.DMA((5,)),
            pltpu.SemaphoreType.DMA((144,)),
            pltpu.SemaphoreType.DMA((144,)),
        ]
    )
    return pl.pallas_call(
        layer_kernel,
        out_shape=out_shape,
        in_specs=[vmem] * 10,
        out_specs=[hbm, hbm, vmem, hbm, hbm, hbm] + [vmem] * 3,
        scratch_shapes=scratch,
        compiler_params=pltpu.CompilerParams(
            collective_id=0, has_side_effects=True, vmem_limit_bytes=63 * 2**20
        ),
    )(inputs, grad, valid, gain_one, taps, gain_two, mixer, *ffn)


def reduce_kernel(
    grad_ref, small_ref, own_ref, sum_ref, work, c0, c1, a0, a1, b0, b1, z0, z1,
    small, load_sem, send, recv,
):
    place = Place()
    links = Links(place, send, recv)
    load = pltpu.make_async_copy(grad_ref, work, load_sem)
    load.start()
    half = work.shape[-1] // 2
    parts = [
        Reduce(
            links,
            lambda z, y, c, x: work.at[z, y, c, x, :, pl.ds(0, half)],
            ["c", "x", "y"],
            [c0, a0, b0],
            z0,
        ),
        Reduce(
            links,
            lambda z, y, c, x: work.at[z, y, c, x, :, pl.ds(half, half)],
            ["c", "y", "x"],
            [c1, a1, b1],
            z1,
        ),
    ]
    ring = ("c", "x", "y", "pair", "far")
    first = links.take(len(ring))
    place.greet(["c", "y", "x", "up", "down", "far"])
    load.wait()
    for distance in (3, 2, 1, 0):
        for part in parts:
            part.begin(distance)
    small[0] = small_ref[...]
    rounds = [
        links.copy(small.at[i], small.at[len(ring) + 1 + i], first + i, name)
        for i, name in enumerate(ring)
    ]
    steps = list(zip(parts[0].steps(), parts[1].steps()))
    rounds[0].start()
    for number, (one, two) in enumerate(steps):
        one()
        two()
        if number < len(ring):
            rounds[number].wait_recv()
            small[number + 1] = small[number] + small[len(ring) + 1 + number]
            if number + 1 < len(ring):
                rounds[number + 1].start()
    sum_ref[...] = small[len(ring)]
    own_ref[...] = work[place.z, place.y, place.c, place.x].astype(F32)
    for part in parts:
        part.drain()
    for copy in rounds:
        copy.wait_send()


def reduce_all(grad, small):
    columns = grad.shape[-1]
    half = columns // 2
    vmem = pl.BlockSpec(memory_space=pltpu.VMEM)
    hbm = pl.BlockSpec(memory_space=pl.ANY)
    return pl.pallas_call(
        reduce_kernel,
        out_shape=[
            jax.ShapeDtypeStruct((32, columns), F32),
            jax.ShapeDtypeStruct(small.shape, F32),
        ],
        in_specs=[hbm, vmem],
        out_specs=[vmem, vmem],
        scratch_shapes=[pltpu.VMEM(grad.shape, BF16)]
        + [pltpu.VMEM((DEPTH, 2, 2, 32, half), BF16)] * 2
        + [pltpu.VMEM((DEPTH, 2, 32, half), BF16)] * 2
        + [pltpu.VMEM((DEPTH, 32, half), BF16)] * 2
        + [pltpu.VMEM((DEPTH + 1, 32, half), BF16)] * 2
        + [
            pltpu.VMEM((11,) + small.shape, F32),
            pltpu.SemaphoreType.DMA,
            pltpu.SemaphoreType.DMA((64,)),
            pltpu.SemaphoreType.DMA((64,)),
        ],
        compiler_params=pltpu.CompilerParams(
            collective_id=2, has_side_effects=True, vmem_limit_bytes=40 * 2**20
        ),
    )(grad, small)


def shifted(block, axis, distance):
    devices = range(lax.axis_size(axis))
    route = [(i - distance, i) for i in devices if i - distance in devices]
    return lax.ppermute(block, axis, route)


def mixer_forward(inputs, lengths, norm_one_gain, conv_weight, norm_two_gain, in_all, out_all):
    tok_rows, feat_width = inputs.shape[1:]
    kept = {}
    x_float = inputs[0].astype(F32)
    kernel = conv_weight.astype(F32)
    position = lax.axis_index("seq") * tok_rows + lax.iota(jnp.int32, tok_rows)
    valid_mask = (position < lengths[0]).astype(F32)[:, None]
    scale_one = lax.rsqrt(jnp.mean(x_float * x_float, axis=1, keepdims=True) + epsilon)
    hat_one = x_float * scale_one
    normed_one = (hat_one * norm_one_gain.astype(F32)).astype(BF16)
    projected = rounded_dot(normed_one, in_all)
    b_part = projected[:, :feat_width]
    c_part = projected[:, feat_width : 2 * feat_width]
    v_part = projected[:, 2 * feat_width :]
    product = (b_part * v_part).astype(BF16)
    carried = shifted(product[tok_rows - 2 :], "seq", 1)
    extended = jnp.concatenate([carried, product], axis=0).astype(F32)
    conv_out = (
        kernel[0] * extended[:tok_rows]
        + kernel[1] * extended[1 : tok_rows + 1]
        + kernel[2] * extended[2:]
    )
    gated_mix = (c_part * conv_out).astype(BF16)
    mixer_out = rounded_dot(gated_mix, out_all)
    middle = x_float + valid_mask * mixer_out
    scale_two = lax.rsqrt(jnp.mean(middle * middle, axis=1, keepdims=True) + epsilon)
    hat_two = middle * scale_two
    normed_two = (hat_two * norm_two_gain.astype(F32)).astype(BF16)
    kept.update(locals())
    return kept


def mixer_again(inputs, norm_one_gain, conv_weight, valid_mask, middle, parts, edge):
    tok_rows = inputs.shape[1]
    x_float = inputs[0].astype(F32)
    kernel = conv_weight.astype(F32)
    scale_one = lax.rsqrt(jnp.mean(x_float * x_float, axis=1, keepdims=True) + epsilon)
    hat_one = x_float * scale_one
    normed_one = (hat_one * norm_one_gain.astype(F32)).astype(BF16)
    b_part, c_part, v_part = (
        parts[i * tok_rows : (i + 1) * tok_rows].astype(F32) for i in range(3)
    )
    product = (b_part * v_part).astype(BF16).astype(F32)
    extended = jnp.concatenate([edge[6:], product], axis=0)
    conv_out = (
        kernel[0] * extended[:tok_rows]
        + kernel[1] * extended[1 : tok_rows + 1]
        + kernel[2] * extended[2:]
    )
    gated_mix = (c_part * conv_out).astype(BF16)
    scale_two = lax.rsqrt(jnp.mean(middle * middle, axis=1, keepdims=True) + epsilon)
    hat_two = middle * scale_two
    return dict(locals())


def mixer_backward(kept, grad_out, normed_part, norm_one_gain, norm_two_gain, in_all, out_all):
    tok_rows, feat_width = grad_out.shape
    kernel = kept["kernel"]
    extended, conv_out = kept["extended"], kept["conv_out"]
    hat_one, hat_two = kept["hat_one"], kept["hat_two"]
    grad_gain_two = jnp.sum(normed_part * hat_two, axis=0)
    scaled_two = normed_part * norm_two_gain.astype(F32)
    grad_middle = grad_out + kept["scale_two"] * (
        scaled_two - hat_two * jnp.mean(scaled_two * hat_two, axis=1, keepdims=True)
    )
    grad_mix = (kept["valid_mask"] * grad_middle).astype(BF16)
    grad_out_w = over_rows(kept["gated_mix"], grad_mix)
    grad_gated = by_rows(grad_mix, out_all)
    grad_c = grad_gated * conv_out
    grad_conv_in = grad_gated * kept["c_part"]
    grad_kernel = jnp.stack(
        [
            jnp.sum(grad_conv_in * extended[:tok_rows], axis=0),
            jnp.sum(grad_conv_in * extended[1 : tok_rows + 1], axis=0),
            jnp.sum(grad_conv_in * extended[2:], axis=0),
        ]
    )
    padded_grad = jnp.pad(grad_conv_in, ((2, 2), (0, 0)))
    grad_extended = (
        kernel[0] * padded_grad[2 : tok_rows + 4]
        + kernel[1] * padded_grad[1 : tok_rows + 3]
        + kernel[2] * padded_grad[: tok_rows + 2]
    )
    returned = shifted(grad_extended[:2], "seq", -1)
    grad_product = grad_extended[2:] + jnp.concatenate(
        [jnp.zeros((tok_rows - 2, feat_width), F32), returned], axis=0
    )
    grad_projected = jnp.concatenate(
        [grad_product * kept["v_part"], grad_c, grad_product * kept["b_part"]], axis=1
    ).astype(BF16)
    grad_in_w = over_rows(kept["normed_one"], grad_projected)
    grad_normed_one = by_rows(grad_projected, in_all)
    grad_gain_one = jnp.sum(grad_normed_one * hat_one, axis=0)
    scaled_one = grad_normed_one * norm_one_gain.astype(F32)
    grad_inputs = grad_middle + kept["scale_one"] * (
        scaled_one - hat_one * jnp.mean(scaled_one * hat_one, axis=1, keepdims=True)
    )
    return grad_inputs, grad_in_w, grad_out_w, grad_gain_one, grad_kernel, grad_gain_two


def in_blocks(
    inputs,
    lengths,
    norm_one_gain,
    w_in,
    conv_weight,
    w_out,
    norm_two_gain,
    w_gate,
    w_up,
    w_down,
    cotangent,
):
    width = inputs.shape[2]
    quarter = w_gate.shape[1] // 2
    down = w_down.T
    starts = [sum(PARTS[:i]) for i in range(len(PARTS))]
    ffn = [
        jnp.stack(
            [
                jnp.concatenate(
                    [
                        w[:, h * quarter + start : h * quarter + start + size]
                        for w in (w_gate, w_up, down)
                    ],
                    axis=1,
                )
                for h in range(2)
            ]
        )
        for start, size in zip(starts, PARTS)
    ]
    tok_rows = inputs.shape[1]
    position = lax.axis_index("seq") * tok_rows + lax.iota(jnp.int32, tok_rows)
    valid_mask = (position < lengths[0]).astype(F32)[:, None]
    mixer, parts, edge, middle, ffn_sum, normed_part, *ffn_grads = layer(
        inputs[0],
        cotangent[0],
        valid_mask,
        norm_one_gain[None],
        conv_weight,
        norm_two_gain[None],
        jnp.concatenate([w_in, w_out], axis=1),
        ffn,
    )
    mixer = mixer.reshape(width, 4 * width)
    in_all, out_all = mixer[:, : 3 * width], mixer[:, 3 * width :]
    grad_out = cotangent[0].astype(F32)
    kept = mixer_again(
        inputs, norm_one_gain, conv_weight, valid_mask, middle, parts, edge
    )
    ffn_out = ffn_sum.astype(BF16).astype(F32)
    result = (middle + valid_mask * ffn_out).astype(BF16)
    grad_inputs, grad_in_w, grad_out_w, gain_one, taps, gain_two = mixer_backward(
        kept, grad_out, normed_part, norm_one_gain, norm_two_gain, in_all, out_all
    )
    small = jnp.concatenate(
        [gain_one[None], taps, gain_two[None], jnp.zeros((3, width), F32)]
    )
    mixer_grad = jnp.concatenate(
        [grad_in_w.astype(BF16), grad_out_w.astype(BF16)], axis=1
    ).reshape(DEPTH, 2, 2, 2, 32, 4 * width)
    own, total = reduce_all(mixer_grad, small)
    sides = []
    for index in range(3):
        pieces = [
            grad[h, :, index * size : (index + 1) * size]
            for h in range(2)
            for grad, size in zip(ffn_grads, PARTS)
        ]
        sides.append(jnp.concatenate(pieces, axis=1).astype(F32))
    return (
        result[None],
        grad_inputs[None],
        total[0],
        own[:, : 3 * width],
        total[1:4],
        own[:, 3 * width :],
        total[4],
        sides[0],
        sides[1],
        sides[2].T,
    )


def anywhere(
    inputs,
    lengths,
    norm_one_gain,
    w_in,
    conv_weight,
    w_out,
    norm_two_gain,
    w_gate,
    w_up,
    w_down,
    cotangent,
):
    both = ("seq", "batch")
    in_all = lax.all_gather(w_in, both, axis=0, tiled=True)
    out_all = lax.all_gather(w_out, both, axis=0, tiled=True)
    gate_use, up_use = (
        lax.all_gather(
            lax.all_gather(w, "seq", axis=0, tiled=True), "batch", axis=1, tiled=True
        )
        for w in (w_gate, w_up)
    )
    down_use = lax.all_gather(
        lax.all_gather(w_down, "seq", axis=1, tiled=True), "batch", axis=0, tiled=True
    )
    kept = mixer_forward(
        inputs, lengths, norm_one_gain, conv_weight, norm_two_gain, in_all, out_all
    )
    rows_norm = kept["normed_two"]
    grad_out = cotangent[0].astype(F32)
    rows_grad = (kept["valid_mask"] * grad_out).astype(BF16)
    gate_val = rounded_dot(rows_norm, gate_use)
    up_val = rounded_dot(rows_norm, up_use)
    hidden = (jax.nn.silu(gate_val) * up_val).astype(BF16)
    ffn_out = rounded_dot(hidden, down_use)
    result = (kept["middle"] + kept["valid_mask"] * ffn_out).astype(BF16)
    grad_down = over_rows(hidden, rows_grad)
    grad_hidden = by_rows(rows_grad, down_use)
    sigmoid_gate = jax.nn.sigmoid(gate_val)
    slope_gate = sigmoid_gate * (1.0 + gate_val * (1.0 - sigmoid_gate))
    grad_gate = (grad_hidden * up_val * slope_gate).astype(BF16)
    grad_up = (grad_hidden * gate_val * sigmoid_gate).astype(BF16)
    grad_gate_w = over_rows(rows_norm, grad_gate)
    grad_up_w = over_rows(rows_norm, grad_up)
    normed_part = by_rows(grad_gate, gate_use) + by_rows(grad_up, up_use)

    def owned(grad, axis):
        half = lax.psum_scatter(
            grad.astype(BF16), "batch", scatter_dimension=axis, tiled=True
        ).astype(F32)
        return lax.psum_scatter(half, "seq", scatter_dimension=1 - axis, tiled=True)

    shards = owned(grad_gate_w, 1), owned(grad_up_w, 1), owned(grad_down, 0)
    grad_inputs, grad_in_w, grad_out_w, gain_one, taps, gain_two = mixer_backward(
        kept, grad_out, normed_part, norm_one_gain, norm_two_gain, in_all, out_all
    )
    shard_in, shard_out = (
        lax.psum_scatter(grad, both, scatter_dimension=0, tiled=True)
        for grad in (grad_in_w, grad_out_w)
    )
    total_one, total_two, total_kernel = lax.psum((gain_one, gain_two, taps), both)
    return (
        result[None],
        grad_inputs[None],
        total_one,
        shard_in,
        total_kernel,
        shard_out,
        total_two,
    ) + shards


def solution(mesh):
    in_specs = (
        P("batch", "seq", None),
        P("batch"),
        P(),
        P(("seq", "batch"), None),
        P(),
        P(("seq", "batch"), None),
        P(),
        P("seq", "batch"),
        P("seq", "batch"),
        P("batch", "seq"),
        P("batch", "seq", None),
    )
    out_specs = (
        P("batch", "seq", None),
        P("batch", "seq", None),
        P(),
        P(("seq", "batch"), None),
        P(),
        P(("seq", "batch"), None),
        P(),
        P("seq", "batch"),
        P("seq", "batch"),
        P("batch", "seq"),
    )
    by_blocks = mesh.shape["seq"] == 4 * DEPTH and mesh.shape["batch"] == 2
    return jax.shard_map(
        in_blocks if by_blocks else anywhere,
        mesh=mesh,
        in_specs=in_specs,
        out_specs=out_specs,
        check_vma=False,
    )
```

```python
import functools

import jax
import jax.numpy as jnp
from jax import lax
from jax.experimental import pallas as pl
from jax.experimental.pallas import tpu as pltpu
from jax.sharding import PartitionSpec as P

epsilon = 1e-05
MESH = pl.DeviceIdType.MESH
F32, BF16 = jnp.float32, jnp.bfloat16
DEPTH = 4
PARTS = (256, 384, 256, 256)
KINDS = ("y", "z", "z", "z")
ORDER = (0, 1, 2, 3)
SPOTS = (0, 768, 0, 768)
PAIRS = tuple(k for k, kind in enumerate(KINDS) if kind == "y")
PAIR_EARLY = 1
MIXER = (
    (0, ["y", "x", "c"]),
    (2, ["x", "y", "c"]),
    (1, ["y", "x", "c"]),
    (3, ["x", "y", "c"]),
)
Z_GATE = 2
ACTS = 1920
EARLY = 1
STEPS = (
    0, 1, 2, 3, 4, 5, 6, 7, 8, 9, 10, 11, 12, 13, 14, 18, 20, 21, 22, 23, 24, 25, 26,
    27, 15, 16, 17, 19, 28, 29, 34, 52, 46, 47, 70, 88, 64, 65, 82, 83, 30, 31, 35, 48,
    49, 158, 66, 67, 56, 84, 85, 100, 38, 60, 32, 33, 42, 92, 50, 51, 53, 96, 68, 69,
    71, 86, 87, 74, 36, 78, 72, 89, 37, 101, 55, 39, 73, 54, 43, 90, 91, 141, 142, 143,
    57, 61, 59, 63, 102, 105, 109, 75, 93, 79, 97, 40, 41, 58, 44, 45, 144, 62, 76, 77,
    94, 95, 145, 80, 81, 98, 146, 147, 99, 148, 149, 103, 159, 150, 153, 151, 152, 113,
    106, 110, 117, 121, 160, 154, 155, 156, 157, 166, 164, 161, 104, 167, 114, 107, 111,
    162, 125, 118, 122, 129, 133, 115, 108, 112, 163, 119, 123, 165, 169, 170, 126, 130,
    134, 171, 172, 137, 116, 120, 124, 168, 127, 131, 135, 178, 179, 138, 173, 128, 132,
    136, 139, 180, 181, 182, 183, 184, 140, 193, 174, 194, 195, 196, 185, 186, 198, 203,
    197, 187, 201, 175, 176, 199, 200, 202, 217, 189, 188, 204, 205, 206, 207, 208, 191,
    218, 219, 220, 221, 222, 231, 232, 234, 177, 263, 190, 209, 210, 264, 265, 211, 233,
    235, 236, 237, 238, 241, 239, 243, 213, 192, 266, 240, 267, 212, 215, 247, 242, 244,
    245, 223, 224, 246, 248, 249, 256, 250, 214, 225, 251, 252, 253, 226, 227, 254, 255,
    257, 261, 258, 216, 269, 229, 259, 260, 228, 270, 262, 268, 271, 230, 272, 273, 274,
    275,
)


def over_rows(left, right):
    return lax.dot_general(
        left, right, (((0,), (0,)), ((), ())), preferred_element_type=F32
    )


def by_rows(left, right):
    return lax.dot_general(
        left, right, (((1,), (1,)), ((), ())), preferred_element_type=F32
    )


def dot(left, right):
    return jnp.dot(left, right, preferred_element_type=F32)


def rounded_dot(left, right):
    return dot(left, right).astype(BF16).astype(F32)


class Place:
    def __init__(self):
        self.s = lax.axis_index("seq")
        self.x = lax.axis_index("batch")
        self.z = self.s // 4
        self.y = (self.s // 2) % 2
        self.c = self.s % 2
        self.last = lax.axis_size("seq") - 1
        self.own = {"y": self.y, "c": self.c, "x": self.x}
        self.device = {
            "c": (self.s + 1 - 2 * self.c, self.x),
            "y": (self.s + 2 - 4 * self.y, self.x),
            "x": (self.s, 1 - self.x),
            "up": (self.s + 4, self.x),
            "down": (self.s - 4, self.x),
            "next": (self.s + 1, self.x),
            "prev": (self.s - 1, self.x),
            "pair": (self.s + 4 - 8 * (self.z % 2), self.x),
            "far": (self.s + 8 - 16 * (self.z // 2), self.x),
        }

    def greet(self, names):
        barrier = pltpu.get_barrier_semaphore()
        ends = {
            "up": self.z < DEPTH - 1,
            "down": self.z > 0,
            "next": self.s < self.last,
            "prev": self.s > 0,
        }

        def signal(name):
            pl.semaphore_signal(
                barrier, inc=1, device_id=self.device[name], device_id_type=MESH
            )

        expected = 0
        for name in names:
            if name in ends:
                pl.when(ends[name])(functools.partial(signal, name))
                expected = expected + ends[name].astype(jnp.int32)
            else:
                signal(name)
                expected = expected + 1
        pl.semaphore_wait(barrier, expected)


class Links:
    def __init__(self, place, send, recv):
        self.place, self.send, self.recv = place, send, recv
        self.used = 0

    def take(self, count):
        first = self.used
        self.used += count
        assert self.used <= self.send.shape[0]
        return first

    def copy(self, source, target, index, name):
        return pltpu.make_async_remote_copy(
            src_ref=source,
            dst_ref=target,
            send_sem=self.send.at[index],
            recv_sem=self.recv.at[index],
            device_id=self.place.device[name],
            device_id_type=MESH,
        )


def way(direction):
    return (1 - direction) // 2


class Line:
    def take_line(self):
        self.first = self.links.take(2 * DEPTH)

    def hop(self, source, target, direction, level):
        place = self.place
        index = self.first + DEPTH * way(direction) + level
        return pltpu.make_async_remote_copy(
            src_ref=source,
            dst_ref=target,
            send_sem=self.links.send.at[index],
            recv_sem=self.links.recv.at[index],
            device_id=(place.s + 4 * direction, place.x),
            device_id_type=MESH,
        )

    def levels(self, distance, action):
        z = self.place.z
        if distance == 0:
            action(z, None)
            return

        def side(i, carry):
            direction = 1 - 2 * i
            level = z - direction * distance

            @pl.when((level >= 0) & (level < DEPTH))
            def _():
                action(level, direction)

            return carry

        lax.fori_loop(0, 2, side, 0)

    def beyond(self, direction):
        further = self.place.z + direction
        return (further >= 0) & (further < DEPTH)


class Gather(Line):
    def __init__(self, links, view, stages):
        self.links, self.view, self.stages = links, view, stages
        self.place = links.place
        self.take_line()
        self.rows = {name: links.take(DEPTH) for name in stages}

    def block(self, stage, level, theirs=False):
        where = dict(self.place.own)
        if stage is not None:
            for name in self.stages[:stage]:
                where[name] = slice(None)
            if theirs:
                where[self.stages[stage]] = 1 - where[self.stages[stage]]
        return self.view(level, where["y"], where["c"], where["x"])

    def line(self, direction, level):
        ref = self.block(None, level)
        return self.hop(ref, ref, direction, level)

    def staged(self, stage, level, theirs=False):
        name = self.stages[stage]
        ref = self.block(stage, level, theirs)
        return self.links.copy(ref, ref, self.rows[name] + level, name)

    def along(self, distance):
        def hand_on(level, direction):
            if distance:
                self.line(direction, level).wait_recv()

            @pl.when(self.beyond(direction))
            def _():
                self.line(direction, level).start()

        if distance == 0:
            hand_on(self.place.z, 1)
            hand_on(self.place.z, -1)
        else:
            self.levels(distance, hand_on)

    def depart(self, distance):
        self.levels(distance, lambda level, _: self.staged(0, level).start())

    def across(self, stage, distance):
        def pass_on(level, _):
            self.staged(stage, level, True).wait_recv()
            if stage + 1 < len(self.stages):
                self.staged(stage + 1, level).start()

        self.levels(distance, pass_on)

    def drain_line(self):
        z = self.place.z

        def sent(level, carry):
            @pl.when((z >= level) & (z < DEPTH - 1))
            def _():
                self.line(1, level).wait_send()

            @pl.when((z <= level) & (z > 0))
            def _():
                self.line(-1, level).wait_send()

            return carry

        lax.fori_loop(0, DEPTH, sent, 0)

    def drain(self):
        self.drain_line()

        def sent(level, carry):
            for stage in range(len(self.stages)):
                self.staged(stage, level).wait_send()
            return carry

        lax.fori_loop(0, DEPTH, sent, 0)


class PairGather(Gather):
    def __init__(self, links, ref):
        super().__init__(links, lambda z, y, c, x: ref.at[z, y], ["y"])
        self.ref = ref

    def line(self, direction, level):
        ref = self.ref.at[level]
        return self.hop(ref, ref, direction, level)

    def begin(self):
        self.staged(0, self.place.z).start()

    def join(self):
        self.staged(0, self.place.z, True).wait_recv()
        self.along(0)

    def drain(self):
        self.staged(0, self.place.z).wait_send()
        self.drain_line()


def add_into(target, source):
    def add(i, carry):
        target[i] = (target[i].astype(F32) + source[i].astype(F32)).astype(BF16)
        return carry

    if len(target.shape) > 2:
        lax.fori_loop(0, target.shape[0], add, 0)
    else:
        add(Ellipsis, 0)


class Reduce(Line):
    def __init__(self, links, view, stages, slots, line_slots):
        self.links, self.view, self.stages = links, view, stages
        self.slots, self.line_slots = slots, line_slots
        self.place = links.place
        self.take_line()
        self.rows = {name: links.take(DEPTH) for name in stages}

    def block(self, stage, level, theirs=False):
        where = dict(self.place.own)
        for name in self.stages[stage + 1 :]:
            where[name] = slice(None)
        if theirs:
            where[self.stages[stage]] = 1 - where[self.stages[stage]]
        return self.view(level, where["y"], where["c"], where["x"])

    def staged(self, stage, level):
        name = self.stages[stage]
        return self.links.copy(
            self.block(stage, level, True),
            self.slots[stage].at[level],
            self.rows[name] + level,
            name,
        )

    def slot(self, direction, level):
        return self.line_slots.at[level + 1 - way(direction)]

    def line(self, direction, level):
        ref = self.block(len(self.stages) - 1, level)
        return self.hop(ref, self.slot(direction, level), direction, level)

    def begin(self, distance):
        self.levels(distance, lambda level, _: self.staged(0, level).start())

    def across(self, stage, distance):
        def take(level, _):
            self.staged(stage, level).wait_recv()
            add_into(self.block(stage, level), self.slots[stage].at[level])
            if stage + 1 < len(self.stages):
                self.staged(stage + 1, level).start()

        self.levels(distance, take)

    def take(self, direction, level):
        self.line(direction, level).wait_recv()
        add_into(
            self.block(len(self.stages) - 1, level), self.slot(direction, level)
        )

    def along(self, distance):
        if distance == 0:

            def side(i, carry):
                direction = 1 - 2 * i

                @pl.when(self.beyond(-direction))
                def _():
                    self.take(direction, self.place.z)

                return carry

            lax.fori_loop(0, 2, side, 0)
            return

        def send(level, back):
            @pl.when(self.beyond(back))
            def _():
                self.take(-back, level)

            self.line(-back, level).start()

        self.levels(distance, send)

    def drain_line(self):
        z = self.place.z

        def sent(level, carry):
            @pl.when(z > level)
            def _():
                self.line(-1, level).wait_send()

            @pl.when(z < level)
            def _():
                self.line(1, level).wait_send()

            return carry

        lax.fori_loop(0, DEPTH, sent, 0)

    def drain(self):
        self.drain_line()

        def sent(level, carry):
            for stage in range(len(self.stages)):
                self.staged(stage, level).wait_send()
            return carry

        lax.fori_loop(0, DEPTH, sent, 0)

    def steps(self):
        found = []
        count = len(self.stages)
        for time in range(DEPTH + count):
            for stage in range(count, -1, -1):
                if 0 <= time - stage < DEPTH:
                    distance = DEPTH - 1 - (time - stage)
                    if stage == count:
                        found.append(functools.partial(self.along, distance))
                    else:
                        found.append(functools.partial(self.across, stage, distance))
        return found


class PairReduce(Reduce):
    def __init__(self, links, ref, slot, line_slots):
        super().__init__(links, lambda z, y, c, x: ref.at[z, y], ["y"], None, line_slots)
        self.ref, self.last_slot = ref, slot

    def block(self, stage, level, theirs=False):
        return self.ref.at[level]

    def final(self):
        place = self.place
        return self.links.copy(
            self.ref.at[place.z, 1 - place.y], self.last_slot, self.rows["y"], "y"
        )

    def finish(self):
        self.final().wait_recv()
        add_into(self.ref.at[self.place.z, self.place.y], self.last_slot)

    def drain(self):
        self.drain_line()
        self.final().wait_send()


class Plan:
    def __init__(self):
        self.steps = []

    def add(self, needs, action, *args, busy=False):
        self.steps.append((tuple(needs), functools.partial(action, *args), busy))
        return len(self.steps) - 1

    def run(self, order):
        seen = set()
        assert sorted(order) == list(range(len(self.steps)))
        for index in order:
            needs, action, _ = self.steps[index]
            assert seen.issuperset(needs)
            action()
            seen.add(index)


def mean_of(values):
    return jnp.mean(values, axis=1, keepdims=True)


def layer_kernel(
    length_ref,
    x_ref,
    grad_ref,
    grad_rows_ref,
    gain_one_ref,
    taps_ref,
    gain_two_ref,
    in_ref,
    out_ref,
    gate_ref,
    up_ref,
    down_ref,
    mixer_hbm,
    parts_hbm,
    middle_hbm,
    mixer_grad,
    small,
    result_ref,
    input_grad,
    gate_grad,
    up_grad,
    down_grad,
    wm,
    w0,
    w1,
    w2,
    w3,
    product,
    middle,
    tokens,
    grads,
    r0,
    r1,
    r2,
    r3,
    l0,
    l1,
    l2,
    l3,
    e0,
    e1,
    e2,
    e3,
    acts,
    out_sum,
    back_sum,
    keep_sem,
    send,
    recv,
):
    place = Place()
    links = Links(place, send, recv)
    plan = Plan()
    rows, depth = parts_hbm.shape[0] // 3, parts_hbm.shape[1]
    tile = rows // 2
    weights, edges = (w0, w1, w2, w3), (e0, e1, e2, e3)
    quarter = sum(PARTS)
    offsets = [sum(PARTS[:k]) for k in range(len(PARTS))]

    def columns(first, count):
        return lambda z, y, c, x: wm.at[z, y, c, x, :, pl.ds(first, count)]

    mixers = [
        Gather(links, columns(depth * j, depth), stages)
        for j, stages in MIXER
    ]
    gathers, reduces = [], []
    for kind, w, r, l in zip(KINDS, weights, (r0, r1, r2, r3), (l0, l1, l2, l3)):
        if kind == "y":
            gathers.append(PairGather(links, w))
            reduces.append(PairReduce(links, w, r, l))
        else:
            view = lambda z, y, c, x, w=w: w.at[z, y]
            gathers.append(Gather(links, view, ["y"]))
            reduces.append(Reduce(links, view, ["y"], [r], l))

    def sides(number, quarter_index):
        width = PARTS[number]
        start = pl.multiple_of(quarter_index * quarter + offsets[number], 128)
        return [
            (ref.at[:, pl.ds(start, width)], pl.ds(side * width, width))
            for side, ref in enumerate((gate_ref, up_ref, down_ref))
        ]

    twins = [
        [
            links.copy(
                source,
                weights[number].at[place.z, place.y, place.c, :, where],
                links.take(1),
                "c",
            )
            for source, where in sides(number, 1 - place.c)
        ]
        for number in range(len(PARTS))
    ]


    def share(ref):
        first = links.take(3)
        return (
            links.copy(ref[0], ref[1], first, "c"),
            links.copy(ref[0], ref[2], first + 1, "x"),
            links.copy(ref[2], ref[3], first + 2, "c"),
        )

    shared_grads = [
        share([grads.at[i // 2, 2 * (i % 2) + h, q] for i in range(4)])
        for h in range(2)
        for q in range(2)
    ]
    shared_tokens = [
        share([tokens.at[i // 2, 2 * (i % 2) + h] for i in range(4)]) for h in range(2)
    ]
    edge = links.copy(
        product.at[pl.ds(rows, 8)], product.at[pl.ds(0, 8)], links.take(1), "next"
    )
    back_edge = links.copy(
        middle.at[pl.ds(0, 8)], middle.at[pl.ds(rows, 8)], links.take(1), "prev"
    )
    has_next, has_prev = place.s < place.last, place.s > 0
    slots = [
        wm.at[pl.ds(2 * (i // 4), 2), :, :, :, :, pl.ds(depth * (i % 4), depth)]
        for i in range(6)
    ]

    def give_back(total, slots):
        first = links.take(3)
        return (
            links.copy(total.at[3], slots[2], first, "c"),
            links.copy(total.at[2], slots[1], first + 1, "x"),
            links.copy(total.at[1], slots[0], first + 2, "c"),
        )

    returned = [give_back(back_sum, slots[:3]), give_back(out_sum, slots[3:])]
    trades = [
        links.copy(w.at[place.z, place.y, 1 - place.c], e, links.take(1), "c")
        for w, e in zip(weights, edges)
    ]

    count = iter(range(keep_sem.shape[0]))

    def local(source, target):
        return pltpu.make_async_copy(source, target, keep_sem.at[next(count)])

    parts = acts.at[pl.ds(0, 3 * rows), pl.ds(0, depth)]
    save_mixer = local(wm, mixer_hbm)
    save_parts = local(parts, parts_hbm)
    save_middle = local(middle.at[pl.ds(0, rows)], middle_hbm)
    fills = [
        [
            local(source, weights[number].at[place.z, place.y, place.c, :, where])
            for source, where in sides(number, place.c)
        ]
        for number in range(len(PARTS))
    ]
    mine = wm.at[place.z, place.y, place.c, place.x]
    fill_in = local(in_ref, mine.at[:, pl.ds(0, 3 * depth)])
    fill_out = local(out_ref, mine.at[:, pl.ds(3 * depth, depth)])
    inner = pl.ds(0, rows)
    low_x, high_x = out_sum.at[1], back_sum.at[0]
    view = (2,) + tokens.shape[2:]
    load_x = [local(x_ref, x) for x in (low_x, high_x)]
    load_grad = local(grad_ref, grads.at[0, pl.ds(0, 2)])
    load_grad_rows = local(grad_rows_ref, acts.at[pl.ds(3 * rows, rows), pl.ds(0, depth)])
    save_result = local(back_sum.at[1], result_ref)
    blocks = [tokens.at[0], tokens.at[1], grads.at[0], grads.at[1]]
    load_mixer = [
        local(mixer_hbm.at[:, :, :, :, :, pl.ds(depth * j, depth)], block)
        for j, block in enumerate(blocks)
    ]
    load_parts = local(parts_hbm, parts)
    load_middle = local(middle_hbm, product.at[pl.ds(8, rows)])
    staging = [acts.at[pl.ds(2 * rows * i, 2 * rows), pl.ds(depth, 2 * tile)] for i in range(2)]
    stores = [
        local(staging[j % 2], mixer_grad.at[:, pl.ds(2 * tile * ((j + 6) % 8), 2 * tile)])
        for j in range(8)
    ]
    save_grad, save_inputs = (
        local(middle.at[pl.ds(0, rows)], input_grad) for _ in range(2)
    )
    load_back = local(input_grad, middle.at[pl.ds(0, rows)])

    def hear(*copies):
        for copy in copies:
            copy.wait_recv()

    def begin(*copies):
        for copy in copies:
            copy.start()

    def done(*copies):
        for copy in copies:
            copy.wait()

    def valid_rows(first, count):
        position = place.s * rows + first + lax.broadcasted_iota(
            jnp.int32, (count, 1), 0
        )
        return (position < length_ref[0]).astype(F32)

    def open_all():
        for copy in [fill_in, fill_out, load_x[0], load_grad] + sum(fills, []):
            copy.start()
        place.greet(["c", "y", "x", "up", "down", "next", "prev"])
        fill_in.wait()
        fill_out.wait()

    def clear():
        @pl.when(place.s == 0)
        def _():
            product[pl.ds(0, 8)] = jnp.zeros((8, depth), F32)

        @pl.when(place.s == place.last)
        def _():
            middle[pl.ds(rows, 8)] = jnp.zeros((8, depth), F32)

    def first_norm(source, target):
        x = source[...].reshape(rows, depth).astype(F32)
        scale = lax.rsqrt(mean_of(x * x) + epsilon)
        normed = (x * scale * gain_one_ref[...].astype(F32)).astype(BF16)
        target[...] = normed.reshape(view)

    def mask_grads():
        masked = grads[0, pl.ds(0, 2)].reshape(rows, depth).astype(F32)
        masked *= valid_rows(0, rows)
        grads[0, pl.ds(0, 2)] = masked.astype(BF16).reshape(view)

    def project(index):
        weight = wm[..., depth * index : depth * (index + 1)].reshape(depth, depth)
        acts[rows * index : rows * (index + 1), :depth] = dot(
            out_sum[0].reshape(rows, depth), weight
        ).astype(BF16)

    def multiply():
        b_part = acts[:rows, :depth].astype(F32)
        v_part = acts[2 * rows : 3 * rows, :depth].astype(F32)
        product[pl.ds(8, rows)] = (b_part * v_part).astype(BF16).astype(F32)

    def conv_rows(start):
        total = 0.0
        for tap in range(3):
            first = start + 6 + tap
            total += taps_ref[tap : tap + 1].astype(F32) * product[first : first + tile]
        return total

    def mix(index):
        start = tile * index
        where = slice(start, start + tile)
        c_part = acts[rows + start : rows + start + tile, :depth].astype(F32)
        gated = (c_part * conv_rows(start)).astype(BF16)
        weight = wm[..., 3 * depth :].reshape(depth, depth)
        x = low_x[index].reshape(tile, depth).astype(F32)
        total = x + valid_rows(start, tile) * dot(gated, weight)
        middle[where] = total
        scale = lax.rsqrt(mean_of(total * total) + epsilon)
        new = (total * scale * gain_two_ref[...].astype(F32)).astype(BF16)
        tokens[0, index] = new.reshape(tokens.shape[2:])

    def one_block(number, pair, i, carry):
        weight, width, spot = weights[number], PARTS[number], SPOTS[number]
        where = pl.ds(pl.multiple_of(rows * (2 * pair + i), rows), rows)
        gate_up = weight[..., : 2 * width].reshape(depth, 2 * width)
        both = dot(tokens[pair, pl.ds(2 * i, 2)].reshape(rows, depth), gate_up)
        gate, up = both[:, :width], both[:, width:]
        sigmoid = jax.nn.sigmoid(gate)
        silu = gate * sigmoid
        slope = sigmoid + silu * (1.0 - sigmoid)
        kept = (silu * up).astype(BF16)
        down = weight[..., 2 * width :].reshape(depth, width)
        grad_hidden = dot(grads[pair, pl.ds(2 * i, 2)].reshape(rows, depth), down)
        acts[where, spot : spot + width] = (grad_hidden * up * slope).astype(BF16)
        acts[where, spot + width : spot + 2 * width] = (grad_hidden * silu).astype(BF16)
        acts[where, spot + 2 * width : spot + 3 * width] = kept
        out_part = by_rows(kept, down)
        back_part = by_rows(acts[where, spot : spot + 2 * width], gate_up)
        shape = out_sum.shape[1:]
        index = 2 * pair + i
        if number != ORDER[0]:
            out_part += out_sum[index].reshape(rows, depth).astype(F32)
            back_part += back_sum[index].reshape(rows, depth).astype(F32)
        out_sum[index] = out_part.astype(BF16).reshape(shape)
        back_sum[index] = back_part.astype(BF16).reshape(shape)
        return carry

    def block(number, pair):
        lax.fori_loop(0, 2, functools.partial(one_block, number, pair), 0)

    def weigh(number):
        weight, width, spot = weights[number], PARTS[number], SPOTS[number]
        for source, first, size in ((tokens, 0, 2 * width), (grads, 2 * width, width)):
            step = 256 if size % 256 == 0 else size

            def column(i, carry):
                factor = acts[:, pl.ds(pl.multiple_of(spot + first + i * step, 128), step)]
                part = over_rows(source[...].reshape(4 * rows, depth), factor)
                where = pl.ds(pl.multiple_of(first + i * step, 128), step)
                weight[..., where] = part.astype(BF16).reshape(
                    weight.shape[:-1] + (step,)
                )
                return carry

            lax.fori_loop(0, size // step, column, 0)

    def lift(index):
        hear(returned[index][0])
        add_into((back_sum, out_sum)[index].at[2], slots[3 * index + 2])
        begin(returned[index][1])

    def returned_rows(index, start):
        total = (back_sum, out_sum)[index]
        i = start // tile
        found = total[0, i].reshape(tile, depth).astype(F32)
        for slot in slots[3 * index : 3 * index + 2]:
            found += slot[i].reshape(tile, depth).astype(F32)
        return found

    def note(row, values, fresh):
        total = jnp.sum(values, axis=0, keepdims=True)
        small[row : row + 1] = total if fresh else small[row : row + 1] + total

    def turn(index):
        start = tile * index
        where = slice(start, start + tile)
        part = returned_rows(0, start)
        total = middle[where]
        scale = lax.rsqrt(mean_of(total * total) + epsilon)
        hat = total * scale
        note(4, part * hat, index == 0)
        scaled = part * gain_two_ref[...].astype(F32)
        spot = slice(3 * rows + start, 3 * rows + start + tile)
        grad = acts[spot, :depth].astype(F32) + scale * (
            scaled - hat * mean_of(scaled * hat)
        )
        middle[where] = grad
        acts[spot, :depth] = (valid_rows(start, tile) * grad).astype(BF16)

    def unmix(index):
        start = tile * index
        spot = slice(rows + start, rows + start + tile)
        weight = grads[1].reshape(depth, depth)
        gated_grad = by_rows(
            acts[3 * rows + start : 3 * rows + start + tile, :depth], weight
        )
        c_part = acts[spot, :depth].astype(F32)
        conv = conv_rows(start)
        back_sum[3, index] = (c_part * conv).astype(BF16).reshape(tokens.shape[2:])
        acts[spot, :depth] = (gated_grad * conv).astype(BF16)
        conv_grad = gated_grad * c_part
        middle[start : start + tile] = conv_grad
        for tap in range(3):
            first = start + 6 + tap
            note(1 + tap, conv_grad * product[first : first + tile], index == 0)

    def unconv(index):
        start = tile * index
        grad = 0.0
        for tap in range(3):
            first = start + 2 - tap
            grad += taps_ref[tap : tap + 1].astype(F32) * middle[first : first + tile]
        b_spot = slice(start, start + tile)
        v_spot = slice(2 * rows + start, 2 * rows + start + tile)
        b_part = acts[b_spot, :depth].astype(F32)
        v_part = acts[v_spot, :depth].astype(F32)
        acts[b_spot, :depth] = (grad * v_part).astype(BF16)
        acts[v_spot, :depth] = (grad * b_part).astype(BF16)

    def project_back(index):
        start = tile * index
        where = slice(start, start + tile)
        part = 0.0
        for j in range(3):
            spot = slice(rows * j + start, rows * j + start + tile)
            part += by_rows(acts[spot, :depth], blocks[j][...].reshape(depth, depth))
        x = high_x[index].reshape(tile, depth).astype(F32)
        scale = lax.rsqrt(mean_of(x * x) + epsilon)
        hat = x * scale
        note(0, part * hat, index == 0)
        scaled = part * gain_one_ref[...].astype(F32)
        middle[where] = middle[where] + scale * (scaled - hat * mean_of(scaled * hat))

    def weigh_mixer(j):
        if j >= 2:
            stores[j - 2].wait()
        wide = 2 * tile
        if j >= 2:
            first = rows * (j // 2 - 1)
            left = back_sum[2].reshape(rows, depth)
        else:
            first = 3 * rows
            left = back_sum[3].reshape(rows, depth)
        start = wide * (j % 2)
        part = over_rows(left, acts[first : first + rows, start : start + wide])
        staging[j % 2][...] = part.astype(BF16)
        stores[j].start()

    def close_result():
        for index in range(2):
            start = tile * index
            total = product[8 + start : 8 + start + tile] + valid_rows(
                start, tile
            ) * returned_rows(1, start)
            back_sum[1, index] = total.astype(BF16).reshape(tokens.shape[2:])
        save_result.start()

    def own(number):
        width = PARTS[number]
        for side, target in enumerate((gate_grad, up_grad, down_grad)):
            spot = pl.ds(side * width, width)
            mine = pl.multiple_of(place.c * quarter + offsets[number], 128)
            twin = pl.multiple_of((1 - place.c) * quarter + offsets[number], 128)
            target[:, pl.ds(mine, width)] = weights[number][
                place.z, place.y, place.c, :, spot
            ]
            target[:, pl.ds(twin, width)] = edges[number][:, spot]

    def work_on(needs, action, *args):
        return plan.add(needs, action, *args, busy=True)

    start = plan.add([], open_all)
    for part in mixers:
        plan.add([start], part.along, 0)
        plan.add([start], part.depart, 0)
    for twin in twins:
        plan.add([start], begin, *twin)
    plan.add([start], clear)
    masked = plan.add([start], load_grad.wait)
    masked = work_on([masked], mask_grads)
    plan.add([masked], begin, *[group[0] for group in shared_grads])
    early = [plan.add([masked], begin, group[1]) for group in shared_grads[:EARLY]]
    norm = plan.add([start], load_x[0].wait)
    norm = work_on([norm], first_norm, low_x, out_sum.at[0])
    filled = [plan.add([start], done, *copies) for copies in fills]
    arrived = [
        plan.add([filled[number]], hear, *twins[number]) for number in range(len(PARTS))
    ]

    gone, whole, passed = [], {}, []
    for number, part in enumerate(mixers):
        last = {(0, 0): start}
        for distance in range(1, DEPTH):
            step = plan.add([start], part.along, distance)
            last[0, distance] = plan.add([step], part.depart, distance)
            passed += [step] * (distance == Z_GATE)
        for stage in range(3):
            for distance in range(DEPTH):
                last[stage + 1, distance] = plan.add(
                    [last[stage, distance]], part.across, stage, distance
                )
        gone += [last[stage, d] for stage in (0, 1) for d in range(DEPTH)]
        whole[MIXER[number][0]] = list(last.values())

    ready = {}
    z_gate, y_gate = [start] + passed, list(gone)
    pair_opening = passed if PAIR_EARLY else gone
    pair_gate = {}
    for number in PAIRS:
        pair_gate[number] = [plan.add([arrived[number]] + pair_opening, gathers[number].begin)]
    for number in ORDER:
        part = gathers[number]
        opening = part.join if KINDS[number] == "y" else functools.partial(part.along, 0)
        found = [plan.add([arrived[number]] + z_gate + pair_gate.get(number, []), opening)]
        for distance in range(1, DEPTH):
            found.append(plan.add(found[-1:], part.along, distance))
        z_gate = found[1:2]
        if KINDS[number] == "z":
            sends = [
                plan.add([found[distance]] + y_gate, part.depart, distance)
                for distance in range(DEPTH)
            ]
            y_gate = sends[1:2]
            last_sends = sends
            found += sends
            found += [
                plan.add([sends[distance]], part.across, 0, distance)
                for distance in range(DEPTH)
            ]
        ready[number] = found

    y_gate = last_sends

    x_free = early + [
        plan.add(gone, begin, group[1]) for group in shared_grads[EARLY:]
    ]
    b_step = work_on(whole[0] + [norm], project, 0)
    v_step = work_on(whole[2] + [norm], project, 2)
    times = work_on([b_step, v_step], multiply)

    def send_edge():
        pl.when(has_next)(edge.start)

    def take_edge():
        pl.when(has_prev)(edge.wait_recv)

    def edge_sent():
        pl.when(has_next)(edge.wait_send)

    sent = plan.add([times], send_edge)
    c_step = work_on(whole[1] + [times], project, 1)
    saving = plan.add([c_step], begin, save_parts)
    late_mix = work_on(whole[3] + [c_step, sent], mix, 1)
    drained = plan.add([late_mix], lambda: [part.drain() for part in mixers])
    saved = plan.add([drained], begin, save_mixer)
    token_sends = {}
    token_sends[1] = plan.add([late_mix] + x_free, begin, *shared_tokens[1][1::-1])
    edge_in = plan.add([sent], take_edge)
    mixed = work_on([edge_in, late_mix], mix, 0)
    kept = plan.add([mixed, saved], lambda: (save_middle.start(), save_mixer.wait()))
    token_sends[0] = plan.add([kept, token_sends[1]], begin, *shared_tokens[0][1::-1])

    grads_x, tokens_x = [], []

    def pass_grads(group):
        hear(group[1])
        begin(group[2])

    for step, group in zip(x_free, shared_grads):
        grads_x.append(plan.add([step], pass_grads, group))
    for h in (1, 0):
        group = shared_tokens[h]

        def pass_on(group=group):
            hear(group[1])
            begin(group[2])

        tokens_x.append(plan.add([token_sends[h]], pass_on))
    near = plan.add(
        [token_sends[0], masked],
        hear,
        *[group[0] for group in shared_grads + shared_tokens],
    )
    far = plan.add(
        tokens_x + grads_x, hear, *[group[2] for group in shared_grads + shared_tokens]
    )
    def flush():
        done(save_parts, save_middle)
        edge_sent()

    flushed = plan.add([kept, mixed], flush)
    own_side, other_side = [near, flushed], [near, far, flushed]
    blocks_done = {}
    weighed = {}
    reduced = {}
    previous = []

    def reduce_steps(number, needs):
        part = reduces[number]
        if KINDS[number] == "y":
            chain = list(needs)
            steps = []
            for distance in (3, 2, 1, 0):
                chain = [plan.add(chain, part.along, distance)]
                steps += chain
            chain = [plan.add(chain, lambda: part.final().start())]
            steps.append(plan.add(chain, part.finish))
            return steps
        steps = []
        opened = {
            distance: plan.add(needs + y_gate, part.begin, distance)
            for distance in (3, 2, 1, 0)
        }
        chain = []
        for distance in (3, 2, 1, 0):
            step = plan.add([opened[distance]], part.across, 0, distance)
            chain = [plan.add([step] + chain, part.along, distance)]
            steps += [step] + chain
        return steps

    def drain_and_weigh(number, needs):
        drain = plan.add(needs, gathers[number].drain)
        weighed[number] = work_on([drain], weigh, number)
        reduced[number] = reduce_steps(number, [weighed[number]])

    def columns_of(number):
        return set(range(SPOTS[number], SPOTS[number] + 3 * PARTS[number], 128))

    def run_block(number, pair):
        needs = [
            weighed[other]
            for other in ORDER[: ORDER.index(number)]
            if columns_of(other) & columns_of(number)
        ]
        blocks_done[number, pair] = work_on(
            ready[number] + (other_side if pair else own_side) + needs, block, number, pair
        )

    def finish_part(number):
        drain_and_weigh(number, [blocks_done[number, 0], blocks_done[number, 1]])

    first, second, third, fourth = ORDER
    for number in (first, second):
        if not columns_of(first) & columns_of(second):
            run_block(number, 0)
    for number in (first, second):
        if columns_of(first) & columns_of(second):
            run_block(number, 0)
        run_block(number, 1)
        finish_part(number)
    run_block(third, 1)
    run_block(fourth, 1)
    last_far = [blocks_done[third, 1], blocks_done[fourth, 1]]
    back_up = plan.add(last_far, begin, returned[0][0])
    out_up = plan.add([back_up], begin, returned[1][0])
    back_over = plan.add([back_up], lift, 0)
    run_block(third, 0)
    run_block(fourth, 0)
    near_done = [blocks_done[third, 0], blocks_done[fourth, 0]]
    back_near = plan.add(near_done + [back_over], begin, returned[0][2])
    out_over = plan.add([out_up, back_over], lift, 1)
    out_near = plan.add([back_near, out_over], begin, returned[1][2])
    finish_part(third)
    finish_part(fourth)

    def sent_tokens():
        for group in shared_grads + shared_tokens:
            for copy in group:
                copy.wait_send()

    freed = plan.add([weighed[number] for number in ORDER], sent_tokens)
    loads = plan.add(
        [freed], begin, load_parts, load_grad_rows, *load_mixer
    )
    back_in = plan.add([back_near], hear, returned[0][1], returned[0][2])
    loaded = plan.add([loads], done, load_parts, load_grad_rows, *load_mixer)
    turned = [work_on([back_in, loaded], turn, index) for index in range(2)]

    def free_sums():
        done(save_grad)
        for copy in returned[0]:
            copy.wait_send()
        load_x[1].start()

    freed = plan.add(turned, save_grad.start)
    freed = plan.add([freed], free_sums)
    unmixed = [work_on([freed], unmix, index) for index in range(2)]
    again = plan.add([freed], load_x[1].wait)
    again = work_on([again], first_norm, high_x, back_sum.at[2])

    def send_back():
        pl.when(has_prev)(back_edge.start)

    def take_back():
        pl.when(has_next)(back_edge.wait_recv)

    def back_sent():
        pl.when(has_prev)(back_edge.wait_send)

    back_edge_sent = plan.add([unmixed[0]], send_back)
    weigh_steps = [work_on(unmixed, weigh_mixer, j) for j in (0, 1)]
    low = work_on([unmixed[1], back_edge_sent], unconv, 0)
    taken = plan.add([back_edge_sent], take_back)
    high = work_on([taken, low], unconv, 1)
    fetched = plan.add([low, high] + [edge_in], begin, load_middle)
    for j in range(2, 8):
        weigh_steps.append(work_on([again, low, high, weigh_steps[-1]], weigh_mixer, j))
    revived = plan.add([low, high], lambda: (back_sent(), load_back.start()))
    revived = plan.add([revived, weigh_steps[-1]], load_back.wait)
    projected = [work_on([revived], project_back, index) for index in range(2)]
    stored = plan.add(projected, begin, save_inputs)
    def finish_result():
        load_middle.wait()
        close_result()

    out_in = plan.add([out_near, fetched], hear, returned[1][1], returned[1][2])
    finished = work_on([out_in, fetched] + weigh_steps, finish_result)

    finals = []
    for number in ORDER:
        trade = plan.add(reduced[number], begin, trades[number])
        heard = plan.add([trade], hear, trades[number])
        finals.append(work_on([heard], own, number))

    def close():
        small[pl.ds(5, 3)] = jnp.zeros((3, depth), F32)
        done(save_inputs, save_result, *stores[6:8])
        for reduce in reduces:
            reduce.drain()
        for group in returned[1:] + twins + [trades]:
            for copy in group:
                copy.wait_send()

    plan.add(finals + weigh_steps + projected + [stored, finished], close)
    plan.run(STEPS or list(range(len(plan.steps))))


def layer(lengths, inputs, cotangent, gain_one, taps, gain_two, shards):
    rows, depth = inputs.shape
    ffn_columns = shards[2].shape[1]
    vmem = pl.BlockSpec(memory_space=pltpu.VMEM)
    hbm = pl.BlockSpec(memory_space=pl.ANY)
    shape = jax.ShapeDtypeStruct
    blocks = (DEPTH, 2, 2, 2, depth // (8 * DEPTH))
    half = (2, 2, 2, 2, rows // 16, depth)
    out_shape = [
        shape(blocks + (4 * depth,), BF16),
        shape((3 * rows, depth), BF16),
        shape((rows, depth), F32),
        shape((depth, 4 * depth), BF16),
        shape((8, depth), F32),
        shape(half, BF16),
        shape((rows, depth), F32),
    ] + [shape((64, ffn_columns), BF16)] * 3
    pair = (2, 64)
    widths = [3 * w for w in PARTS]

    def slots(lead, width, kind):
        if kind == "y":
            return (lead, 2) if lead > DEPTH else ()
        return (lead,)

    token = (2, 4, 2, 2, 2, 32, depth)
    total = (4, 2, 2, 2, 2, 32, depth)
    scratch = (
        [pltpu.VMEM(blocks + (4 * depth,), BF16)]
        + [pltpu.VMEM((DEPTH, 2) + pair + (w,), BF16) for w in widths]
        + [
            pltpu.VMEM((rows + 8, depth), F32),
            pltpu.VMEM((rows + 8, depth), F32),
        ]
        + [pltpu.VMEM(token, BF16)] * 2
        + [
            pltpu.VMEM(slots(lead, w, kind) + pair + (w,), BF16)
            for lead in (DEPTH, DEPTH + 1)
            for w, kind in zip(widths, KINDS)
        ]
        + [pltpu.VMEM((64, w), BF16) for w in widths]
        + [pltpu.VMEM((4 * rows, ACTS), BF16)]
        + [pltpu.VMEM(total, BF16)] * 2
        + [
            pltpu.SemaphoreType.DMA((40,)),
            pltpu.SemaphoreType.DMA((240,)),
            pltpu.SemaphoreType.DMA((240,)),
        ]
    )
    smem = pl.BlockSpec(memory_space=pltpu.SMEM)
    return pl.pallas_call(
        layer_kernel,
        out_shape=out_shape,
        in_specs=[smem] + [hbm] * 3 + [vmem] * 3 + [hbm] * 5,
        out_specs=[hbm] * 4 + [vmem, hbm, hbm] + [vmem] * 3,
        scratch_shapes=scratch,
        compiler_params=pltpu.CompilerParams(
            collective_id=0, has_side_effects=True, vmem_limit_bytes=63 * 2**20
        ),
    )(
        lengths,
        inputs.reshape(half),
        cotangent.reshape(half),
        cotangent,
        gain_one,
        taps,
        gain_two,
        *shards
    )


def reduce_kernel(
    grad_ref, small_ref, own_ref, sum_ref, work, c0, c1, a0, a1, b0, b1, z0, z1,
    small, load_sem, send, recv,
):
    place = Place()
    links = Links(place, send, recv)
    load = pltpu.make_async_copy(grad_ref, work, load_sem)
    load.start()
    half = work.shape[-1] // 2
    parts = [
        Reduce(
            links,
            lambda z, y, c, x: work.at[z, y, c, x, :, pl.ds(0, half)],
            ["c", "x", "y"],
            [c0, a0, b0],
            z0,
        ),
        Reduce(
            links,
            lambda z, y, c, x: work.at[z, y, c, x, :, pl.ds(half, half)],
            ["c", "y", "x"],
            [c1, a1, b1],
            z1,
        ),
    ]
    ring = ("c", "x", "y", "pair", "far")
    first = links.take(len(ring))
    place.greet(["c", "y", "x", "up", "down", "far"])
    load.wait()
    for distance in (3, 2, 1, 0):
        for part in parts:
            part.begin(distance)
    small[0] = small_ref[...]
    rounds = [
        links.copy(small.at[i], small.at[len(ring) + 1 + i], first + i, name)
        for i, name in enumerate(ring)
    ]
    steps = list(zip(parts[0].steps(), parts[1].steps()))
    rounds[0].start()
    for number, (one, two) in enumerate(steps):
        one()
        two()
        if number < len(ring):
            rounds[number].wait_recv()
            small[number + 1] = small[number] + small[len(ring) + 1 + number]
            if number + 1 < len(ring):
                rounds[number + 1].start()
    sum_ref[...] = small[len(ring)]
    own_ref[...] = work[place.z, place.y, place.c, place.x].astype(F32)
    for part in parts:
        part.drain()
    for copy in rounds:
        copy.wait_send()


def reduce_all(grad, small):
    columns = grad.shape[-1]
    half = columns // 2
    vmem = pl.BlockSpec(memory_space=pltpu.VMEM)
    hbm = pl.BlockSpec(memory_space=pl.ANY)
    return pl.pallas_call(
        reduce_kernel,
        out_shape=[
            jax.ShapeDtypeStruct((32, columns), F32),
            jax.ShapeDtypeStruct(small.shape, F32),
        ],
        in_specs=[hbm, vmem],
        out_specs=[vmem, vmem],
        scratch_shapes=[pltpu.VMEM(grad.shape, BF16)]
        + [pltpu.VMEM((DEPTH, 2, 2, 32, half), BF16)] * 2
        + [pltpu.VMEM((DEPTH, 2, 32, half), BF16)] * 2
        + [pltpu.VMEM((DEPTH, 32, half), BF16)] * 2
        + [pltpu.VMEM((DEPTH + 1, 32, half), BF16)] * 2
        + [
            pltpu.VMEM((11,) + small.shape, F32),
            pltpu.SemaphoreType.DMA,
            pltpu.SemaphoreType.DMA((64,)),
            pltpu.SemaphoreType.DMA((64,)),
        ],
        compiler_params=pltpu.CompilerParams(
            collective_id=2, has_side_effects=True, vmem_limit_bytes=40 * 2**20
        ),
    )(grad, small)


def shifted(block, axis, distance):
    devices = range(lax.axis_size(axis))
    route = [(i - distance, i) for i in devices if i - distance in devices]
    return lax.ppermute(block, axis, route)


def mixer_forward(inputs, lengths, norm_one_gain, conv_weight, norm_two_gain, in_all, out_all):
    tok_rows, feat_width = inputs.shape[1:]
    kept = {}
    x_float = inputs[0].astype(F32)
    kernel = conv_weight.astype(F32)
    position = lax.axis_index("seq") * tok_rows + lax.iota(jnp.int32, tok_rows)
    valid_mask = (position < lengths[0]).astype(F32)[:, None]
    scale_one = lax.rsqrt(jnp.mean(x_float * x_float, axis=1, keepdims=True) + epsilon)
    hat_one = x_float * scale_one
    normed_one = (hat_one * norm_one_gain.astype(F32)).astype(BF16)
    projected = rounded_dot(normed_one, in_all)
    b_part = projected[:, :feat_width]
    c_part = projected[:, feat_width : 2 * feat_width]
    v_part = projected[:, 2 * feat_width :]
    product = (b_part * v_part).astype(BF16)
    carried = shifted(product[tok_rows - 2 :], "seq", 1)
    extended = jnp.concatenate([carried, product], axis=0).astype(F32)
    conv_out = (
        kernel[0] * extended[:tok_rows]
        + kernel[1] * extended[1 : tok_rows + 1]
        + kernel[2] * extended[2:]
    )
    gated_mix = (c_part * conv_out).astype(BF16)
    mixer_out = rounded_dot(gated_mix, out_all)
    middle = x_float + valid_mask * mixer_out
    scale_two = lax.rsqrt(jnp.mean(middle * middle, axis=1, keepdims=True) + epsilon)
    hat_two = middle * scale_two
    normed_two = (hat_two * norm_two_gain.astype(F32)).astype(BF16)
    kept.update(locals())
    return kept


def mixer_backward(kept, grad_out, normed_part, norm_one_gain, norm_two_gain, in_all, out_all):
    tok_rows, feat_width = grad_out.shape
    kernel = kept["kernel"]
    extended, conv_out = kept["extended"], kept["conv_out"]
    hat_one, hat_two = kept["hat_one"], kept["hat_two"]
    grad_gain_two = jnp.sum(normed_part * hat_two, axis=0)
    scaled_two = normed_part * norm_two_gain.astype(F32)
    grad_middle = grad_out + kept["scale_two"] * (
        scaled_two - hat_two * jnp.mean(scaled_two * hat_two, axis=1, keepdims=True)
    )
    grad_mix = (kept["valid_mask"] * grad_middle).astype(BF16)
    grad_out_w = over_rows(kept["gated_mix"], grad_mix)
    grad_gated = by_rows(grad_mix, out_all)
    grad_c = grad_gated * conv_out
    grad_conv_in = grad_gated * kept["c_part"]
    grad_kernel = jnp.stack(
        [
            jnp.sum(grad_conv_in * extended[:tok_rows], axis=0),
            jnp.sum(grad_conv_in * extended[1 : tok_rows + 1], axis=0),
            jnp.sum(grad_conv_in * extended[2:], axis=0),
        ]
    )
    padded_grad = jnp.pad(grad_conv_in, ((2, 2), (0, 0)))
    grad_extended = (
        kernel[0] * padded_grad[2 : tok_rows + 4]
        + kernel[1] * padded_grad[1 : tok_rows + 3]
        + kernel[2] * padded_grad[: tok_rows + 2]
    )
    returned = shifted(grad_extended[:2], "seq", -1)
    grad_product = grad_extended[2:] + jnp.concatenate(
        [jnp.zeros((tok_rows - 2, feat_width), F32), returned], axis=0
    )
    grad_projected = jnp.concatenate(
        [grad_product * kept["v_part"], grad_c, grad_product * kept["b_part"]], axis=1
    ).astype(BF16)
    grad_in_w = over_rows(kept["normed_one"], grad_projected)
    grad_normed_one = by_rows(grad_projected, in_all)
    grad_gain_one = jnp.sum(grad_normed_one * hat_one, axis=0)
    scaled_one = grad_normed_one * norm_one_gain.astype(F32)
    grad_inputs = grad_middle + kept["scale_one"] * (
        scaled_one - hat_one * jnp.mean(scaled_one * hat_one, axis=1, keepdims=True)
    )
    return grad_inputs, grad_in_w, grad_out_w, grad_gain_one, grad_kernel, grad_gain_two


def in_blocks(
    inputs,
    lengths,
    norm_one_gain,
    w_in,
    conv_weight,
    w_out,
    norm_two_gain,
    w_gate,
    w_up,
    w_down,
    cotangent,
):
    width = inputs.shape[2]
    found = layer(
        lengths,
        inputs[0],
        cotangent[0],
        norm_one_gain[None],
        conv_weight,
        norm_two_gain[None],
        (w_in, w_out, w_gate, w_up, w_down.T),
    )
    mixer_grad, small, result, grad_inputs, gate, up, down = found[3:]
    own, total = reduce_all(
        mixer_grad.reshape(DEPTH, 2, 2, 2, 32, 4 * width), small
    )
    return (
        result.reshape(inputs.shape),
        grad_inputs[None],
        total[0],
        own[:, : 3 * width],
        total[1:4],
        own[:, 3 * width :],
        total[4],
        gate.astype(F32),
        up.astype(F32),
        down.T.astype(F32),
    )


def anywhere(
    inputs,
    lengths,
    norm_one_gain,
    w_in,
    conv_weight,
    w_out,
    norm_two_gain,
    w_gate,
    w_up,
    w_down,
    cotangent,
):
    both = ("seq", "batch")
    in_all = lax.all_gather(w_in, both, axis=0, tiled=True)
    out_all = lax.all_gather(w_out, both, axis=0, tiled=True)
    gate_use, up_use = (
        lax.all_gather(
            lax.all_gather(w, "seq", axis=0, tiled=True), "batch", axis=1, tiled=True
        )
        for w in (w_gate, w_up)
    )
    down_use = lax.all_gather(
        lax.all_gather(w_down, "seq", axis=1, tiled=True), "batch", axis=0, tiled=True
    )
    kept = mixer_forward(
        inputs, lengths, norm_one_gain, conv_weight, norm_two_gain, in_all, out_all
    )
    rows_norm = kept["normed_two"]
    grad_out = cotangent[0].astype(F32)
    rows_grad = (kept["valid_mask"] * grad_out).astype(BF16)
    gate_val = rounded_dot(rows_norm, gate_use)
    up_val = rounded_dot(rows_norm, up_use)
    hidden = (jax.nn.silu(gate_val) * up_val).astype(BF16)
    ffn_out = rounded_dot(hidden, down_use)
    result = (kept["middle"] + kept["valid_mask"] * ffn_out).astype(BF16)
    grad_down = over_rows(hidden, rows_grad)
    grad_hidden = by_rows(rows_grad, down_use)
    sigmoid_gate = jax.nn.sigmoid(gate_val)
    slope_gate = sigmoid_gate * (1.0 + gate_val * (1.0 - sigmoid_gate))
    grad_gate = (grad_hidden * up_val * slope_gate).astype(BF16)
    grad_up = (grad_hidden * gate_val * sigmoid_gate).astype(BF16)
    grad_gate_w = over_rows(rows_norm, grad_gate)
    grad_up_w = over_rows(rows_norm, grad_up)
    normed_part = by_rows(grad_gate, gate_use) + by_rows(grad_up, up_use)

    def owned(grad, axis):
        half = lax.psum_scatter(
            grad.astype(BF16), "batch", scatter_dimension=axis, tiled=True
        ).astype(F32)
        return lax.psum_scatter(half, "seq", scatter_dimension=1 - axis, tiled=True)

    shards = owned(grad_gate_w, 1), owned(grad_up_w, 1), owned(grad_down, 0)
    grad_inputs, grad_in_w, grad_out_w, gain_one, taps, gain_two = mixer_backward(
        kept, grad_out, normed_part, norm_one_gain, norm_two_gain, in_all, out_all
    )
    shard_in, shard_out = (
        lax.psum_scatter(grad, both, scatter_dimension=0, tiled=True)
        for grad in (grad_in_w, grad_out_w)
    )
    total_one, total_two, total_kernel = lax.psum((gain_one, gain_two, taps), both)
    return (
        result[None],
        grad_inputs[None],
        total_one,
        shard_in,
        total_kernel,
        shard_out,
        total_two,
    ) + shards


def solution(mesh):
    in_specs = (
        P("batch", "seq", None),
        P("batch"),
        P(),
        P(("seq", "batch"), None),
        P(),
        P(("seq", "batch"), None),
        P(),
        P("seq", "batch"),
        P("seq", "batch"),
        P("batch", "seq"),
        P("batch", "seq", None),
    )
    out_specs = (
        P("batch", "seq", None),
        P("batch", "seq", None),
        P(),
        P(("seq", "batch"), None),
        P(),
        P(("seq", "batch"), None),
        P(),
        P("seq", "batch"),
        P("seq", "batch"),
        P("batch", "seq"),
    )
    by_blocks = mesh.shape["seq"] == 4 * DEPTH and mesh.shape["batch"] == 2
    return jax.shard_map(
        in_blocks if by_blocks else anywhere,
        mesh=mesh,
        in_specs=in_specs,
        out_specs=out_specs,
        check_vma=False,
    )
```

```python
import functools

import jax
import jax.numpy as jnp
from jax import lax
from jax.experimental import pallas as pl
from jax.experimental.pallas import tpu as pltpu
from jax.sharding import PartitionSpec as P

epsilon = 1e-05
MESH = pl.DeviceIdType.MESH
F32, BF16 = jnp.float32, jnp.bfloat16
DEPTH = 4
PARTS = (256, 384, 256, 256)
KINDS = ("y", "z", "z", "z")
ORDER = (0, 1, 2, 3)
SPOTS = (0, 768, 0, 768)
PAIRS = tuple(k for k, kind in enumerate(KINDS) if kind == "y")
PAIR_EARLY = 1
MIXER = (
    (0, ["y", "x", "c"]),
    (2, ["x", "y", "c"]),
    (1, ["y", "x", "c"]),
    (3, ["x", "y", "c"]),
)
MIXER_GRADS = (
    (0, ["c", "x", "y"], []),
    (2, ["c", "y", "x"], []),
    (3, ["c"], ["x", "y"]),
    (1, ["c", "y", "x"], []),
)
LAST_STEPS = (
    0, 1, 2, 3, 4, 5, 6, 7, 8, 9, 10, 11, 12, 13, 14, 15, 16, 17, 34, 51, 64, 81, 18,
    22, 26, 30, 35, 39, 43, 47, 52, 53, 54, 56, 58, 65, 19, 69, 73, 77, 82, 83, 36, 23,
    40, 27, 55, 44, 31, 84, 85, 37, 38, 48, 41, 66, 45, 20, 21, 57, 49, 42, 67, 68, 70,
    74, 71, 78, 59, 60, 24, 25, 46, 75, 28, 72, 79, 32, 86, 87, 29, 61, 62, 50, 76, 88,
    89, 33, 63, 80, 90, 91,
)
Z_GATE = 2
ACTS = 1920
EARLY = 1
STEPS = (
    0, 1, 2, 3, 4, 5, 6, 7, 8, 9, 10, 11, 12, 13, 14, 18, 20, 21, 22, 23, 24, 25, 26,
    27, 15, 16, 17, 19, 28, 29, 34, 52, 46, 47, 70, 88, 64, 65, 82, 83, 30, 31, 35, 48,
    49, 158, 66, 67, 56, 84, 85, 100, 38, 60, 32, 33, 42, 92, 50, 51, 53, 96, 68, 69,
    71, 86, 87, 74, 36, 78, 72, 89, 37, 101, 55, 39, 73, 54, 43, 90, 91, 141, 142, 143,
    57, 61, 59, 63, 102, 105, 109, 75, 93, 79, 97, 40, 41, 58, 44, 45, 144, 62, 76, 77,
    94, 95, 145, 80, 81, 98, 146, 147, 99, 148, 149, 103, 159, 150, 153, 151, 152, 113,
    106, 110, 117, 121, 160, 154, 155, 156, 157, 166, 164, 161, 104, 167, 114, 107, 111,
    162, 125, 118, 122, 129, 133, 115, 108, 112, 163, 119, 123, 165, 169, 170, 126, 130,
    134, 171, 172, 137, 116, 120, 124, 168, 127, 131, 135, 178, 179, 138, 173, 128, 132,
    136, 139, 180, 181, 182, 183, 184, 140, 193, 174, 194, 195, 196, 185, 186, 198, 203,
    197, 187, 201, 175, 176, 199, 200, 202, 217, 189, 188, 204, 205, 206, 207, 208, 191,
    218, 219, 220, 221, 222, 231, 232, 234, 177, 263, 190, 209, 210, 264, 265, 211, 233,
    235, 236, 237, 238, 241, 239, 243, 213, 192, 266, 240, 267, 212, 215, 247, 242, 244,
    245, 223, 224, 246, 248, 249, 256, 250, 214, 225, 251, 252, 253, 226, 227, 254, 255,
    257, 261, 258, 216, 269, 229, 259, 260, 228, 270, 262, 268, 271, 230, 272, 273, 274,
    275,
)


def over_rows(left, right):
    return lax.dot_general(
        left, right, (((0,), (0,)), ((), ())), preferred_element_type=F32
    )


def by_rows(left, right):
    return lax.dot_general(
        left, right, (((1,), (1,)), ((), ())), preferred_element_type=F32
    )


def dot(left, right):
    return jnp.dot(left, right, preferred_element_type=F32)


def rounded_dot(left, right):
    return dot(left, right).astype(BF16).astype(F32)


class Place:
    def __init__(self):
        self.s = lax.axis_index("seq")
        self.x = lax.axis_index("batch")
        self.z = self.s // 4
        self.y = (self.s // 2) % 2
        self.c = self.s % 2
        self.last = lax.axis_size("seq") - 1
        self.own = {"y": self.y, "c": self.c, "x": self.x}
        self.device = {
            "c": (self.s + 1 - 2 * self.c, self.x),
            "y": (self.s + 2 - 4 * self.y, self.x),
            "x": (self.s, 1 - self.x),
            "up": (self.s + 4, self.x),
            "down": (self.s - 4, self.x),
            "next": (self.s + 1, self.x),
            "prev": (self.s - 1, self.x),
            "pair": (self.s + 4 - 8 * (self.z % 2), self.x),
            "far": (self.s + 8 - 16 * (self.z // 2), self.x),
        }

    def greet(self, names):
        barrier = pltpu.get_barrier_semaphore()
        ends = {
            "up": self.z < DEPTH - 1,
            "down": self.z > 0,
            "next": self.s < self.last,
            "prev": self.s > 0,
        }

        def signal(name):
            pl.semaphore_signal(
                barrier, inc=1, device_id=self.device[name], device_id_type=MESH
            )

        expected = 0
        for name in names:
            if name in ends:
                pl.when(ends[name])(functools.partial(signal, name))
                expected = expected + ends[name].astype(jnp.int32)
            else:
                signal(name)
                expected = expected + 1
        pl.semaphore_wait(barrier, expected)


class Links:
    def __init__(self, place, send, recv):
        self.place, self.send, self.recv = place, send, recv
        self.used = 0

    def take(self, count):
        first = self.used
        self.used += count
        assert self.used <= self.send.shape[0]
        return first

    def copy(self, source, target, index, name):
        return pltpu.make_async_remote_copy(
            src_ref=source,
            dst_ref=target,
            send_sem=self.send.at[index],
            recv_sem=self.recv.at[index],
            device_id=self.place.device[name],
            device_id_type=MESH,
        )


def way(direction):
    return (1 - direction) // 2


class Line:
    def take_line(self):
        self.first = self.links.take(2 * DEPTH)

    def hop(self, source, target, direction, level):
        place = self.place
        index = self.first + DEPTH * way(direction) + level
        return pltpu.make_async_remote_copy(
            src_ref=source,
            dst_ref=target,
            send_sem=self.links.send.at[index],
            recv_sem=self.links.recv.at[index],
            device_id=(place.s + 4 * direction, place.x),
            device_id_type=MESH,
        )

    def levels(self, distance, action):
        z = self.place.z
        if distance == 0:
            action(z, None)
            return

        def side(i, carry):
            direction = 1 - 2 * i
            level = z - direction * distance

            @pl.when((level >= 0) & (level < DEPTH))
            def _():
                action(level, direction)

            return carry

        lax.fori_loop(0, 2, side, 0)

    def beyond(self, direction):
        further = self.place.z + direction
        return (further >= 0) & (further < DEPTH)


class Gather(Line):
    def __init__(self, links, view, stages):
        self.links, self.view, self.stages = links, view, stages
        self.place = links.place
        self.take_line()
        self.rows = {name: links.take(DEPTH) for name in stages}

    def block(self, stage, level, theirs=False):
        where = dict(self.place.own)
        if stage is not None:
            for name in self.stages[:stage]:
                where[name] = slice(None)
            if theirs:
                where[self.stages[stage]] = 1 - where[self.stages[stage]]
        return self.view(level, where["y"], where["c"], where["x"])

    def line(self, direction, level):
        ref = self.block(None, level)
        return self.hop(ref, ref, direction, level)

    def staged(self, stage, level, theirs=False):
        name = self.stages[stage]
        ref = self.block(stage, level, theirs)
        return self.links.copy(ref, ref, self.rows[name] + level, name)

    def along(self, distance):
        def hand_on(level, direction):
            if distance:
                self.line(direction, level).wait_recv()

            @pl.when(self.beyond(direction))
            def _():
                self.line(direction, level).start()

        if distance == 0:
            hand_on(self.place.z, 1)
            hand_on(self.place.z, -1)
        else:
            self.levels(distance, hand_on)

    def depart(self, distance):
        self.levels(distance, lambda level, _: self.staged(0, level).start())

    def across(self, stage, distance):
        def pass_on(level, _):
            self.staged(stage, level, True).wait_recv()
            if stage + 1 < len(self.stages):
                self.staged(stage + 1, level).start()

        self.levels(distance, pass_on)

    def drain_line(self):
        z = self.place.z

        def sent(level, carry):
            @pl.when((z >= level) & (z < DEPTH - 1))
            def _():
                self.line(1, level).wait_send()

            @pl.when((z <= level) & (z > 0))
            def _():
                self.line(-1, level).wait_send()

            return carry

        lax.fori_loop(0, DEPTH, sent, 0)

    def drain(self):
        self.drain_line()

        def sent(level, carry):
            for stage in range(len(self.stages)):
                self.staged(stage, level).wait_send()
            return carry

        lax.fori_loop(0, DEPTH, sent, 0)


class PairGather(Gather):
    def __init__(self, links, ref):
        super().__init__(links, lambda z, y, c, x: ref.at[z, y], ["y"])
        self.ref = ref

    def line(self, direction, level):
        ref = self.ref.at[level]
        return self.hop(ref, ref, direction, level)

    def begin(self):
        self.staged(0, self.place.z).start()

    def join(self):
        self.staged(0, self.place.z, True).wait_recv()
        self.along(0)

    def drain(self):
        self.staged(0, self.place.z).wait_send()
        self.drain_line()


def add_into(target, source):
    def add(i, carry):
        target[i] = (target[i].astype(F32) + source[i].astype(F32)).astype(BF16)
        return carry

    if len(target.shape) > 2:
        lax.fori_loop(0, target.shape[0], add, 0)
    else:
        add(Ellipsis, 0)


class Reduce(Line):
    def __init__(self, links, view, stages, slots, line_slots, after=(), source=None):
        self.links, self.view, self.stages = links, view, list(stages) + list(after)
        self.slots, self.line_slots = slots, line_slots
        self.source = source or view
        self.before = len(stages)
        self.place = links.place
        self.take_line()
        self.rows = {name: links.take(DEPTH) for name in stages}
        self.rows.update({name: links.take(1) for name in after})

    def block(self, stage, level, theirs=False):
        where = dict(self.place.own)
        for name in self.stages[stage + 1 :]:
            where[name] = slice(None)
        if theirs:
            where[self.stages[stage]] = 1 - where[self.stages[stage]]
        view = self.source if theirs and stage == 0 else self.view
        return view(level, where["y"], where["c"], where["x"])

    def staged(self, stage, level):
        name = self.stages[stage]
        late = stage >= self.before
        return self.links.copy(
            self.block(stage, level, True),
            self.slots[stage] if late else self.slots[stage].at[level],
            self.rows[name] + (0 if late else level),
            name,
        )

    def late_start(self, stage):
        self.staged(stage, self.place.z).start()

    def late_take(self, stage):
        z = self.place.z
        self.staged(stage, z).wait_recv()
        add_into(self.block(stage, z), self.slots[stage])

    def slot(self, direction, level):
        return self.line_slots.at[level + 1 - way(direction)]

    def line(self, direction, level):
        ref = self.block(self.before - 1, level)
        return self.hop(ref, self.slot(direction, level), direction, level)

    def begin(self, distance):
        self.levels(distance, lambda level, _: self.staged(0, level).start())

    def across(self, stage, distance):
        def take(level, _):
            self.staged(stage, level).wait_recv()
            add_into(self.block(stage, level), self.slots[stage].at[level])
            if stage + 1 < self.before:
                self.staged(stage + 1, level).start()

        self.levels(distance, take)

    def take(self, direction, level):
        self.line(direction, level).wait_recv()
        add_into(self.block(self.before - 1, level), self.slot(direction, level))

    def along(self, distance):
        if distance == 0:

            def side(i, carry):
                direction = 1 - 2 * i

                @pl.when(self.beyond(-direction))
                def _():
                    self.take(direction, self.place.z)

                return carry

            lax.fori_loop(0, 2, side, 0)
            return

        def send(level, back):
            @pl.when(self.beyond(back))
            def _():
                self.take(-back, level)

            self.line(-back, level).start()

        self.levels(distance, send)

    def drain_line(self):
        z = self.place.z

        def sent(level, carry):
            @pl.when(z > level)
            def _():
                self.line(-1, level).wait_send()

            @pl.when(z < level)
            def _():
                self.line(1, level).wait_send()

            return carry

        lax.fori_loop(0, DEPTH, sent, 0)

    def drain(self):
        self.drain_line()

        def sent(level, carry):
            for stage in range(self.before):
                self.staged(stage, level).wait_send()
            return carry

        lax.fori_loop(0, DEPTH, sent, 0)
        for stage in range(self.before, len(self.stages)):
            self.staged(stage, self.place.z).wait_send()


class PairReduce(Reduce):
    def __init__(self, links, ref, slot, line_slots):
        super().__init__(links, lambda z, y, c, x: ref.at[z, y], ["y"], None, line_slots)
        self.ref, self.last_slot = ref, slot

    def block(self, stage, level, theirs=False):
        return self.ref.at[level]

    def final(self):
        place = self.place
        return self.links.copy(
            self.ref.at[place.z, 1 - place.y], self.last_slot, self.rows["y"], "y"
        )

    def finish(self):
        self.final().wait_recv()
        add_into(self.ref.at[self.place.z, self.place.y], self.last_slot)

    def drain(self):
        self.drain_line()
        self.final().wait_send()


class Plan:
    def __init__(self):
        self.steps = []

    def add(self, needs, action, *args, busy=False):
        self.steps.append((tuple(needs), functools.partial(action, *args), busy))
        return len(self.steps) - 1

    def run(self, order):
        seen = set()
        assert sorted(order) == list(range(len(self.steps)))
        for index in order:
            needs, action, _ = self.steps[index]
            assert seen.issuperset(needs)
            action()
            seen.add(index)


def mean_of(values):
    return jnp.mean(values, axis=1, keepdims=True)


def layer_kernel(
    length_ref,
    x_ref,
    grad_ref,
    grad_rows_ref,
    vectors_ref,
    in_ref,
    out_ref,
    gate_ref,
    up_ref,
    down_ref,
    mixer_hbm,
    parts_hbm,
    middle_hbm,
    mixer_grad,
    small,
    result_ref,
    input_grad,
    gate_grad,
    up_grad,
    down_grad,
    wm,
    w0,
    w1,
    w2,
    w3,
    product,
    middle,
    tokens,
    grads,
    r0,
    r1,
    r2,
    r3,
    l0,
    l1,
    l2,
    l3,
    e0,
    e1,
    e2,
    e3,
    acts,
    out_sum,
    back_sum,
    keep_sem,
    send,
    recv,
):
    place = Place()
    links = Links(place, send, recv)
    plan = Plan()
    rows, depth = parts_hbm.shape[0] // 3, parts_hbm.shape[1]
    tile = rows // 2
    weights, edges = (w0, w1, w2, w3), (e0, e1, e2, e3)
    quarter = sum(PARTS)
    offsets = [sum(PARTS[:k]) for k in range(len(PARTS))]

    def columns(first, count):
        return lambda z, y, c, x: wm.at[z, y, c, x, :, pl.ds(first, count)]

    mixers = [
        Gather(links, columns(depth * j, depth), stages)
        for j, stages in MIXER
    ]
    gathers, reduces = [], []
    for kind, w, r, l in zip(KINDS, weights, (r0, r1, r2, r3), (l0, l1, l2, l3)):
        if kind == "y":
            gathers.append(PairGather(links, w))
            reduces.append(PairReduce(links, w, r, l))
        else:
            view = lambda z, y, c, x, w=w: w.at[z, y]
            gathers.append(Gather(links, view, ["y"]))
            reduces.append(Reduce(links, view, ["y"], [r], l))

    def sides(number, quarter_index):
        width = PARTS[number]
        start = pl.multiple_of(quarter_index * quarter + offsets[number], 128)
        return [
            (ref.at[:, pl.ds(start, width)], pl.ds(side * width, width))
            for side, ref in enumerate((gate_ref, up_ref, down_ref))
        ]

    twins = [
        [
            links.copy(
                source,
                weights[number].at[place.z, place.y, place.c, :, where],
                links.take(1),
                "c",
            )
            for source, where in sides(number, 1 - place.c)
        ]
        for number in range(len(PARTS))
    ]


    def share(ref):
        first = links.take(3)
        return (
            links.copy(ref[0], ref[1], first, "c"),
            links.copy(ref[0], ref[2], first + 1, "x"),
            links.copy(ref[2], ref[3], first + 2, "c"),
        )

    shared_grads = [
        share([grads.at[i // 2, 2 * (i % 2) + h, q] for i in range(4)])
        for h in range(2)
        for q in range(2)
    ]
    shared_tokens = [
        share([tokens.at[i // 2, 2 * (i % 2) + h] for i in range(4)]) for h in range(2)
    ]
    edge = links.copy(
        product.at[pl.ds(rows, 8)], product.at[pl.ds(0, 8)], links.take(1), "next"
    )
    back_edge = links.copy(
        middle.at[pl.ds(0, 8)], middle.at[pl.ds(rows, 8)], links.take(1), "prev"
    )
    has_next, has_prev = place.s < place.last, place.s > 0
    slots = [
        wm.at[pl.ds(2 * (i // 4), 2), :, :, :, :, pl.ds(depth * (i % 4), depth)]
        for i in range(6)
    ]

    def give_back(total, slots):
        first = links.take(3)
        return (
            links.copy(total.at[3], slots[2], first, "c"),
            links.copy(total.at[2], slots[1], first + 1, "x"),
            links.copy(total.at[1], slots[0], first + 2, "c"),
        )

    returned = [give_back(back_sum, slots[:3]), give_back(out_sum, slots[3:])]
    trades = [
        links.copy(w.at[place.z, place.y, 1 - place.c], e, links.take(1), "c")
        for w, e in zip(weights, edges)
    ]

    count = iter(range(keep_sem.shape[0]))

    def local(source, target):
        return pltpu.make_async_copy(source, target, keep_sem.at[next(count)])

    parts = acts.at[pl.ds(0, 3 * rows), pl.ds(0, depth)]
    save_mixer = local(wm, mixer_hbm)
    save_parts = local(parts, parts_hbm)
    save_middle = local(middle.at[pl.ds(0, rows)], middle_hbm)
    fills = [
        [
            local(source, weights[number].at[place.z, place.y, place.c, :, where])
            for source, where in sides(number, place.c)
        ]
        for number in range(len(PARTS))
    ]
    mine = wm.at[place.z, place.y, place.c, place.x]
    fill_in = local(in_ref, mine.at[:, pl.ds(0, 3 * depth)])
    fill_out = local(out_ref, mine.at[:, pl.ds(3 * depth, depth)])
    inner = pl.ds(0, rows)
    low_x, high_x = out_sum.at[1], back_sum.at[0]
    view = (2,) + tokens.shape[2:]
    load_x = [local(x_ref, x) for x in (low_x, high_x)]
    load_grad = local(grad_ref, grads.at[0, pl.ds(0, 2)])
    load_grad_rows = local(grad_rows_ref, acts.at[pl.ds(3 * rows, rows), pl.ds(0, depth)])
    save_result = local(back_sum.at[1], result_ref)
    blocks = [tokens.at[0], tokens.at[1], grads.at[0], grads.at[1]]
    load_mixer = [
        local(mixer_hbm.at[:, :, :, :, :, pl.ds(depth * j, depth)], block)
        for j, block in enumerate(blocks)
    ]
    load_parts = local(parts_hbm, parts)
    load_middle = local(middle_hbm, product.at[pl.ds(8, rows)])
    staging = [acts.at[pl.ds(2 * rows * i, 2 * rows), pl.ds(depth, 2 * tile)] for i in range(2)]
    stores = [
        local(staging[j % 2], mixer_grad.at[:, pl.ds(2 * tile * ((j + 6) % 8), 2 * tile)])
        for j in range(8)
    ]
    save_grad, save_inputs = (
        local(middle.at[pl.ds(0, rows)], input_grad) for _ in range(2)
    )
    load_back = local(input_grad, middle.at[pl.ds(0, rows)])

    def hear(*copies):
        for copy in copies:
            copy.wait_recv()

    def begin(*copies):
        for copy in copies:
            copy.start()

    def done(*copies):
        for copy in copies:
            copy.wait()

    def valid_rows(first, count):
        position = place.s * rows + first + lax.broadcasted_iota(
            jnp.int32, (count, 1), 0
        )
        return (position < length_ref[0]).astype(F32)

    def open_all():
        for copy in [fill_in, fill_out, load_x[0], load_grad] + sum(fills, []):
            copy.start()
        place.greet(["c", "y", "x", "up", "down", "next", "prev"])
        fill_in.wait()
        fill_out.wait()

    def clear():
        @pl.when(place.s == 0)
        def _():
            product[pl.ds(0, 8)] = jnp.zeros((8, depth), F32)

        @pl.when(place.s == place.last)
        def _():
            middle[pl.ds(rows, 8)] = jnp.zeros((8, depth), F32)

    def first_norm(source, target):
        x = source[...].reshape(rows, depth).astype(F32)
        scale = lax.rsqrt(mean_of(x * x) + epsilon)
        normed = (x * scale * vectors_ref[0:1]).astype(BF16)
        target[...] = normed.reshape(view)

    def mask_grads():
        masked = grads[0, pl.ds(0, 2)].reshape(rows, depth).astype(F32)
        masked *= valid_rows(0, rows)
        grads[0, pl.ds(0, 2)] = masked.astype(BF16).reshape(view)

    def project(index):
        weight = wm[..., depth * index : depth * (index + 1)].reshape(depth, depth)
        acts[rows * index : rows * (index + 1), :depth] = dot(
            out_sum[0].reshape(rows, depth), weight
        ).astype(BF16)

    def multiply():
        b_part = acts[:rows, :depth].astype(F32)
        v_part = acts[2 * rows : 3 * rows, :depth].astype(F32)
        product[pl.ds(8, rows)] = (b_part * v_part).astype(BF16).astype(F32)

    def conv_rows(start):
        total = 0.0
        for tap in range(3):
            first = start + 6 + tap
            total += vectors_ref[1 + tap : 2 + tap] * product[first : first + tile]
        return total

    def mix(index):
        start = tile * index
        where = slice(start, start + tile)
        c_part = acts[rows + start : rows + start + tile, :depth].astype(F32)
        gated = (c_part * conv_rows(start)).astype(BF16)
        weight = wm[..., 3 * depth :].reshape(depth, depth)
        x = low_x[index].reshape(tile, depth).astype(F32)
        total = x + valid_rows(start, tile) * dot(gated, weight)
        middle[where] = total
        scale = lax.rsqrt(mean_of(total * total) + epsilon)
        new = (total * scale * vectors_ref[4:5]).astype(BF16)
        tokens[0, index] = new.reshape(tokens.shape[2:])

    def one_block(number, pair, i, carry):
        weight, width, spot = weights[number], PARTS[number], SPOTS[number]
        where = pl.ds(pl.multiple_of(rows * (2 * pair + i), rows), rows)
        gate_up = weight[..., : 2 * width].reshape(depth, 2 * width)
        both = dot(tokens[pair, pl.ds(2 * i, 2)].reshape(rows, depth), gate_up)
        gate, up = both[:, :width], both[:, width:]
        sigmoid = jax.nn.sigmoid(gate)
        silu = gate * sigmoid
        slope = sigmoid + silu * (1.0 - sigmoid)
        kept = (silu * up).astype(BF16)
        down = weight[..., 2 * width :].reshape(depth, width)
        grad_hidden = dot(grads[pair, pl.ds(2 * i, 2)].reshape(rows, depth), down)
        acts[where, spot : spot + width] = (grad_hidden * up * slope).astype(BF16)
        acts[where, spot + width : spot + 2 * width] = (grad_hidden * silu).astype(BF16)
        acts[where, spot + 2 * width : spot + 3 * width] = kept
        out_part = by_rows(kept, down)
        back_part = by_rows(acts[where, spot : spot + 2 * width], gate_up)
        shape = out_sum.shape[1:]
        index = 2 * pair + i
        if number != ORDER[0]:
            out_part += out_sum[index].reshape(rows, depth).astype(F32)
            back_part += back_sum[index].reshape(rows, depth).astype(F32)
        out_sum[index] = out_part.astype(BF16).reshape(shape)
        back_sum[index] = back_part.astype(BF16).reshape(shape)
        return carry

    def block(number, pair):
        lax.fori_loop(0, 2, functools.partial(one_block, number, pair), 0)

    def weigh(number):
        weight, width, spot = weights[number], PARTS[number], SPOTS[number]
        for source, first, size in ((tokens, 0, 2 * width), (grads, 2 * width, width)):
            step = 256 if size % 256 == 0 else size

            def column(i, carry):
                factor = acts[:, pl.ds(pl.multiple_of(spot + first + i * step, 128), step)]
                part = over_rows(source[...].reshape(4 * rows, depth), factor)
                where = pl.ds(pl.multiple_of(first + i * step, 128), step)
                weight[..., where] = part.astype(BF16).reshape(
                    weight.shape[:-1] + (step,)
                )
                return carry

            lax.fori_loop(0, size // step, column, 0)

    def lift(index):
        hear(returned[index][0])
        add_into((back_sum, out_sum)[index].at[2], slots[3 * index + 2])
        begin(returned[index][1])

    def returned_rows(index, start):
        total = (back_sum, out_sum)[index]
        i = start // tile
        found = total[0, i].reshape(tile, depth).astype(F32)
        for slot in slots[3 * index : 3 * index + 2]:
            found += slot[i].reshape(tile, depth).astype(F32)
        return found

    def note(row, values, fresh):
        total = jnp.sum(values, axis=0, keepdims=True)
        small[row : row + 1] = total if fresh else small[row : row + 1] + total

    def turn(index):
        start = tile * index
        where = slice(start, start + tile)
        part = returned_rows(0, start)
        total = middle[where]
        scale = lax.rsqrt(mean_of(total * total) + epsilon)
        hat = total * scale
        note(4, part * hat, index == 0)
        scaled = part * vectors_ref[4:5]
        spot = slice(3 * rows + start, 3 * rows + start + tile)
        grad = acts[spot, :depth].astype(F32) + scale * (
            scaled - hat * mean_of(scaled * hat)
        )
        middle[where] = grad
        acts[spot, :depth] = (valid_rows(start, tile) * grad).astype(BF16)

    def unmix(index):
        start = tile * index
        spot = slice(rows + start, rows + start + tile)
        weight = grads[1].reshape(depth, depth)
        gated_grad = by_rows(
            acts[3 * rows + start : 3 * rows + start + tile, :depth], weight
        )
        c_part = acts[spot, :depth].astype(F32)
        conv = conv_rows(start)
        back_sum[3, index] = (c_part * conv).astype(BF16).reshape(tokens.shape[2:])
        acts[spot, :depth] = (gated_grad * conv).astype(BF16)
        conv_grad = gated_grad * c_part
        middle[start : start + tile] = conv_grad
        for tap in range(3):
            first = start + 6 + tap
            note(1 + tap, conv_grad * product[first : first + tile], index == 0)

    def unconv(index):
        start = tile * index
        grad = 0.0
        for tap in range(3):
            first = start + 2 - tap
            grad += vectors_ref[1 + tap : 2 + tap] * middle[first : first + tile]
        b_spot = slice(start, start + tile)
        v_spot = slice(2 * rows + start, 2 * rows + start + tile)
        b_part = acts[b_spot, :depth].astype(F32)
        v_part = acts[v_spot, :depth].astype(F32)
        acts[b_spot, :depth] = (grad * v_part).astype(BF16)
        acts[v_spot, :depth] = (grad * b_part).astype(BF16)

    def project_back(index):
        start = tile * index
        where = slice(start, start + tile)
        part = 0.0
        for j in range(3):
            spot = slice(rows * j + start, rows * j + start + tile)
            part += by_rows(acts[spot, :depth], blocks[j][...].reshape(depth, depth))
        x = high_x[index].reshape(tile, depth).astype(F32)
        scale = lax.rsqrt(mean_of(x * x) + epsilon)
        hat = x * scale
        note(0, part * hat, index == 0)
        scaled = part * vectors_ref[0:1]
        middle[where] = middle[where] + scale * (scaled - hat * mean_of(scaled * hat))

    def weigh_mixer(j):
        if j >= 2:
            stores[j - 2].wait()
        wide = 2 * tile
        if j >= 2:
            first = rows * (j // 2 - 1)
            left = back_sum[2].reshape(rows, depth)
        else:
            first = 3 * rows
            left = back_sum[3].reshape(rows, depth)
        start = wide * (j % 2)
        part = over_rows(left, acts[first : first + rows, start : start + wide])
        staging[j % 2][...] = part.astype(BF16)
        stores[j].start()

    def close_result():
        for index in range(2):
            start = tile * index
            total = product[8 + start : 8 + start + tile] + valid_rows(
                start, tile
            ) * returned_rows(1, start)
            back_sum[1, index] = total.astype(BF16).reshape(tokens.shape[2:])
        save_result.start()

    def own(number):
        width = PARTS[number]
        for side, target in enumerate((gate_grad, up_grad, down_grad)):
            spot = pl.ds(side * width, width)
            mine = pl.multiple_of(place.c * quarter + offsets[number], 128)
            twin = pl.multiple_of((1 - place.c) * quarter + offsets[number], 128)
            target[:, pl.ds(mine, width)] = weights[number][
                place.z, place.y, place.c, :, spot
            ]
            target[:, pl.ds(twin, width)] = edges[number][:, spot]

    def work_on(needs, action, *args):
        return plan.add(needs, action, *args, busy=True)

    start = plan.add([], open_all)
    for part in mixers:
        plan.add([start], part.along, 0)
        plan.add([start], part.depart, 0)
    for twin in twins:
        plan.add([start], begin, *twin)
    plan.add([start], clear)
    masked = plan.add([start], load_grad.wait)
    masked = work_on([masked], mask_grads)
    plan.add([masked], begin, *[group[0] for group in shared_grads])
    early = [plan.add([masked], begin, group[1]) for group in shared_grads[:EARLY]]
    norm = plan.add([start], load_x[0].wait)
    norm = work_on([norm], first_norm, low_x, out_sum.at[0])
    filled = [plan.add([start], done, *copies) for copies in fills]
    arrived = [
        plan.add([filled[number]], hear, *twins[number]) for number in range(len(PARTS))
    ]

    gone, whole, passed = [], {}, []
    for number, part in enumerate(mixers):
        last = {(0, 0): start}
        for distance in range(1, DEPTH):
            step = plan.add([start], part.along, distance)
            last[0, distance] = plan.add([step], part.depart, distance)
            passed += [step] * (distance == Z_GATE)
        for stage in range(3):
            for distance in range(DEPTH):
                last[stage + 1, distance] = plan.add(
                    [last[stage, distance]], part.across, stage, distance
                )
        gone += [last[stage, d] for stage in (0, 1) for d in range(DEPTH)]
        whole[MIXER[number][0]] = list(last.values())

    ready = {}
    z_gate, y_gate = [start] + passed, list(gone)
    pair_opening = passed if PAIR_EARLY else gone
    pair_gate = {}
    for number in PAIRS:
        pair_gate[number] = [plan.add([arrived[number]] + pair_opening, gathers[number].begin)]
    for number in ORDER:
        part = gathers[number]
        opening = part.join if KINDS[number] == "y" else functools.partial(part.along, 0)
        found = [plan.add([arrived[number]] + z_gate + pair_gate.get(number, []), opening)]
        for distance in range(1, DEPTH):
            found.append(plan.add(found[-1:], part.along, distance))
        z_gate = found[1:2]
        if KINDS[number] == "z":
            sends = [
                plan.add([found[distance]] + y_gate, part.depart, distance)
                for distance in range(DEPTH)
            ]
            y_gate = sends[1:2]
            last_sends = sends
            found += sends
            found += [
                plan.add([sends[distance]], part.across, 0, distance)
                for distance in range(DEPTH)
            ]
        ready[number] = found

    y_gate = last_sends

    x_free = early + [
        plan.add(gone, begin, group[1]) for group in shared_grads[EARLY:]
    ]
    b_step = work_on(whole[0] + [norm], project, 0)
    v_step = work_on(whole[2] + [norm], project, 2)
    times = work_on([b_step, v_step], multiply)

    def send_edge():
        pl.when(has_next)(edge.start)

    def take_edge():
        pl.when(has_prev)(edge.wait_recv)

    def edge_sent():
        pl.when(has_next)(edge.wait_send)

    sent = plan.add([times], send_edge)
    c_step = work_on(whole[1] + [times], project, 1)
    saving = plan.add([c_step], begin, save_parts)
    late_mix = work_on(whole[3] + [c_step, sent], mix, 1)
    drained = plan.add([late_mix], lambda: [part.drain() for part in mixers])
    saved = plan.add([drained], begin, save_mixer)
    token_sends = {}
    token_sends[1] = plan.add([late_mix] + x_free, begin, *shared_tokens[1][1::-1])
    edge_in = plan.add([sent], take_edge)
    mixed = work_on([edge_in, late_mix], mix, 0)
    kept = plan.add([mixed, saved], lambda: (save_middle.start(), save_mixer.wait()))
    token_sends[0] = plan.add([kept, token_sends[1]], begin, *shared_tokens[0][1::-1])

    grads_x, tokens_x = [], []

    def pass_grads(group):
        hear(group[1])
        begin(group[2])

    for step, group in zip(x_free, shared_grads):
        grads_x.append(plan.add([step], pass_grads, group))
    for h in (1, 0):
        group = shared_tokens[h]

        def pass_on(group=group):
            hear(group[1])
            begin(group[2])

        tokens_x.append(plan.add([token_sends[h]], pass_on))
    near = plan.add(
        [token_sends[0], masked],
        hear,
        *[group[0] for group in shared_grads + shared_tokens],
    )
    far = plan.add(
        tokens_x + grads_x, hear, *[group[2] for group in shared_grads + shared_tokens]
    )
    def flush():
        done(save_parts, save_middle)
        edge_sent()

    flushed = plan.add([kept, mixed], flush)
    own_side, other_side = [near, flushed], [near, far, flushed]
    blocks_done = {}
    weighed = {}
    reduced = {}
    previous = []

    def reduce_steps(number, needs):
        part = reduces[number]
        if KINDS[number] == "y":
            chain = list(needs)
            steps = []
            for distance in (3, 2, 1, 0):
                chain = [plan.add(chain, part.along, distance)]
                steps += chain
            chain = [plan.add(chain, lambda: part.final().start())]
            steps.append(plan.add(chain, part.finish))
            return steps
        steps = []
        opened = {
            distance: plan.add(needs + y_gate, part.begin, distance)
            for distance in (3, 2, 1, 0)
        }
        chain = []
        for distance in (3, 2, 1, 0):
            step = plan.add([opened[distance]], part.across, 0, distance)
            chain = [plan.add([step] + chain, part.along, distance)]
            steps += [step] + chain
        return steps

    def drain_and_weigh(number, needs):
        drain = plan.add(needs, gathers[number].drain)
        weighed[number] = work_on([drain], weigh, number)
        reduced[number] = reduce_steps(number, [weighed[number]])

    def columns_of(number):
        return set(range(SPOTS[number], SPOTS[number] + 3 * PARTS[number], 128))

    def run_block(number, pair):
        needs = [
            weighed[other]
            for other in ORDER[: ORDER.index(number)]
            if columns_of(other) & columns_of(number)
        ]
        blocks_done[number, pair] = work_on(
            ready[number] + (other_side if pair else own_side) + needs, block, number, pair
        )

    def finish_part(number):
        drain_and_weigh(number, [blocks_done[number, 0], blocks_done[number, 1]])

    first, second, third, fourth = ORDER
    for number in (first, second):
        if not columns_of(first) & columns_of(second):
            run_block(number, 0)
    for number in (first, second):
        if columns_of(first) & columns_of(second):
            run_block(number, 0)
        run_block(number, 1)
        finish_part(number)
    run_block(third, 1)
    run_block(fourth, 1)
    last_far = [blocks_done[third, 1], blocks_done[fourth, 1]]
    back_up = plan.add(last_far, begin, returned[0][0])
    out_up = plan.add([back_up], begin, returned[1][0])
    back_over = plan.add([back_up], lift, 0)
    run_block(third, 0)
    run_block(fourth, 0)
    near_done = [blocks_done[third, 0], blocks_done[fourth, 0]]
    back_near = plan.add(near_done + [back_over], begin, returned[0][2])
    out_over = plan.add([out_up, back_over], lift, 1)
    out_near = plan.add([back_near, out_over], begin, returned[1][2])
    finish_part(third)
    finish_part(fourth)

    def sent_tokens():
        for group in shared_grads + shared_tokens:
            for copy in group:
                copy.wait_send()

    freed = plan.add([weighed[number] for number in ORDER], sent_tokens)
    loads = plan.add(
        [freed], begin, load_parts, load_grad_rows, *load_mixer
    )
    back_in = plan.add([back_near], hear, returned[0][1], returned[0][2])
    loaded = plan.add([loads], done, load_parts, load_grad_rows, *load_mixer)
    turned = [work_on([back_in, loaded], turn, index) for index in range(2)]

    def free_sums():
        done(save_grad)
        for copy in returned[0]:
            copy.wait_send()
        load_x[1].start()

    freed = plan.add(turned, save_grad.start)
    freed = plan.add([freed], free_sums)
    unmixed = [work_on([freed], unmix, index) for index in range(2)]
    again = plan.add([freed], load_x[1].wait)
    again = work_on([again], first_norm, high_x, back_sum.at[2])

    def send_back():
        pl.when(has_prev)(back_edge.start)

    def take_back():
        pl.when(has_next)(back_edge.wait_recv)

    def back_sent():
        pl.when(has_prev)(back_edge.wait_send)

    back_edge_sent = plan.add([unmixed[0]], send_back)
    weigh_steps = [work_on(unmixed, weigh_mixer, j) for j in (0, 1)]
    low = work_on([unmixed[1], back_edge_sent], unconv, 0)
    taken = plan.add([back_edge_sent], take_back)
    high = work_on([taken, low], unconv, 1)
    fetched = plan.add([low, high] + [edge_in], begin, load_middle)
    for j in range(2, 8):
        weigh_steps.append(work_on([again, low, high, weigh_steps[-1]], weigh_mixer, j))
    revived = plan.add([low, high], lambda: (back_sent(), load_back.start()))
    revived = plan.add([revived, weigh_steps[-1]], load_back.wait)
    projected = [work_on([revived], project_back, index) for index in range(2)]
    stored = plan.add(projected, begin, save_inputs)
    def finish_result():
        load_middle.wait()
        close_result()

    out_in = plan.add([out_near, fetched], hear, returned[1][1], returned[1][2])
    finished = work_on([out_in, fetched] + weigh_steps, finish_result)

    finals = []
    for number in ORDER:
        trade = plan.add(reduced[number], begin, trades[number])
        heard = plan.add([trade], hear, trades[number])
        finals.append(work_on([heard], own, number))

    def close():
        small[pl.ds(5, 3)] = jnp.zeros((3, depth), F32)
        done(save_inputs, save_result, *stores[6:8])
        for reduce in reduces:
            reduce.drain()
        for group in returned[1:] + twins + [trades]:
            for copy in group:
                copy.wait_send()

    plan.add(finals + weigh_steps + projected + [stored, finished], close)
    plan.run(STEPS or list(range(len(plan.steps))))


def layer(lengths, inputs, cotangent, vectors, shards):
    rows, depth = inputs.shape
    ffn_columns = shards[2].shape[1]
    vmem = pl.BlockSpec(memory_space=pltpu.VMEM)
    hbm = pl.BlockSpec(memory_space=pl.ANY)
    shape = jax.ShapeDtypeStruct
    blocks = (DEPTH, 2, 2, 2, depth // (8 * DEPTH))
    half = (2, 2, 2, 2, rows // 16, depth)
    out_shape = [
        shape(blocks + (4 * depth,), BF16),
        shape((3 * rows, depth), BF16),
        shape((rows, depth), F32),
        shape((depth, 4 * depth), BF16),
        shape((8, depth), F32),
        shape(half, BF16),
        shape((rows, depth), F32),
    ] + [shape((64, ffn_columns), BF16)] * 3
    pair = (2, 64)
    widths = [3 * w for w in PARTS]

    def slots(lead, width, kind):
        if kind == "y":
            return (lead, 2) if lead > DEPTH else ()
        return (lead,)

    token = (2, 4, 2, 2, 2, 32, depth)
    total = (4, 2, 2, 2, 2, 32, depth)
    scratch = (
        [pltpu.VMEM(blocks + (4 * depth,), BF16)]
        + [pltpu.VMEM((DEPTH, 2) + pair + (w,), BF16) for w in widths]
        + [
            pltpu.VMEM((rows + 8, depth), F32),
            pltpu.VMEM((rows + 8, depth), F32),
        ]
        + [pltpu.VMEM(token, BF16)] * 2
        + [
            pltpu.VMEM(slots(lead, w, kind) + pair + (w,), BF16)
            for lead in (DEPTH, DEPTH + 1)
            for w, kind in zip(widths, KINDS)
        ]
        + [pltpu.VMEM((64, w), BF16) for w in widths]
        + [pltpu.VMEM((4 * rows, ACTS), BF16)]
        + [pltpu.VMEM(total, BF16)] * 2
        + [
            pltpu.SemaphoreType.DMA((40,)),
            pltpu.SemaphoreType.DMA((240,)),
            pltpu.SemaphoreType.DMA((240,)),
        ]
    )
    smem = pl.BlockSpec(memory_space=pltpu.SMEM)
    return pl.pallas_call(
        layer_kernel,
        out_shape=out_shape,
        in_specs=[smem] + [hbm] * 3 + [vmem] + [hbm] * 5,
        out_specs=[hbm] * 4 + [vmem, hbm, hbm] + [vmem] * 3,
        scratch_shapes=scratch,
        compiler_params=pltpu.CompilerParams(
            collective_id=0, has_side_effects=True, vmem_limit_bytes=63 * 2**20
        ),
    )(
        lengths,
        inputs.reshape(half),
        cotangent.reshape(half),
        cotangent,
        vectors,
        *shards
    )


def reduce_kernel(grad_ref, small_ref, in_grad, out_grad, sum_ref, work, small, *rest):
    slots, (load_sem, send, recv) = rest[:-3], rest[-3:]
    place = Place()
    links = Links(place, send, recv)
    plan = Plan()
    depth = in_grad.shape[1] // 3
    parts = []
    remaining = list(slots)
    for j, before, after in MIXER_GRADS:
        where = pl.ds(depth * j, depth)
        count = len(before) + 1 + len(after)
        mine, remaining = remaining[:count], remaining[count:]
        parts.append(
            Reduce(
                links,
                lambda z, y, c, x, where=where: work.at[z, y, x, :, where],
                before,
                mine[: len(before)] + mine[len(before) + 1 :],
                mine[len(before)],
                after,
                lambda z, y, c, x, where=where: grad_ref.at[z, y, c, x, :, where],
            )
        )
    loads = [
        pltpu.make_async_copy(
            grad_ref.at[:, :, place.c, :, :, pl.ds(depth * j, depth)],
            work.at[:, :, :, :, pl.ds(depth * j, depth)],
            load_sem.at[number],
        )
        for number, (j, _, _) in enumerate(MIXER_GRADS)
    ]
    ring = ("c", "x", "y", "pair", "far")
    first = links.take(len(ring))
    rounds = [
        links.copy(small.at[i], small.at[len(ring) + 1 + i], first + i, name)
        for i, name in enumerate(ring)
    ]

    def open_all():
        for load in loads:
            load.start()
        place.greet(["c", "y", "x", "up", "down", "far"])
        small[0] = small_ref[...]

    start = plan.add([], open_all)
    opened = [
        [plan.add([start], part.begin, distance) for distance in (3, 2, 1, 0)]
        for part in parts
    ]
    ends = []
    for part, load, begun in zip(parts, loads, opened):
        loaded = plan.add([start], load.wait)
        line = []
        for number, distance in enumerate((3, 2, 1, 0)):
            step = plan.add([loaded, begun[number]], part.across, 0, distance)
            for stage in range(1, part.before):
                step = plan.add([step], part.across, stage, distance)
            line = [plan.add([step] + line, part.along, distance)]
        for stage in range(part.before, len(part.stages)):
            line = [plan.add(line, part.late_start, stage)]
            line = [plan.add(line, part.late_take, stage)]
        ends += line

    def add_round(number):
        rounds[number].wait_recv()
        small[number + 1] = small[number] + small[len(ring) + 1 + number]

    step = plan.add(sum(opened, []), rounds[0].start)
    for number in range(len(ring)):
        step = plan.add([step], add_round, number)
        if number + 1 < len(ring):
            step = plan.add([step], rounds[number + 1].start)

    def close():
        sum_ref[...] = small[len(ring)]
        own = work[place.z, place.y, place.x].astype(F32)
        in_grad[...] = own[:, : 3 * depth]
        out_grad[...] = own[:, 3 * depth :]
        for part in parts:
            part.drain()
        for copy in rounds:
            copy.wait_send()

    plan.add(ends + [step], close)
    plan.run(LAST_STEPS or list(range(len(plan.steps))))


def reduce_all(grad, small):
    columns = grad.shape[-1]
    depth = columns // 4
    block = (grad.shape[-2], depth)
    slots = []
    for _, before, after in MIXER_GRADS:
        left = len(before) + len(after)
        for _ in before:
            left -= 1
            slots.append((DEPTH,) + (2,) * left + block)
        slots.append((DEPTH + 1,) + (2,) * left + block)
        for _ in after:
            left -= 1
            slots.append((2,) * left + block)
    vmem = pl.BlockSpec(memory_space=pltpu.VMEM)
    hbm = pl.BlockSpec(memory_space=pl.ANY)
    return pl.pallas_call(
        reduce_kernel,
        out_shape=[
            jax.ShapeDtypeStruct((block[0], 3 * depth), F32),
            jax.ShapeDtypeStruct((block[0], depth), F32),
            jax.ShapeDtypeStruct(small.shape, F32),
        ],
        in_specs=[hbm, vmem],
        out_specs=[vmem] * 3,
        scratch_shapes=[
            pltpu.VMEM((DEPTH, 2, 2) + block[:1] + (columns,), BF16),
            pltpu.VMEM((11,) + small.shape, F32),
        ]
        + [pltpu.VMEM(slot, BF16) for slot in slots]
        + [
            pltpu.SemaphoreType.DMA((len(MIXER_GRADS),)),
            pltpu.SemaphoreType.DMA((96,)),
            pltpu.SemaphoreType.DMA((96,)),
        ],
        compiler_params=pltpu.CompilerParams(
            collective_id=2, has_side_effects=True, vmem_limit_bytes=58 * 2**20
        ),
    )(grad, small)


def shifted(block, axis, distance):
    devices = range(lax.axis_size(axis))
    route = [(i - distance, i) for i in devices if i - distance in devices]
    return lax.ppermute(block, axis, route)


def mixer_forward(inputs, lengths, norm_one_gain, conv_weight, norm_two_gain, in_all, out_all):
    tok_rows, feat_width = inputs.shape[1:]
    kept = {}
    x_float = inputs[0].astype(F32)
    kernel = conv_weight.astype(F32)
    position = lax.axis_index("seq") * tok_rows + lax.iota(jnp.int32, tok_rows)
    valid_mask = (position < lengths[0]).astype(F32)[:, None]
    scale_one = lax.rsqrt(jnp.mean(x_float * x_float, axis=1, keepdims=True) + epsilon)
    hat_one = x_float * scale_one
    normed_one = (hat_one * norm_one_gain.astype(F32)).astype(BF16)
    projected = rounded_dot(normed_one, in_all)
    b_part = projected[:, :feat_width]
    c_part = projected[:, feat_width : 2 * feat_width]
    v_part = projected[:, 2 * feat_width :]
    product = (b_part * v_part).astype(BF16)
    carried = shifted(product[tok_rows - 2 :], "seq", 1)
    extended = jnp.concatenate([carried, product], axis=0).astype(F32)
    conv_out = (
        kernel[0] * extended[:tok_rows]
        + kernel[1] * extended[1 : tok_rows + 1]
        + kernel[2] * extended[2:]
    )
    gated_mix = (c_part * conv_out).astype(BF16)
    mixer_out = rounded_dot(gated_mix, out_all)
    middle = x_float + valid_mask * mixer_out
    scale_two = lax.rsqrt(jnp.mean(middle * middle, axis=1, keepdims=True) + epsilon)
    hat_two = middle * scale_two
    normed_two = (hat_two * norm_two_gain.astype(F32)).astype(BF16)
    kept.update(locals())
    return kept


def mixer_backward(kept, grad_out, normed_part, norm_one_gain, norm_two_gain, in_all, out_all):
    tok_rows, feat_width = grad_out.shape
    kernel = kept["kernel"]
    extended, conv_out = kept["extended"], kept["conv_out"]
    hat_one, hat_two = kept["hat_one"], kept["hat_two"]
    grad_gain_two = jnp.sum(normed_part * hat_two, axis=0)
    scaled_two = normed_part * norm_two_gain.astype(F32)
    grad_middle = grad_out + kept["scale_two"] * (
        scaled_two - hat_two * jnp.mean(scaled_two * hat_two, axis=1, keepdims=True)
    )
    grad_mix = (kept["valid_mask"] * grad_middle).astype(BF16)
    grad_out_w = over_rows(kept["gated_mix"], grad_mix)
    grad_gated = by_rows(grad_mix, out_all)
    grad_c = grad_gated * conv_out
    grad_conv_in = grad_gated * kept["c_part"]
    grad_kernel = jnp.stack(
        [
            jnp.sum(grad_conv_in * extended[:tok_rows], axis=0),
            jnp.sum(grad_conv_in * extended[1 : tok_rows + 1], axis=0),
            jnp.sum(grad_conv_in * extended[2:], axis=0),
        ]
    )
    padded_grad = jnp.pad(grad_conv_in, ((2, 2), (0, 0)))
    grad_extended = (
        kernel[0] * padded_grad[2 : tok_rows + 4]
        + kernel[1] * padded_grad[1 : tok_rows + 3]
        + kernel[2] * padded_grad[: tok_rows + 2]
    )
    returned = shifted(grad_extended[:2], "seq", -1)
    grad_product = grad_extended[2:] + jnp.concatenate(
        [jnp.zeros((tok_rows - 2, feat_width), F32), returned], axis=0
    )
    grad_projected = jnp.concatenate(
        [grad_product * kept["v_part"], grad_c, grad_product * kept["b_part"]], axis=1
    ).astype(BF16)
    grad_in_w = over_rows(kept["normed_one"], grad_projected)
    grad_normed_one = by_rows(grad_projected, in_all)
    grad_gain_one = jnp.sum(grad_normed_one * hat_one, axis=0)
    scaled_one = grad_normed_one * norm_one_gain.astype(F32)
    grad_inputs = grad_middle + kept["scale_one"] * (
        scaled_one - hat_one * jnp.mean(scaled_one * hat_one, axis=1, keepdims=True)
    )
    return grad_inputs, grad_in_w, grad_out_w, grad_gain_one, grad_kernel, grad_gain_two


def in_blocks(
    inputs,
    lengths,
    norm_one_gain,
    w_in,
    conv_weight,
    w_out,
    norm_two_gain,
    w_gate,
    w_up,
    w_down,
    cotangent,
):
    width = inputs.shape[2]
    vectors = jnp.concatenate([norm_one_gain[None], conv_weight, norm_two_gain[None]])
    found = layer(
        lengths,
        inputs[0],
        cotangent[0],
        vectors.astype(F32),
        (w_in, w_out, w_gate, w_up, w_down.T),
    )
    mixer_grad, small, result, grad_inputs, gate, up, down = found[3:]
    in_grad, out_grad, total = reduce_all(
        mixer_grad.reshape(DEPTH, 2, 2, 2, 32, 4 * width), small
    )
    return (
        result.reshape(inputs.shape),
        grad_inputs[None],
        total[0],
        in_grad,
        total[1:4],
        out_grad,
        total[4],
        gate.astype(F32),
        up.astype(F32),
        down.T.astype(F32),
    )


def anywhere(
    inputs,
    lengths,
    norm_one_gain,
    w_in,
    conv_weight,
    w_out,
    norm_two_gain,
    w_gate,
    w_up,
    w_down,
    cotangent,
):
    both = ("seq", "batch")
    in_all = lax.all_gather(w_in, both, axis=0, tiled=True)
    out_all = lax.all_gather(w_out, both, axis=0, tiled=True)
    gate_use, up_use = (
        lax.all_gather(
            lax.all_gather(w, "seq", axis=0, tiled=True), "batch", axis=1, tiled=True
        )
        for w in (w_gate, w_up)
    )
    down_use = lax.all_gather(
        lax.all_gather(w_down, "seq", axis=1, tiled=True), "batch", axis=0, tiled=True
    )
    kept = mixer_forward(
        inputs, lengths, norm_one_gain, conv_weight, norm_two_gain, in_all, out_all
    )
    rows_norm = kept["normed_two"]
    grad_out = cotangent[0].astype(F32)
    rows_grad = (kept["valid_mask"] * grad_out).astype(BF16)
    gate_val = rounded_dot(rows_norm, gate_use)
    up_val = rounded_dot(rows_norm, up_use)
    hidden = (jax.nn.silu(gate_val) * up_val).astype(BF16)
    ffn_out = rounded_dot(hidden, down_use)
    result = (kept["middle"] + kept["valid_mask"] * ffn_out).astype(BF16)
    grad_down = over_rows(hidden, rows_grad)
    grad_hidden = by_rows(rows_grad, down_use)
    sigmoid_gate = jax.nn.sigmoid(gate_val)
    slope_gate = sigmoid_gate * (1.0 + gate_val * (1.0 - sigmoid_gate))
    grad_gate = (grad_hidden * up_val * slope_gate).astype(BF16)
    grad_up = (grad_hidden * gate_val * sigmoid_gate).astype(BF16)
    grad_gate_w = over_rows(rows_norm, grad_gate)
    grad_up_w = over_rows(rows_norm, grad_up)
    normed_part = by_rows(grad_gate, gate_use) + by_rows(grad_up, up_use)

    def owned(grad, axis):
        half = lax.psum_scatter(
            grad.astype(BF16), "batch", scatter_dimension=axis, tiled=True
        ).astype(F32)
        return lax.psum_scatter(half, "seq", scatter_dimension=1 - axis, tiled=True)

    shards = owned(grad_gate_w, 1), owned(grad_up_w, 1), owned(grad_down, 0)
    grad_inputs, grad_in_w, grad_out_w, gain_one, taps, gain_two = mixer_backward(
        kept, grad_out, normed_part, norm_one_gain, norm_two_gain, in_all, out_all
    )
    shard_in, shard_out = (
        lax.psum_scatter(grad, both, scatter_dimension=0, tiled=True)
        for grad in (grad_in_w, grad_out_w)
    )
    total_one, total_two, total_kernel = lax.psum((gain_one, gain_two, taps), both)
    return (
        result[None],
        grad_inputs[None],
        total_one,
        shard_in,
        total_kernel,
        shard_out,
        total_two,
    ) + shards


def solution(mesh):
    in_specs = (
        P("batch", "seq", None),
        P("batch"),
        P(),
        P(("seq", "batch"), None),
        P(),
        P(("seq", "batch"), None),
        P(),
        P("seq", "batch"),
        P("seq", "batch"),
        P("batch", "seq"),
        P("batch", "seq", None),
    )
    out_specs = (
        P("batch", "seq", None),
        P("batch", "seq", None),
        P(),
        P(("seq", "batch"), None),
        P(),
        P(("seq", "batch"), None),
        P(),
        P("seq", "batch"),
        P("seq", "batch"),
        P("batch", "seq"),
    )
    by_blocks = mesh.shape["seq"] == 4 * DEPTH and mesh.shape["batch"] == 2
    return jax.shard_map(
        in_blocks if by_blocks else anywhere,
        mesh=mesh,
        in_specs=in_specs,
        out_specs=out_specs,
        check_vma=False,
    )
```

```python
import functools

import jax
import jax.numpy as jnp
from jax import lax
from jax.experimental import pallas as pl
from jax.experimental.pallas import tpu as pltpu
from jax.sharding import PartitionSpec as P

epsilon = 1e-05
MESH = pl.DeviceIdType.MESH
F32, BF16 = jnp.float32, jnp.bfloat16
DEPTH = 4
PARTS = [384, 256, 256, 256]
KINDS = ("z", "y", "z", "z")
GRAD_KINDS = ("y", "z", "z", "z")
ORDER = (0, 1, 2, 3)
SPOTS = [0, 1152, 0, 768]
PAIRS = tuple(k for k, kind in enumerate(KINDS) if kind == "y")
PAIR_EARLY = 1
MIXER = (
    (2, ["x", "y", "c"]),
    (0, ["y", "x", "c"]),
    (1, ["y", "x", "c"]),
    (3, ["x", "y", "c"]),
)
MIXER_GRADS = (
    (0, ["c", "x", "y"], []),
    (2, ["c", "y", "x"], []),
    (3, ["c"], ["x", "y"]),
    (1, ["c", "y", "x"], []),
)
LAST_STEPS = (
    0, 1, 2, 3, 4, 5, 6, 7, 8, 9, 10, 11, 12, 13, 14, 15, 16, 17, 34, 51, 64, 81, 18,
    22, 26, 30, 35, 39, 43, 47, 52, 53, 54, 56, 58, 65, 19, 69, 73, 77, 82, 83, 36, 23,
    40, 27, 55, 44, 31, 84, 85, 37, 38, 48, 41, 66, 45, 20, 21, 57, 49, 42, 67, 68, 70,
    74, 71, 78, 59, 60, 24, 25, 46, 75, 28, 72, 79, 32, 86, 87, 29, 61, 62, 50, 76, 88,
    89, 33, 63, 80, 90, 91,
)
Z_GATE = 1
ACTS = 1920
EARLY = 1
STEPS = (
    0, 1, 2, 3, 4, 5, 6, 7, 8, 9, 10, 11, 12, 13, 14, 18, 20, 21, 22, 23, 24, 25, 26,
    27, 15, 16, 17, 19, 28, 29, 34, 52, 46, 47, 88, 70, 64, 65, 82, 83, 100, 101, 30,
    31, 38, 48, 49, 158, 42, 66, 67, 53, 84, 85, 35, 92, 56, 96, 60, 71, 74, 102, 78,
    32, 33, 89, 113, 50, 51, 36, 54, 68, 69, 72, 86, 87, 37, 57, 55, 90, 61, 39, 103,
    43, 73, 75, 91, 105, 106, 107, 141, 142, 143, 41, 93, 79, 45, 97, 58, 59, 40, 114,
    117, 121, 62, 63, 144, 44, 76, 77, 94, 95, 145, 80, 81, 98, 146, 147, 99, 148, 149,
    104, 108, 159, 150, 153, 151, 152, 109, 160, 115, 161, 118, 122, 129, 154, 155, 156,
    157, 166, 110, 164, 111, 116, 168, 162, 112, 125, 167, 119, 123, 133, 130, 134, 126,
    163, 165, 169, 170, 120, 124, 127, 131, 135, 137, 171, 172, 132, 136, 178, 179, 128,
    138, 180, 181, 182, 183, 184, 139, 193, 140, 194, 195, 196, 185, 186, 173, 198, 203,
    187, 197, 201, 189, 188, 199, 200, 202, 217, 191, 204, 205, 206, 207, 208, 218, 219,
    220, 221, 222, 231, 232, 234, 174, 209, 210, 190, 211, 233, 235, 213, 236, 237, 238,
    241, 239, 243, 215, 240, 175, 176, 242, 223, 224, 212, 244, 245, 225, 246, 192, 266,
    247, 248, 249, 256, 250, 267, 251, 227, 252, 226, 253, 254, 229, 261, 255, 257, 214,
    258, 228, 177, 263, 259, 260, 264, 216, 269, 262, 270, 265, 268, 271, 230, 272, 273,
    274, 275,
)


def over_rows(left, right):
    return lax.dot_general(
        left, right, (((0,), (0,)), ((), ())), preferred_element_type=F32
    )


def by_rows(left, right):
    return lax.dot_general(
        left, right, (((1,), (1,)), ((), ())), preferred_element_type=F32
    )


def dot(left, right):
    return jnp.dot(left, right, preferred_element_type=F32)


def rounded_dot(left, right):
    return dot(left, right).astype(BF16).astype(F32)


class Place:
    def __init__(self):
        self.s = lax.axis_index("seq")
        self.x = lax.axis_index("batch")
        self.z = self.s // 4
        self.y = (self.s // 2) % 2
        self.c = self.s % 2
        self.last = lax.axis_size("seq") - 1
        self.own = {"y": self.y, "c": self.c, "x": self.x}
        self.device = {
            "c": (self.s + 1 - 2 * self.c, self.x),
            "y": (self.s + 2 - 4 * self.y, self.x),
            "x": (self.s, 1 - self.x),
            "up": (self.s + 4, self.x),
            "down": (self.s - 4, self.x),
            "next": (self.s + 1, self.x),
            "prev": (self.s - 1, self.x),
            "pair": (self.s + 4 - 8 * (self.z % 2), self.x),
            "far": (self.s + 8 - 16 * (self.z // 2), self.x),
        }

    def greet(self, names):
        barrier = pltpu.get_barrier_semaphore()
        ends = {
            "up": self.z < DEPTH - 1,
            "down": self.z > 0,
            "next": self.s < self.last,
            "prev": self.s > 0,
        }

        def signal(name):
            pl.semaphore_signal(
                barrier, inc=1, device_id=self.device[name], device_id_type=MESH
            )

        expected = 0
        for name in names:
            if name in ends:
                pl.when(ends[name])(functools.partial(signal, name))
                expected = expected + ends[name].astype(jnp.int32)
            else:
                signal(name)
                expected = expected + 1
        pl.semaphore_wait(barrier, expected)


class Links:
    def __init__(self, place, send, recv):
        self.place, self.send, self.recv = place, send, recv
        self.used = 0

    def take(self, count):
        first = self.used
        self.used += count
        assert self.used <= self.send.shape[0]
        return first

    def copy(self, source, target, index, name):
        return pltpu.make_async_remote_copy(
            src_ref=source,
            dst_ref=target,
            send_sem=self.send.at[index],
            recv_sem=self.recv.at[index],
            device_id=self.place.device[name],
            device_id_type=MESH,
        )


def way(direction):
    return (1 - direction) // 2


class Line:
    def take_line(self):
        self.first = self.links.take(2 * DEPTH)

    def hop(self, source, target, direction, level):
        place = self.place
        index = self.first + DEPTH * way(direction) + level
        return pltpu.make_async_remote_copy(
            src_ref=source,
            dst_ref=target,
            send_sem=self.links.send.at[index],
            recv_sem=self.links.recv.at[index],
            device_id=(place.s + 4 * direction, place.x),
            device_id_type=MESH,
        )

    def levels(self, distance, action):
        z = self.place.z
        if distance == 0:
            action(z, None)
            return

        def side(i, carry):
            direction = 1 - 2 * i
            level = z - direction * distance

            @pl.when((level >= 0) & (level < DEPTH))
            def _():
                action(level, direction)

            return carry

        lax.fori_loop(0, 2, side, 0)

    def beyond(self, direction):
        further = self.place.z + direction
        return (further >= 0) & (further < DEPTH)


class Gather(Line):
    def __init__(self, links, view, stages):
        self.links, self.view, self.stages = links, view, stages
        self.place = links.place
        self.take_line()
        self.rows = {name: links.take(DEPTH) for name in stages}

    def block(self, stage, level, theirs=False):
        where = dict(self.place.own)
        if stage is not None:
            for name in self.stages[:stage]:
                where[name] = slice(None)
            if theirs:
                where[self.stages[stage]] = 1 - where[self.stages[stage]]
        return self.view(level, where["y"], where["c"], where["x"])

    def line(self, direction, level):
        ref = self.block(None, level)
        return self.hop(ref, ref, direction, level)

    def staged(self, stage, level, theirs=False):
        name = self.stages[stage]
        ref = self.block(stage, level, theirs)
        return self.links.copy(ref, ref, self.rows[name] + level, name)

    def along(self, distance):
        def hand_on(level, direction):
            if distance:
                self.line(direction, level).wait_recv()

            @pl.when(self.beyond(direction))
            def _():
                self.line(direction, level).start()

        if distance == 0:
            hand_on(self.place.z, 1)
            hand_on(self.place.z, -1)
        else:
            self.levels(distance, hand_on)

    def depart(self, distance):
        self.levels(distance, lambda level, _: self.staged(0, level).start())

    def across(self, stage, distance):
        def pass_on(level, _):
            self.staged(stage, level, True).wait_recv()
            if stage + 1 < len(self.stages):
                self.staged(stage + 1, level).start()

        self.levels(distance, pass_on)

    def drain_line(self):
        z = self.place.z

        def sent(level, carry):
            @pl.when((z >= level) & (z < DEPTH - 1))
            def _():
                self.line(1, level).wait_send()

            @pl.when((z <= level) & (z > 0))
            def _():
                self.line(-1, level).wait_send()

            return carry

        lax.fori_loop(0, DEPTH, sent, 0)

    def drain(self):
        self.drain_line()

        def sent(level, carry):
            for stage in range(len(self.stages)):
                self.staged(stage, level).wait_send()
            return carry

        lax.fori_loop(0, DEPTH, sent, 0)


class PairGather(Gather):
    def __init__(self, links, ref):
        super().__init__(links, lambda z, y, c, x: ref.at[z, y], ["y"])
        self.ref = ref

    def line(self, direction, level):
        ref = self.ref.at[level]
        return self.hop(ref, ref, direction, level)

    def begin(self):
        self.staged(0, self.place.z).start()

    def join(self):
        self.staged(0, self.place.z, True).wait_recv()
        self.along(0)

    def drain(self):
        self.staged(0, self.place.z).wait_send()
        self.drain_line()


def add_into(target, source):
    def add(i, carry):
        target[i] = (target[i].astype(F32) + source[i].astype(F32)).astype(BF16)
        return carry

    if len(target.shape) > 2:
        lax.fori_loop(0, target.shape[0], add, 0)
    else:
        add(Ellipsis, 0)


class Reduce(Line):
    def __init__(self, links, view, stages, slots, line_slots, after=(), source=None):
        self.links, self.view, self.stages = links, view, list(stages) + list(after)
        self.slots, self.line_slots = slots, line_slots
        self.source = source or view
        self.before = len(stages)
        self.place = links.place
        self.take_line()
        self.rows = {name: links.take(DEPTH) for name in stages}
        self.rows.update({name: links.take(1) for name in after})

    def block(self, stage, level, theirs=False):
        where = dict(self.place.own)
        for name in self.stages[stage + 1 :]:
            where[name] = slice(None)
        if theirs:
            where[self.stages[stage]] = 1 - where[self.stages[stage]]
        view = self.source if theirs and stage == 0 else self.view
        return view(level, where["y"], where["c"], where["x"])

    def staged(self, stage, level):
        name = self.stages[stage]
        late = stage >= self.before
        return self.links.copy(
            self.block(stage, level, True),
            self.slots[stage] if late else self.slots[stage].at[level],
            self.rows[name] + (0 if late else level),
            name,
        )

    def late_start(self, stage):
        self.staged(stage, self.place.z).start()

    def late_take(self, stage):
        z = self.place.z
        self.staged(stage, z).wait_recv()
        add_into(self.block(stage, z), self.slots[stage])

    def slot(self, direction, level):
        return self.line_slots.at[level + 1 - way(direction)]

    def line(self, direction, level):
        ref = self.block(self.before - 1, level)
        return self.hop(ref, self.slot(direction, level), direction, level)

    def begin(self, distance):
        self.levels(distance, lambda level, _: self.staged(0, level).start())

    def across(self, stage, distance):
        def take(level, _):
            self.staged(stage, level).wait_recv()
            add_into(self.block(stage, level), self.slots[stage].at[level])
            if stage + 1 < self.before:
                self.staged(stage + 1, level).start()

        self.levels(distance, take)

    def take(self, direction, level):
        self.line(direction, level).wait_recv()
        add_into(self.block(self.before - 1, level), self.slot(direction, level))

    def along(self, distance):
        if distance == 0:

            def side(i, carry):
                direction = 1 - 2 * i

                @pl.when(self.beyond(-direction))
                def _():
                    self.take(direction, self.place.z)

                return carry

            lax.fori_loop(0, 2, side, 0)
            return

        def send(level, back):
            @pl.when(self.beyond(back))
            def _():
                self.take(-back, level)

            self.line(-back, level).start()

        self.levels(distance, send)

    def drain_line(self):
        z = self.place.z

        def sent(level, carry):
            @pl.when(z > level)
            def _():
                self.line(-1, level).wait_send()

            @pl.when(z < level)
            def _():
                self.line(1, level).wait_send()

            return carry

        lax.fori_loop(0, DEPTH, sent, 0)

    def drain(self):
        self.drain_line()

        def sent(level, carry):
            for stage in range(self.before):
                self.staged(stage, level).wait_send()
            return carry

        lax.fori_loop(0, DEPTH, sent, 0)
        for stage in range(self.before, len(self.stages)):
            self.staged(stage, self.place.z).wait_send()


class PairReduce(Reduce):
    def __init__(self, links, ref, slot, line_slots):
        super().__init__(links, lambda z, y, c, x: ref.at[z, y], ["y"], None, line_slots)
        self.ref, self.last_slot = ref, slot

    def block(self, stage, level, theirs=False):
        return self.ref.at[level]

    def final(self):
        place = self.place
        return self.links.copy(
            self.ref.at[place.z, 1 - place.y], self.last_slot, self.rows["y"], "y"
        )

    def finish(self):
        self.final().wait_recv()
        add_into(self.ref.at[self.place.z, self.place.y], self.last_slot)

    def drain(self):
        self.drain_line()
        self.final().wait_send()


class Plan:
    def __init__(self):
        self.steps = []

    def add(self, needs, action, *args, busy=False):
        self.steps.append((tuple(needs), functools.partial(action, *args), busy))
        return len(self.steps) - 1

    def run(self, order):
        seen = set()
        assert sorted(order) == list(range(len(self.steps)))
        for index in order:
            needs, action, _ = self.steps[index]
            assert seen.issuperset(needs)
            action()
            seen.add(index)


def mean_of(values):
    return jnp.mean(values, axis=1, keepdims=True)


def layer_kernel(
    length_ref,
    x_ref,
    grad_ref,
    grad_rows_ref,
    vectors_ref,
    in_ref,
    out_ref,
    gate_ref,
    up_ref,
    down_ref,
    mixer_hbm,
    parts_hbm,
    middle_hbm,
    mixer_grad,
    small,
    result_ref,
    input_grad,
    gate_grad,
    up_grad,
    down_grad,
    wm,
    w0,
    w1,
    w2,
    w3,
    product,
    middle,
    tokens,
    grads,
    r0,
    r1,
    r2,
    r3,
    l0,
    l1,
    l2,
    l3,
    e0,
    e1,
    e2,
    e3,
    acts,
    out_sum,
    back_sum,
    keep_sem,
    send,
    recv,
):
    place = Place()
    links = Links(place, send, recv)
    plan = Plan()
    rows, depth = parts_hbm.shape[0] // 3, parts_hbm.shape[1]
    tile = rows // 2
    weights, edges = (w0, w1, w2, w3), (e0, e1, e2, e3)
    quarter = sum(PARTS)
    offsets = [sum(PARTS[:k]) for k in range(len(PARTS))]

    def columns(first, count):
        return lambda z, y, c, x: wm.at[z, y, c, x, :, pl.ds(first, count)]

    mixers = [
        Gather(links, columns(depth * j, depth), stages)
        for j, stages in MIXER
    ]
    gathers, reduces = [], []
    for number, (w, r, l) in enumerate(zip(weights, (r0, r1, r2, r3), (l0, l1, l2, l3))):
        view = lambda z, y, c, x, w=w: w.at[z, y]
        if KINDS[number] == "y":
            gathers.append(PairGather(links, w))
        else:
            gathers.append(Gather(links, view, ["y"]))
        if GRAD_KINDS[number] == "y":
            reduces.append(PairReduce(links, w, r, l))
        else:
            reduces.append(Reduce(links, view, ["y"], [r], l))

    def sides(number, quarter_index):
        width = PARTS[number]
        start = pl.multiple_of(quarter_index * quarter + offsets[number], 128)
        return [
            (ref.at[:, pl.ds(start, width)], pl.ds(side * width, width))
            for side, ref in enumerate((gate_ref, up_ref, down_ref))
        ]

    twins = [
        [
            links.copy(
                source,
                weights[number].at[place.z, place.y, place.c, :, where],
                links.take(1),
                "c",
            )
            for source, where in sides(number, 1 - place.c)
        ]
        for number in range(len(PARTS))
    ]


    def share(ref):
        first = links.take(3)
        return (
            links.copy(ref[0], ref[1], first, "c"),
            links.copy(ref[0], ref[2], first + 1, "x"),
            links.copy(ref[2], ref[3], first + 2, "c"),
        )

    shared_grads = [
        share([grads.at[i // 2, 2 * (i % 2) + h, q] for i in range(4)])
        for h in range(2)
        for q in range(2)
    ]
    shared_tokens = [
        share([tokens.at[i // 2, 2 * (i % 2) + h] for i in range(4)]) for h in range(2)
    ]
    edge = links.copy(
        product.at[pl.ds(rows, 8)], product.at[pl.ds(0, 8)], links.take(1), "next"
    )
    back_edge = links.copy(
        middle.at[pl.ds(0, 8)], middle.at[pl.ds(rows, 8)], links.take(1), "prev"
    )
    has_next, has_prev = place.s < place.last, place.s > 0
    slots = [
        wm.at[pl.ds(2 * (i // 4), 2), :, :, :, :, pl.ds(depth * (i % 4), depth)]
        for i in range(6)
    ]

    def give_back(total, slots):
        first = links.take(3)
        return (
            links.copy(total.at[3], slots[2], first, "c"),
            links.copy(total.at[2], slots[1], first + 1, "x"),
            links.copy(total.at[1], slots[0], first + 2, "c"),
        )

    returned = [give_back(back_sum, slots[:3]), give_back(out_sum, slots[3:])]
    trades = [
        links.copy(w.at[place.z, place.y, 1 - place.c], e, links.take(1), "c")
        for w, e in zip(weights, edges)
    ]

    count = iter(range(keep_sem.shape[0]))

    def local(source, target):
        return pltpu.make_async_copy(source, target, keep_sem.at[next(count)])

    parts = acts.at[pl.ds(0, 3 * rows), pl.ds(0, depth)]
    save_mixer = local(wm, mixer_hbm)
    save_parts = local(parts, parts_hbm)
    save_middle = local(middle.at[pl.ds(0, rows)], middle_hbm)
    fills = [
        [
            local(source, weights[number].at[place.z, place.y, place.c, :, where])
            for source, where in sides(number, place.c)
        ]
        for number in range(len(PARTS))
    ]
    mine = wm.at[place.z, place.y, place.c, place.x]
    fill_in = local(in_ref, mine.at[:, pl.ds(0, 3 * depth)])
    fill_out = local(out_ref, mine.at[:, pl.ds(3 * depth, depth)])
    inner = pl.ds(0, rows)
    low_x, high_x = out_sum.at[1], back_sum.at[0]
    view = (2,) + tokens.shape[2:]
    load_x = [local(x_ref, x) for x in (low_x, high_x)]
    load_grad = local(grad_ref, grads.at[0, pl.ds(0, 2)])
    load_grad_rows = local(grad_rows_ref, acts.at[pl.ds(3 * rows, rows), pl.ds(0, depth)])
    save_result = local(back_sum.at[1], result_ref)
    blocks = [tokens.at[0], tokens.at[1], grads.at[0], grads.at[1]]
    load_mixer = [
        local(mixer_hbm.at[:, :, :, :, :, pl.ds(depth * j, depth)], block)
        for j, block in enumerate(blocks)
    ]
    load_parts = local(parts_hbm, parts)
    load_middle = local(middle_hbm, product.at[pl.ds(8, rows)])
    staging = [acts.at[pl.ds(2 * rows * i, 2 * rows), pl.ds(depth, 2 * tile)] for i in range(2)]
    stores = [
        local(staging[j % 2], mixer_grad.at[:, pl.ds(2 * tile * ((j + 6) % 8), 2 * tile)])
        for j in range(8)
    ]
    save_grad, save_inputs = (
        local(middle.at[pl.ds(0, rows)], input_grad) for _ in range(2)
    )
    load_back = local(input_grad, middle.at[pl.ds(0, rows)])

    def hear(*copies):
        for copy in copies:
            copy.wait_recv()

    def begin(*copies):
        for copy in copies:
            copy.start()

    def done(*copies):
        for copy in copies:
            copy.wait()

    def valid_rows(first, count):
        position = place.s * rows + first + lax.broadcasted_iota(
            jnp.int32, (count, 1), 0
        )
        return (position < length_ref[0]).astype(F32)

    def open_all():
        for copy in [fill_in, fill_out, load_x[0], load_grad] + sum(fills, []):
            copy.start()
        place.greet(["c", "y", "x", "up", "down", "next", "prev"])
        fill_in.wait()
        fill_out.wait()

    def clear():
        @pl.when(place.s == 0)
        def _():
            product[pl.ds(0, 8)] = jnp.zeros((8, depth), F32)

        @pl.when(place.s == place.last)
        def _():
            middle[pl.ds(rows, 8)] = jnp.zeros((8, depth), F32)

    def first_norm(source, target):
        x = source[...].reshape(rows, depth).astype(F32)
        scale = lax.rsqrt(mean_of(x * x) + epsilon)
        normed = (x * scale * vectors_ref[0:1]).astype(BF16)
        target[...] = normed.reshape(view)

    def mask_grads():
        masked = grads[0, pl.ds(0, 2)].reshape(rows, depth).astype(F32)
        masked *= valid_rows(0, rows)
        grads[0, pl.ds(0, 2)] = masked.astype(BF16).reshape(view)

    def project(index):
        weight = wm[..., depth * index : depth * (index + 1)].reshape(depth, depth)
        acts[rows * index : rows * (index + 1), :depth] = dot(
            out_sum[0].reshape(rows, depth), weight
        ).astype(BF16)

    def multiply():
        b_part = acts[:rows, :depth].astype(F32)
        v_part = acts[2 * rows : 3 * rows, :depth].astype(F32)
        product[pl.ds(8, rows)] = (b_part * v_part).astype(BF16).astype(F32)

    def conv_rows(start):
        total = 0.0
        for tap in range(3):
            first = start + 6 + tap
            total += vectors_ref[1 + tap : 2 + tap] * product[first : first + tile]
        return total

    def mix(index):
        start = tile * index
        where = slice(start, start + tile)
        c_part = acts[rows + start : rows + start + tile, :depth].astype(F32)
        gated = (c_part * conv_rows(start)).astype(BF16)
        weight = wm[..., 3 * depth :].reshape(depth, depth)
        x = low_x[index].reshape(tile, depth).astype(F32)
        total = x + valid_rows(start, tile) * dot(gated, weight)
        middle[where] = total
        scale = lax.rsqrt(mean_of(total * total) + epsilon)
        new = (total * scale * vectors_ref[4:5]).astype(BF16)
        tokens[0, index] = new.reshape(tokens.shape[2:])

    begun = set()

    def one_block(number, pair, i, carry):
        weight, width, spot = weights[number], PARTS[number], SPOTS[number]
        where = pl.ds(pl.multiple_of(rows * (2 * pair + i), rows), rows)
        gate_up = weight[..., : 2 * width].reshape(depth, 2 * width)
        both = dot(tokens[pair, pl.ds(2 * i, 2)].reshape(rows, depth), gate_up)
        gate, up = both[:, :width], both[:, width:]
        sigmoid = jax.nn.sigmoid(gate)
        silu = gate * sigmoid
        slope = sigmoid + silu * (1.0 - sigmoid)
        kept = (silu * up).astype(BF16)
        down = weight[..., 2 * width :].reshape(depth, width)
        grad_hidden = dot(grads[pair, pl.ds(2 * i, 2)].reshape(rows, depth), down)
        acts[where, spot : spot + width] = (grad_hidden * up * slope).astype(BF16)
        acts[where, spot + width : spot + 2 * width] = (grad_hidden * silu).astype(BF16)
        acts[where, spot + 2 * width : spot + 3 * width] = kept
        out_part = by_rows(kept, down)
        back_part = by_rows(acts[where, spot : spot + 2 * width], gate_up)
        shape = out_sum.shape[1:]
        index = 2 * pair + i
        if pair in begun:
            out_part += out_sum[index].reshape(rows, depth).astype(F32)
            back_part += back_sum[index].reshape(rows, depth).astype(F32)
        out_sum[index] = out_part.astype(BF16).reshape(shape)
        back_sum[index] = back_part.astype(BF16).reshape(shape)
        return carry

    def block(number, pair):
        lax.fori_loop(0, 2, functools.partial(one_block, number, pair), 0)
        begun.add(pair)

    def weigh(number):
        weight, width, spot = weights[number], PARTS[number], SPOTS[number]
        for source, first, size in ((tokens, 0, 2 * width), (grads, 2 * width, width)):
            step = size if size <= 512 else size // 2

            def column(i, carry):
                factor = acts[:, pl.ds(pl.multiple_of(spot + first + i * step, 128), step)]
                part = over_rows(source[...].reshape(4 * rows, depth), factor)
                where = pl.ds(pl.multiple_of(first + i * step, 128), step)
                weight[..., where] = part.astype(BF16).reshape(
                    weight.shape[:-1] + (step,)
                )
                return carry

            lax.fori_loop(0, size // step, column, 0)

    def lift(index):
        hear(returned[index][0])
        add_into((back_sum, out_sum)[index].at[2], slots[3 * index + 2])
        begin(returned[index][1])

    def returned_rows(index, start):
        total = (back_sum, out_sum)[index]
        i = start // tile
        found = total[0, i].reshape(tile, depth).astype(F32)
        for slot in slots[3 * index : 3 * index + 2]:
            found += slot[i].reshape(tile, depth).astype(F32)
        return found

    def note(row, values):
        total = jnp.sum(values, axis=0, keepdims=True)
        if ("row", row) in begun:
            total += small[row : row + 1]
        small[row : row + 1] = total
        begun.add(("row", row))

    def turn(index):
        start = tile * index
        where = slice(start, start + tile)
        part = returned_rows(0, start)
        total = middle[where]
        scale = lax.rsqrt(mean_of(total * total) + epsilon)
        hat = total * scale
        note(4, part * hat)
        scaled = part * vectors_ref[4:5]
        spot = slice(3 * rows + start, 3 * rows + start + tile)
        grad = acts[spot, :depth].astype(F32) + scale * (
            scaled - hat * mean_of(scaled * hat)
        )
        middle[where] = grad
        acts[spot, :depth] = (valid_rows(start, tile) * grad).astype(BF16)

    def unmix(index):
        start = tile * index
        spot = slice(rows + start, rows + start + tile)
        weight = grads[1].reshape(depth, depth)
        gated_grad = by_rows(
            acts[3 * rows + start : 3 * rows + start + tile, :depth], weight
        )
        c_part = acts[spot, :depth].astype(F32)
        conv = conv_rows(start)
        back_sum[3, index] = (c_part * conv).astype(BF16).reshape(tokens.shape[2:])
        acts[spot, :depth] = (gated_grad * conv).astype(BF16)
        conv_grad = gated_grad * c_part
        middle[start : start + tile] = conv_grad
        for tap in range(3):
            first = start + 6 + tap
            note(1 + tap, conv_grad * product[first : first + tile])

    def unconv(index):
        start = tile * index
        grad = 0.0
        for tap in range(3):
            first = start + 2 - tap
            grad += vectors_ref[1 + tap : 2 + tap] * middle[first : first + tile]
        b_spot = slice(start, start + tile)
        v_spot = slice(2 * rows + start, 2 * rows + start + tile)
        b_part = acts[b_spot, :depth].astype(F32)
        v_part = acts[v_spot, :depth].astype(F32)
        acts[b_spot, :depth] = (grad * v_part).astype(BF16)
        acts[v_spot, :depth] = (grad * b_part).astype(BF16)

    def project_back(index):
        start = tile * index
        where = slice(start, start + tile)
        part = 0.0
        for j in range(3):
            spot = slice(rows * j + start, rows * j + start + tile)
            part += by_rows(acts[spot, :depth], blocks[j][...].reshape(depth, depth))
        x = high_x[index].reshape(tile, depth).astype(F32)
        scale = lax.rsqrt(mean_of(x * x) + epsilon)
        hat = x * scale
        note(0, part * hat)
        scaled = part * vectors_ref[0:1]
        middle[where] = middle[where] + scale * (scaled - hat * mean_of(scaled * hat))

    def weigh_mixer(j):
        if j >= 2:
            stores[j - 2].wait()
        wide = 2 * tile
        if j >= 2:
            first = rows * (j // 2 - 1)
            left = back_sum[2].reshape(rows, depth)
        else:
            first = 3 * rows
            left = back_sum[3].reshape(rows, depth)
        start = wide * (j % 2)
        part = over_rows(left, acts[first : first + rows, start : start + wide])
        staging[j % 2][...] = part.astype(BF16)
        stores[j].start()

    def close_result():
        for index in range(2):
            start = tile * index
            total = product[8 + start : 8 + start + tile] + valid_rows(
                start, tile
            ) * returned_rows(1, start)
            back_sum[1, index] = total.astype(BF16).reshape(tokens.shape[2:])
        save_result.start()

    def own(number):
        width = PARTS[number]
        for side, target in enumerate((gate_grad, up_grad, down_grad)):
            spot = pl.ds(side * width, width)
            mine = pl.multiple_of(place.c * quarter + offsets[number], 128)
            twin = pl.multiple_of((1 - place.c) * quarter + offsets[number], 128)
            target[:, pl.ds(mine, width)] = weights[number][
                place.z, place.y, place.c, :, spot
            ]
            target[:, pl.ds(twin, width)] = edges[number][:, spot]

    def work_on(needs, action, *args):
        return plan.add(needs, action, *args, busy=True)

    start = plan.add([], open_all)
    for part in mixers:
        plan.add([start], part.along, 0)
        plan.add([start], part.depart, 0)
    for twin in twins:
        plan.add([start], begin, *twin)
    plan.add([start], clear)
    masked = plan.add([start], load_grad.wait)
    masked = work_on([masked], mask_grads)
    plan.add([masked], begin, *[group[0] for group in shared_grads])
    early = [plan.add([masked], begin, group[1]) for group in shared_grads[:EARLY]]
    norm = plan.add([start], load_x[0].wait)
    norm = work_on([norm], first_norm, low_x, out_sum.at[0])
    filled = [plan.add([start], done, *copies) for copies in fills]
    arrived = [
        plan.add([filled[number]], hear, *twins[number]) for number in range(len(PARTS))
    ]

    gone, whole, passed = [], {}, []
    for number, part in enumerate(mixers):
        last = {(0, 0): start}
        for distance in range(1, DEPTH):
            step = plan.add([start], part.along, distance)
            last[0, distance] = plan.add([step], part.depart, distance)
            passed += [step] * (distance == Z_GATE)
        for stage in range(3):
            for distance in range(DEPTH):
                last[stage + 1, distance] = plan.add(
                    [last[stage, distance]], part.across, stage, distance
                )
        gone += [last[stage, d] for stage in (0, 1) for d in range(DEPTH)]
        whole[MIXER[number][0]] = list(last.values())

    ready = {}
    z_gate, y_gate = [start] + passed, list(gone)
    pair_opening = passed if PAIR_EARLY else gone
    pair_gate = {}
    for number in PAIRS:
        pair_gate[number] = [plan.add([arrived[number]] + pair_opening, gathers[number].begin)]
    for number in ORDER:
        part = gathers[number]
        opening = part.join if KINDS[number] == "y" else functools.partial(part.along, 0)
        found = [plan.add([arrived[number]] + z_gate + pair_gate.get(number, []), opening)]
        for distance in range(1, DEPTH):
            found.append(plan.add(found[-1:], part.along, distance))
        z_gate = found[1:2]
        if KINDS[number] == "z":
            sends = [
                plan.add([found[distance]] + y_gate, part.depart, distance)
                for distance in range(DEPTH)
            ]
            y_gate = sends[2:3]
            last_sends = sends
            found += sends
            found += [
                plan.add([sends[distance]], part.across, 0, distance)
                for distance in range(DEPTH)
            ]
        ready[number] = found

    y_gate = last_sends

    x_free = early + [
        plan.add(gone, begin, group[1]) for group in shared_grads[EARLY:]
    ]
    b_step = work_on(whole[0] + [norm], project, 0)
    v_step = work_on(whole[2] + [norm], project, 2)
    times = work_on([b_step, v_step], multiply)

    def send_edge():
        pl.when(has_next)(edge.start)

    def take_edge():
        pl.when(has_prev)(edge.wait_recv)

    def edge_sent():
        pl.when(has_next)(edge.wait_send)

    sent = plan.add([times], send_edge)
    c_step = work_on(whole[1] + [times], project, 1)
    saving = plan.add([c_step], begin, save_parts)
    late_mix = work_on(whole[3] + [c_step, sent], mix, 1)
    drained = plan.add([late_mix], lambda: [part.drain() for part in mixers])
    saved = plan.add([drained], begin, save_mixer)
    token_sends = {}
    token_sends[1] = plan.add([late_mix] + x_free, begin, *shared_tokens[1][1::-1])
    edge_in = plan.add([sent], take_edge)
    mixed = work_on([edge_in, late_mix], mix, 0)
    kept = plan.add([mixed, saved], lambda: (save_middle.start(), save_mixer.wait()))
    token_sends[0] = plan.add([kept, token_sends[1]], begin, *shared_tokens[0][1::-1])

    grads_x, tokens_x = [], []

    def pass_grads(group):
        hear(group[1])
        begin(group[2])

    for step, group in zip(x_free, shared_grads):
        grads_x.append(plan.add([step], pass_grads, group))
    for h in (1, 0):
        group = shared_tokens[h]

        def pass_on(group=group):
            hear(group[1])
            begin(group[2])

        tokens_x.append(plan.add([token_sends[h]], pass_on))
    near = plan.add(
        [token_sends[0], masked],
        hear,
        *[group[0] for group in shared_grads + shared_tokens],
    )
    far = plan.add(
        tokens_x + grads_x, hear, *[group[2] for group in shared_grads + shared_tokens]
    )
    def flush():
        done(save_parts, save_middle)
        edge_sent()

    flushed = plan.add([kept, mixed], flush)
    own_side, other_side = [near, flushed], [near, far, flushed]
    blocks_done = {}
    weighed = {}
    reduced = {}
    previous = []

    def reduce_steps(number, needs):
        part = reduces[number]
        if GRAD_KINDS[number] == "y":
            chain = list(needs)
            steps = []
            for distance in (3, 2, 1, 0):
                chain = [plan.add(chain, part.along, distance)]
                steps += chain
            chain = [plan.add(chain, lambda: part.final().start())]
            steps.append(plan.add(chain, part.finish))
            return steps
        steps = []
        opened = {
            distance: plan.add(needs + y_gate, part.begin, distance)
            for distance in (3, 2, 1, 0)
        }
        chain = []
        for distance in (3, 2, 1, 0):
            step = plan.add([opened[distance]], part.across, 0, distance)
            chain = [plan.add([step] + chain, part.along, distance)]
            steps += [step] + chain
        return steps

    def drain_and_weigh(number, needs):
        drain = plan.add(needs, gathers[number].drain)
        weighed[number] = work_on([drain], weigh, number)
        reduced[number] = reduce_steps(number, [weighed[number]])

    def columns_of(number):
        return set(range(SPOTS[number], SPOTS[number] + 3 * PARTS[number], 128))

    def run_block(number, pair):
        needs = [
            weighed[other]
            for other in ORDER[: ORDER.index(number)]
            if columns_of(other) & columns_of(number)
        ]
        blocks_done[number, pair] = work_on(
            ready[number] + (other_side if pair else own_side) + needs, block, number, pair
        )

    def finish_part(number):
        drain_and_weigh(number, [blocks_done[number, 0], blocks_done[number, 1]])

    first, second, third, fourth = ORDER
    for number in (first, second):
        if not columns_of(first) & columns_of(second):
            run_block(number, 0)
    for number in (first, second):
        if columns_of(first) & columns_of(second):
            run_block(number, 0)
        run_block(number, 1)
        finish_part(number)
    run_block(third, 1)
    run_block(fourth, 1)
    last_far = [blocks_done[third, 1], blocks_done[fourth, 1]]
    back_up = plan.add(last_far, begin, returned[0][0])
    out_up = plan.add([back_up], begin, returned[1][0])
    back_over = plan.add([back_up], lift, 0)
    run_block(third, 0)
    run_block(fourth, 0)
    near_done = [blocks_done[third, 0], blocks_done[fourth, 0]]
    back_near = plan.add(near_done + [back_over], begin, returned[0][2])
    out_over = plan.add([out_up, back_over], lift, 1)
    out_near = plan.add([back_near, out_over], begin, returned[1][2])
    finish_part(third)
    finish_part(fourth)

    def sent_tokens():
        for group in shared_grads + shared_tokens:
            for copy in group:
                copy.wait_send()

    freed = plan.add([weighed[number] for number in ORDER], sent_tokens)
    loads = plan.add(
        [freed], begin, load_parts, load_grad_rows, *load_mixer
    )
    back_in = plan.add([back_near], hear, returned[0][1], returned[0][2])
    loaded = plan.add([loads], done, load_parts, load_grad_rows, *load_mixer)
    turned = [work_on([back_in, loaded], turn, index) for index in range(2)]

    def free_sums():
        done(save_grad)
        for copy in returned[0]:
            copy.wait_send()
        load_x[1].start()

    freed = plan.add(turned, save_grad.start)
    freed = plan.add([freed], free_sums)
    unmixed = [work_on([freed], unmix, index) for index in range(2)]
    again = plan.add([freed], load_x[1].wait)
    again = work_on([again], first_norm, high_x, back_sum.at[2])

    def send_back():
        pl.when(has_prev)(back_edge.start)

    def take_back():
        pl.when(has_next)(back_edge.wait_recv)

    def back_sent():
        pl.when(has_prev)(back_edge.wait_send)

    back_edge_sent = plan.add([unmixed[0]], send_back)
    weigh_steps = [work_on(unmixed, weigh_mixer, j) for j in (0, 1)]
    low = work_on([unmixed[1], back_edge_sent], unconv, 0)
    taken = plan.add([back_edge_sent], take_back)
    high = work_on([taken, low], unconv, 1)
    fetched = plan.add([low, high] + [edge_in], begin, load_middle)
    for j in range(2, 8):
        weigh_steps.append(work_on([again, low, high, weigh_steps[-1]], weigh_mixer, j))
    revived = plan.add([low, high], lambda: (back_sent(), load_back.start()))
    revived = plan.add([revived, weigh_steps[-1]], load_back.wait)
    projected = [work_on([revived], project_back, index) for index in range(2)]
    stored = plan.add(projected, begin, save_inputs)
    def finish_result():
        load_middle.wait()
        close_result()

    out_in = plan.add([out_near, fetched], hear, returned[1][1], returned[1][2])
    finished = work_on([out_in, fetched] + weigh_steps, finish_result)

    finals = []
    for number in ORDER:
        trade = plan.add(reduced[number], begin, trades[number])
        heard = plan.add([trade], hear, trades[number])
        finals.append(work_on([heard], own, number))

    def close():
        small[pl.ds(5, 3)] = jnp.zeros((3, depth), F32)
        done(save_inputs, save_result, *stores[6:8])
        for reduce in reduces:
            reduce.drain()
        for group in returned[1:] + twins + [trades]:
            for copy in group:
                copy.wait_send()

    plan.add(finals + weigh_steps + projected + [stored, finished], close)
    plan.run(STEPS or list(range(len(plan.steps))))


def layer(lengths, inputs, cotangent, vectors, shards):
    rows, depth = inputs.shape
    ffn_columns = shards[2].shape[1]
    vmem = pl.BlockSpec(memory_space=pltpu.VMEM)
    hbm = pl.BlockSpec(memory_space=pl.ANY)
    shape = jax.ShapeDtypeStruct
    blocks = (DEPTH, 2, 2, 2, depth // (8 * DEPTH))
    half = (2, 2, 2, 2, rows // 16, depth)
    out_shape = [
        shape(blocks + (4 * depth,), BF16),
        shape((3 * rows, depth), BF16),
        shape((rows, depth), F32),
        shape((depth, 4 * depth), BF16),
        shape((8, depth), F32),
        shape(half, BF16),
        shape((rows, depth), F32),
    ] + [shape((64, ffn_columns), BF16)] * 3
    pair = (2, 64)
    widths = [3 * w for w in PARTS]

    def slots(lead, width, kind):
        if kind == "y":
            return (lead, 2) if lead > DEPTH else ()
        return (lead,)

    token = (2, 4, 2, 2, 2, 32, depth)
    total = (4, 2, 2, 2, 2, 32, depth)
    scratch = (
        [pltpu.VMEM(blocks + (4 * depth,), BF16)]
        + [pltpu.VMEM((DEPTH, 2) + pair + (w,), BF16) for w in widths]
        + [
            pltpu.VMEM((rows + 8, depth), F32),
            pltpu.VMEM((rows + 8, depth), F32),
        ]
        + [pltpu.VMEM(token, BF16)] * 2
        + [
            pltpu.VMEM(slots(lead, w, kind) + pair + (w,), BF16)
            for lead in (DEPTH, DEPTH + 1)
            for w, kind in zip(widths, GRAD_KINDS)
        ]
        + [pltpu.VMEM((64, w), BF16) for w in widths]
        + [pltpu.VMEM((4 * rows, ACTS), BF16)]
        + [pltpu.VMEM(total, BF16)] * 2
        + [
            pltpu.SemaphoreType.DMA((40,)),
            pltpu.SemaphoreType.DMA((240,)),
            pltpu.SemaphoreType.DMA((240,)),
        ]
    )
    smem = pl.BlockSpec(memory_space=pltpu.SMEM)
    return pl.pallas_call(
        layer_kernel,
        out_shape=out_shape,
        in_specs=[smem] + [hbm] * 3 + [vmem] + [hbm] * 5,
        out_specs=[hbm] * 4 + [vmem, hbm, hbm] + [vmem] * 3,
        scratch_shapes=scratch,
        compiler_params=pltpu.CompilerParams(
            collective_id=0, has_side_effects=True, vmem_limit_bytes=63 * 2**20
        ),
    )(
        lengths,
        inputs.reshape(half),
        cotangent.reshape(half),
        cotangent,
        vectors,
        *shards
    )


def reduce_kernel(grad_ref, small_ref, in_grad, out_grad, sum_ref, work, small, *rest):
    slots, (load_sem, send, recv) = rest[:-3], rest[-3:]
    place = Place()
    links = Links(place, send, recv)
    plan = Plan()
    depth = in_grad.shape[1] // 3
    parts = []
    remaining = list(slots)
    for j, before, after in MIXER_GRADS:
        where = pl.ds(depth * j, depth)
        count = len(before) + 1 + len(after)
        mine, remaining = remaining[:count], remaining[count:]
        parts.append(
            Reduce(
                links,
                lambda z, y, c, x, where=where: work.at[z, y, x, :, where],
                before,
                mine[: len(before)] + mine[len(before) + 1 :],
                mine[len(before)],
                after,
                lambda z, y, c, x, where=where: grad_ref.at[z, y, c, x, :, where],
            )
        )
    loads = [
        pltpu.make_async_copy(
            grad_ref.at[:, :, place.c, :, :, pl.ds(depth * j, depth)],
            work.at[:, :, :, :, pl.ds(depth * j, depth)],
            load_sem.at[number],
        )
        for number, (j, _, _) in enumerate(MIXER_GRADS)
    ]
    ring = ("c", "x", "y", "pair", "far")
    first = links.take(len(ring))
    rounds = [
        links.copy(small.at[i], small.at[len(ring) + 1 + i], first + i, name)
        for i, name in enumerate(ring)
    ]

    def open_all():
        for load in loads:
            load.start()
        place.greet(["c", "y", "x", "up", "down", "far"])
        small[0] = small_ref[...]

    start = plan.add([], open_all)
    opened = [
        [plan.add([start], part.begin, distance) for distance in (3, 2, 1, 0)]
        for part in parts
    ]
    ends = []
    for part, load, begun in zip(parts, loads, opened):
        loaded = plan.add([start], load.wait)
        line = []
        for number, distance in enumerate((3, 2, 1, 0)):
            step = plan.add([loaded, begun[number]], part.across, 0, distance)
            for stage in range(1, part.before):
                step = plan.add([step], part.across, stage, distance)
            line = [plan.add([step] + line, part.along, distance)]
        for stage in range(part.before, len(part.stages)):
            line = [plan.add(line, part.late_start, stage)]
            line = [plan.add(line, part.late_take, stage)]
        ends += line

    def add_round(number):
        rounds[number].wait_recv()
        small[number + 1] = small[number] + small[len(ring) + 1 + number]

    step = plan.add(sum(opened, []), rounds[0].start)
    for number in range(len(ring)):
        step = plan.add([step], add_round, number)
        if number + 1 < len(ring):
            step = plan.add([step], rounds[number + 1].start)

    def close():
        sum_ref[...] = small[len(ring)]
        own = work[place.z, place.y, place.x].astype(F32)
        in_grad[...] = own[:, : 3 * depth]
        out_grad[...] = own[:, 3 * depth :]
        for part in parts:
            part.drain()
        for copy in rounds:
            copy.wait_send()

    plan.add(ends + [step], close)
    plan.run(LAST_STEPS or list(range(len(plan.steps))))


def reduce_all(grad, small):
    columns = grad.shape[-1]
    depth = columns // 4
    block = (grad.shape[-2], depth)
    slots = []
    for _, before, after in MIXER_GRADS:
        left = len(before) + len(after)
        for _ in before:
            left -= 1
            slots.append((DEPTH,) + (2,) * left + block)
        slots.append((DEPTH + 1,) + (2,) * left + block)
        for _ in after:
            left -= 1
            slots.append((2,) * left + block)
    vmem = pl.BlockSpec(memory_space=pltpu.VMEM)
    hbm = pl.BlockSpec(memory_space=pl.ANY)
    return pl.pallas_call(
        reduce_kernel,
        out_shape=[
            jax.ShapeDtypeStruct((block[0], 3 * depth), F32),
            jax.ShapeDtypeStruct((block[0], depth), F32),
            jax.ShapeDtypeStruct(small.shape, F32),
        ],
        in_specs=[hbm, vmem],
        out_specs=[vmem] * 3,
        scratch_shapes=[
            pltpu.VMEM((DEPTH, 2, 2) + block[:1] + (columns,), BF16),
            pltpu.VMEM((11,) + small.shape, F32),
        ]
        + [pltpu.VMEM(slot, BF16) for slot in slots]
        + [
            pltpu.SemaphoreType.DMA((len(MIXER_GRADS),)),
            pltpu.SemaphoreType.DMA((96,)),
            pltpu.SemaphoreType.DMA((96,)),
        ],
        compiler_params=pltpu.CompilerParams(
            collective_id=2, has_side_effects=True, vmem_limit_bytes=58 * 2**20
        ),
    )(grad, small)


def shifted(block, axis, distance):
    devices = range(lax.axis_size(axis))
    route = [(i - distance, i) for i in devices if i - distance in devices]
    return lax.ppermute(block, axis, route)


def mixer_forward(inputs, lengths, norm_one_gain, conv_weight, norm_two_gain, in_all, out_all):
    tok_rows, feat_width = inputs.shape[1:]
    kept = {}
    x_float = inputs[0].astype(F32)
    kernel = conv_weight.astype(F32)
    position = lax.axis_index("seq") * tok_rows + lax.iota(jnp.int32, tok_rows)
    valid_mask = (position < lengths[0]).astype(F32)[:, None]
    scale_one = lax.rsqrt(jnp.mean(x_float * x_float, axis=1, keepdims=True) + epsilon)
    hat_one = x_float * scale_one
    normed_one = (hat_one * norm_one_gain.astype(F32)).astype(BF16)
    projected = rounded_dot(normed_one, in_all)
    b_part = projected[:, :feat_width]
    c_part = projected[:, feat_width : 2 * feat_width]
    v_part = projected[:, 2 * feat_width :]
    product = (b_part * v_part).astype(BF16)
    carried = shifted(product[tok_rows - 2 :], "seq", 1)
    extended = jnp.concatenate([carried, product], axis=0).astype(F32)
    conv_out = (
        kernel[0] * extended[:tok_rows]
        + kernel[1] * extended[1 : tok_rows + 1]
        + kernel[2] * extended[2:]
    )
    gated_mix = (c_part * conv_out).astype(BF16)
    mixer_out = rounded_dot(gated_mix, out_all)
    middle = x_float + valid_mask * mixer_out
    scale_two = lax.rsqrt(jnp.mean(middle * middle, axis=1, keepdims=True) + epsilon)
    hat_two = middle * scale_two
    normed_two = (hat_two * norm_two_gain.astype(F32)).astype(BF16)
    kept.update(locals())
    return kept


def mixer_backward(kept, grad_out, normed_part, norm_one_gain, norm_two_gain, in_all, out_all):
    tok_rows, feat_width = grad_out.shape
    kernel = kept["kernel"]
    extended, conv_out = kept["extended"], kept["conv_out"]
    hat_one, hat_two = kept["hat_one"], kept["hat_two"]
    grad_gain_two = jnp.sum(normed_part * hat_two, axis=0)
    scaled_two = normed_part * norm_two_gain.astype(F32)
    grad_middle = grad_out + kept["scale_two"] * (
        scaled_two - hat_two * jnp.mean(scaled_two * hat_two, axis=1, keepdims=True)
    )
    grad_mix = (kept["valid_mask"] * grad_middle).astype(BF16)
    grad_out_w = over_rows(kept["gated_mix"], grad_mix)
    grad_gated = by_rows(grad_mix, out_all)
    grad_c = grad_gated * conv_out
    grad_conv_in = grad_gated * kept["c_part"]
    grad_kernel = jnp.stack(
        [
            jnp.sum(grad_conv_in * extended[:tok_rows], axis=0),
            jnp.sum(grad_conv_in * extended[1 : tok_rows + 1], axis=0),
            jnp.sum(grad_conv_in * extended[2:], axis=0),
        ]
    )
    padded_grad = jnp.pad(grad_conv_in, ((2, 2), (0, 0)))
    grad_extended = (
        kernel[0] * padded_grad[2 : tok_rows + 4]
        + kernel[1] * padded_grad[1 : tok_rows + 3]
        + kernel[2] * padded_grad[: tok_rows + 2]
    )
    returned = shifted(grad_extended[:2], "seq", -1)
    grad_product = grad_extended[2:] + jnp.concatenate(
        [jnp.zeros((tok_rows - 2, feat_width), F32), returned], axis=0
    )
    grad_projected = jnp.concatenate(
        [grad_product * kept["v_part"], grad_c, grad_product * kept["b_part"]], axis=1
    ).astype(BF16)
    grad_in_w = over_rows(kept["normed_one"], grad_projected)
    grad_normed_one = by_rows(grad_projected, in_all)
    grad_gain_one = jnp.sum(grad_normed_one * hat_one, axis=0)
    scaled_one = grad_normed_one * norm_one_gain.astype(F32)
    grad_inputs = grad_middle + kept["scale_one"] * (
        scaled_one - hat_one * jnp.mean(scaled_one * hat_one, axis=1, keepdims=True)
    )
    return grad_inputs, grad_in_w, grad_out_w, grad_gain_one, grad_kernel, grad_gain_two


def in_blocks(
    inputs,
    lengths,
    norm_one_gain,
    w_in,
    conv_weight,
    w_out,
    norm_two_gain,
    w_gate,
    w_up,
    w_down,
    cotangent,
):
    width = inputs.shape[2]
    vectors = jnp.concatenate([norm_one_gain[None], conv_weight, norm_two_gain[None]])
    found = layer(
        lengths,
        inputs[0],
        cotangent[0],
        vectors.astype(F32),
        (w_in, w_out, w_gate, w_up, w_down.T),
    )
    mixer_grad, small, result, grad_inputs, gate, up, down = found[3:]
    in_grad, out_grad, total = reduce_all(
        mixer_grad.reshape(DEPTH, 2, 2, 2, 32, 4 * width), small
    )
    return (
        result.reshape(inputs.shape),
        grad_inputs[None],
        total[0],
        in_grad,
        total[1:4],
        out_grad,
        total[4],
        gate.astype(F32),
        up.astype(F32),
        down.T.astype(F32),
    )


def anywhere(
    inputs,
    lengths,
    norm_one_gain,
    w_in,
    conv_weight,
    w_out,
    norm_two_gain,
    w_gate,
    w_up,
    w_down,
    cotangent,
):
    both = ("seq", "batch")
    in_all = lax.all_gather(w_in, both, axis=0, tiled=True)
    out_all = lax.all_gather(w_out, both, axis=0, tiled=True)
    gate_use, up_use = (
        lax.all_gather(
            lax.all_gather(w, "seq", axis=0, tiled=True), "batch", axis=1, tiled=True
        )
        for w in (w_gate, w_up)
    )
    down_use = lax.all_gather(
        lax.all_gather(w_down, "seq", axis=1, tiled=True), "batch", axis=0, tiled=True
    )
    kept = mixer_forward(
        inputs, lengths, norm_one_gain, conv_weight, norm_two_gain, in_all, out_all
    )
    rows_norm = kept["normed_two"]
    grad_out = cotangent[0].astype(F32)
    rows_grad = (kept["valid_mask"] * grad_out).astype(BF16)
    gate_val = rounded_dot(rows_norm, gate_use)
    up_val = rounded_dot(rows_norm, up_use)
    hidden = (jax.nn.silu(gate_val) * up_val).astype(BF16)
    ffn_out = rounded_dot(hidden, down_use)
    result = (kept["middle"] + kept["valid_mask"] * ffn_out).astype(BF16)
    grad_down = over_rows(hidden, rows_grad)
    grad_hidden = by_rows(rows_grad, down_use)
    sigmoid_gate = jax.nn.sigmoid(gate_val)
    slope_gate = sigmoid_gate * (1.0 + gate_val * (1.0 - sigmoid_gate))
    grad_gate = (grad_hidden * up_val * slope_gate).astype(BF16)
    grad_up = (grad_hidden * gate_val * sigmoid_gate).astype(BF16)
    grad_gate_w = over_rows(rows_norm, grad_gate)
    grad_up_w = over_rows(rows_norm, grad_up)
    normed_part = by_rows(grad_gate, gate_use) + by_rows(grad_up, up_use)

    def owned(grad, axis):
        half = lax.psum_scatter(
            grad.astype(BF16), "batch", scatter_dimension=axis, tiled=True
        ).astype(F32)
        return lax.psum_scatter(half, "seq", scatter_dimension=1 - axis, tiled=True)

    shards = owned(grad_gate_w, 1), owned(grad_up_w, 1), owned(grad_down, 0)
    grad_inputs, grad_in_w, grad_out_w, gain_one, taps, gain_two = mixer_backward(
        kept, grad_out, normed_part, norm_one_gain, norm_two_gain, in_all, out_all
    )
    shard_in, shard_out = (
        lax.psum_scatter(grad, both, scatter_dimension=0, tiled=True)
        for grad in (grad_in_w, grad_out_w)
    )
    total_one, total_two, total_kernel = lax.psum((gain_one, gain_two, taps), both)
    return (
        result[None],
        grad_inputs[None],
        total_one,
        shard_in,
        total_kernel,
        shard_out,
        total_two,
    ) + shards


def solution(mesh):
    in_specs = (
        P("batch", "seq", None),
        P("batch"),
        P(),
        P(("seq", "batch"), None),
        P(),
        P(("seq", "batch"), None),
        P(),
        P("seq", "batch"),
        P("seq", "batch"),
        P("batch", "seq"),
        P("batch", "seq", None),
    )
    out_specs = (
        P("batch", "seq", None),
        P("batch", "seq", None),
        P(),
        P(("seq", "batch"), None),
        P(),
        P(("seq", "batch"), None),
        P(),
        P("seq", "batch"),
        P("seq", "batch"),
        P("batch", "seq"),
    )
    by_blocks = mesh.shape["seq"] == 4 * DEPTH and mesh.shape["batch"] == 2
    return jax.shard_map(
        in_blocks if by_blocks else anywhere,
        mesh=mesh,
        in_specs=in_specs,
        out_specs=out_specs,
        check_vma=False,
    )
```

```python
import functools

import jax
import jax.numpy as jnp
from jax import lax
from jax.experimental import pallas as pl
from jax.experimental.pallas import tpu as pltpu
from jax.sharding import PartitionSpec as P

epsilon = 1e-05
MESH = pl.DeviceIdType.MESH
F32, BF16 = jnp.float32, jnp.bfloat16
DEPTH = 4
PARTS = [384, 256, 256, 256]
KINDS = ("z", "y", "z", "z")
GRAD_KINDS = ("y", "z", "z", "z")
ORDER = (0, 1, 2, 3)
SPOTS = [0, 1152, 0, 768]
PAIRS = tuple(k for k, kind in enumerate(KINDS) if kind == "y")
PAIR_EARLY = 1
MIXER = (
    (2, ["x", "y", "c"]),
    (0, ["y", "x", "c"]),
    (1, ["y", "x", "c"]),
    (3, ["x", "y", "c"]),
)
MIXER_GRADS = (
    (0, ["c", "x", "y"], []),
    (2, ["c", "y", "x"], []),
    (3, ["c"], ["x", "y"]),
    (1, ["c", "y", "x"], []),
)
LAST_STEPS = (
    0, 15, 17, 1, 64, 34, 51, 9, 7, 13, 11, 5, 73, 18, 52, 53, 2, 12, 3, 35, 6, 10, 22,
    65, 14, 8, 54, 4, 19, 16, 43, 74, 81, 58, 55, 39, 36, 82, 83, 66, 26, 37, 84, 20,
    21, 69, 38, 67, 56, 68, 85, 30, 23, 57, 77, 40, 75, 70, 27, 86, 87, 47, 31, 24, 44,
    25, 71, 41, 72, 42, 59, 60, 78, 28, 29, 45, 88, 76, 48, 46, 89, 61, 62, 32, 79, 33,
    80, 49, 50, 63, 90, 91,
)
Z_GATE = 1
ACTS = 1920
EARLY = 1
STEPS = (
    0, 8, 14, 7, 15, 17, 4, 10, 6, 3, 21, 5, 82, 88, 9, 83, 1, 64, 84, 2, 20, 65, 85,
    28, 29, 52, 25, 46, 47, 66, 70, 24, 100, 67, 12, 34, 30, 101, 48, 35, 49, 86, 31,
    87, 13, 53, 91, 18, 72, 56, 50, 102, 32, 68, 22, 51, 69, 113, 89, 33, 11, 54, 95,
    71, 73, 36, 16, 37, 90, 57, 93, 55, 103, 141, 58, 77, 38, 99, 39, 42, 40, 74, 76,
    142, 62, 41, 97, 61, 44, 114, 105, 59, 19, 158, 94, 80, 60, 92, 23, 45, 143, 81, 96,
    26, 75, 104, 107, 78, 43, 63, 98, 144, 159, 108, 145, 79, 109, 146, 147, 148, 149,
    150, 117, 153, 106, 27, 121, 151, 154, 115, 160, 161, 152, 155, 118, 156, 157, 166,
    111, 129, 164, 122, 112, 110, 116, 167, 119, 162, 123, 133, 168, 130, 163, 120, 124,
    126, 134, 165, 169, 131, 170, 171, 172, 135, 178, 132, 179, 125, 136, 127, 137, 180,
    183, 139, 128, 138, 193, 173, 181, 140, 194, 195, 196, 184, 185, 197, 198, 182, 186,
    203, 204, 206, 207, 174, 199, 217, 205, 218, 231, 187, 201, 188, 200, 219, 191, 209,
    208, 220, 210, 232, 202, 221, 211, 213, 234, 223, 224, 189, 233, 236, 235, 222, 237,
    238, 241, 175, 239, 243, 212, 240, 190, 246, 242, 247, 248, 244, 225, 245, 250, 215,
    176, 249, 226, 251, 227, 252, 214, 253, 192, 256, 266, 254, 255, 267, 261, 228, 257,
    259, 177, 229, 263, 258, 268, 216, 269, 264, 260, 265, 230, 272, 262, 270, 271, 273,
    274, 275,
)


def over_rows(left, right):
    return lax.dot_general(
        left, right, (((0,), (0,)), ((), ())), preferred_element_type=F32
    )


def by_rows(left, right):
    return lax.dot_general(
        left, right, (((1,), (1,)), ((), ())), preferred_element_type=F32
    )


def dot(left, right):
    return jnp.dot(left, right, preferred_element_type=F32)


def rounded_dot(left, right):
    return dot(left, right).astype(BF16).astype(F32)


class Place:
    def __init__(self):
        self.s = lax.axis_index("seq")
        self.x = lax.axis_index("batch")
        self.z = self.s // 4
        self.y = (self.s // 2) % 2
        self.c = self.s % 2
        self.last = lax.axis_size("seq") - 1
        self.own = {"y": self.y, "c": self.c, "x": self.x}
        self.device = {
            "c": (self.s + 1 - 2 * self.c, self.x),
            "y": (self.s + 2 - 4 * self.y, self.x),
            "x": (self.s, 1 - self.x),
            "up": (self.s + 4, self.x),
            "down": (self.s - 4, self.x),
            "next": (self.s + 1, self.x),
            "prev": (self.s - 1, self.x),
            "pair": (self.s + 4 - 8 * (self.z % 2), self.x),
            "far": (self.s + 8 - 16 * (self.z // 2), self.x),
        }

    def greet(self, names):
        barrier = pltpu.get_barrier_semaphore()
        ends = {
            "up": self.z < DEPTH - 1,
            "down": self.z > 0,
            "next": self.s < self.last,
            "prev": self.s > 0,
        }

        def signal(name):
            pl.semaphore_signal(
                barrier, inc=1, device_id=self.device[name], device_id_type=MESH
            )

        expected = 0
        for name in names:
            if name in ends:
                pl.when(ends[name])(functools.partial(signal, name))
                expected = expected + ends[name].astype(jnp.int32)
            else:
                signal(name)
                expected = expected + 1
        pl.semaphore_wait(barrier, expected)


class Links:
    def __init__(self, place, send, recv):
        self.place, self.send, self.recv = place, send, recv
        self.used = 0

    def take(self, count):
        first = self.used
        self.used += count
        assert self.used <= self.send.shape[0]
        return first

    def copy(self, source, target, index, name):
        return pltpu.make_async_remote_copy(
            src_ref=source,
            dst_ref=target,
            send_sem=self.send.at[index],
            recv_sem=self.recv.at[index],
            device_id=self.place.device[name],
            device_id_type=MESH,
        )


def way(direction):
    return (1 - direction) // 2


class Line:
    def take_line(self):
        self.first = self.links.take(2 * DEPTH)

    def hop(self, source, target, direction, level):
        place = self.place
        index = self.first + DEPTH * way(direction) + level
        return pltpu.make_async_remote_copy(
            src_ref=source,
            dst_ref=target,
            send_sem=self.links.send.at[index],
            recv_sem=self.links.recv.at[index],
            device_id=(place.s + 4 * direction, place.x),
            device_id_type=MESH,
        )

    def levels(self, distance, action):
        z = self.place.z
        if distance == 0:
            action(z, None)
            return

        def side(i, carry):
            direction = 1 - 2 * i
            level = z - direction * distance

            @pl.when((level >= 0) & (level < DEPTH))
            def _():
                action(level, direction)

            return carry

        lax.fori_loop(0, 2, side, 0)

    def beyond(self, direction):
        further = self.place.z + direction
        return (further >= 0) & (further < DEPTH)


class Gather(Line):
    def __init__(self, links, view, stages):
        self.links, self.view, self.stages = links, view, stages
        self.place = links.place
        self.take_line()
        self.rows = {name: links.take(DEPTH) for name in stages}

    def block(self, stage, level, theirs=False):
        where = dict(self.place.own)
        if stage is not None:
            for name in self.stages[:stage]:
                where[name] = slice(None)
            if theirs:
                where[self.stages[stage]] = 1 - where[self.stages[stage]]
        return self.view(level, where["y"], where["c"], where["x"])

    def line(self, direction, level):
        ref = self.block(None, level)
        return self.hop(ref, ref, direction, level)

    def staged(self, stage, level, theirs=False):
        name = self.stages[stage]
        ref = self.block(stage, level, theirs)
        return self.links.copy(ref, ref, self.rows[name] + level, name)

    def along(self, distance):
        def hand_on(level, direction):
            if distance:
                self.line(direction, level).wait_recv()

            @pl.when(self.beyond(direction))
            def _():
                self.line(direction, level).start()

        if distance == 0:
            hand_on(self.place.z, 1)
            hand_on(self.place.z, -1)
        else:
            self.levels(distance, hand_on)

    def depart(self, distance):
        self.levels(distance, lambda level, _: self.staged(0, level).start())

    def across(self, stage, distance):
        def pass_on(level, _):
            self.staged(stage, level, True).wait_recv()
            if stage + 1 < len(self.stages):
                self.staged(stage + 1, level).start()

        self.levels(distance, pass_on)

    def drain_line(self):
        z = self.place.z

        def sent(level, carry):
            @pl.when((z >= level) & (z < DEPTH - 1))
            def _():
                self.line(1, level).wait_send()

            @pl.when((z <= level) & (z > 0))
            def _():
                self.line(-1, level).wait_send()

            return carry

        lax.fori_loop(0, DEPTH, sent, 0)

    def drain(self):
        self.drain_line()

        def sent(level, carry):
            for stage in range(len(self.stages)):
                self.staged(stage, level).wait_send()
            return carry

        lax.fori_loop(0, DEPTH, sent, 0)


class PairGather(Gather):
    def __init__(self, links, ref):
        super().__init__(links, lambda z, y, c, x: ref.at[z, y], ["y"])
        self.ref = ref

    def line(self, direction, level):
        ref = self.ref.at[level]
        return self.hop(ref, ref, direction, level)

    def begin(self):
        self.staged(0, self.place.z).start()

    def join(self):
        self.staged(0, self.place.z, True).wait_recv()
        self.along(0)

    def drain(self):
        self.staged(0, self.place.z).wait_send()
        self.drain_line()


def add_into(target, source):
    def add(i, carry):
        target[i] = (target[i].astype(F32) + source[i].astype(F32)).astype(BF16)
        return carry

    if len(target.shape) > 2:
        lax.fori_loop(0, target.shape[0], add, 0)
    else:
        add(Ellipsis, 0)


class Reduce(Line):
    def __init__(self, links, view, stages, slots, line_slots, after=(), source=None):
        self.links, self.view, self.stages = links, view, list(stages) + list(after)
        self.slots, self.line_slots = slots, line_slots
        self.source = source or view
        self.before = len(stages)
        self.place = links.place
        self.take_line()
        self.rows = {name: links.take(DEPTH) for name in stages}
        self.rows.update({name: links.take(1) for name in after})

    def block(self, stage, level, theirs=False):
        where = dict(self.place.own)
        for name in self.stages[stage + 1 :]:
            where[name] = slice(None)
        if theirs:
            where[self.stages[stage]] = 1 - where[self.stages[stage]]
        view = self.source if theirs and stage == 0 else self.view
        return view(level, where["y"], where["c"], where["x"])

    def staged(self, stage, level):
        name = self.stages[stage]
        late = stage >= self.before
        return self.links.copy(
            self.block(stage, level, True),
            self.slots[stage] if late else self.slots[stage].at[level],
            self.rows[name] + (0 if late else level),
            name,
        )

    def late_start(self, stage):
        self.staged(stage, self.place.z).start()

    def late_take(self, stage):
        z = self.place.z
        self.staged(stage, z).wait_recv()
        add_into(self.block(stage, z), self.slots[stage])

    def slot(self, direction, level):
        return self.line_slots.at[level + 1 - way(direction)]

    def line(self, direction, level):
        ref = self.block(self.before - 1, level)
        return self.hop(ref, self.slot(direction, level), direction, level)

    def begin(self, distance):
        self.levels(distance, lambda level, _: self.staged(0, level).start())

    def across(self, stage, distance):
        def take(level, _):
            self.staged(stage, level).wait_recv()
            add_into(self.block(stage, level), self.slots[stage].at[level])
            if stage + 1 < self.before:
                self.staged(stage + 1, level).start()

        self.levels(distance, take)

    def take(self, direction, level):
        self.line(direction, level).wait_recv()
        add_into(self.block(self.before - 1, level), self.slot(direction, level))

    def along(self, distance):
        if distance == 0:

            def side(i, carry):
                direction = 1 - 2 * i

                @pl.when(self.beyond(-direction))
                def _():
                    self.take(direction, self.place.z)

                return carry

            lax.fori_loop(0, 2, side, 0)
            return

        def send(level, back):
            @pl.when(self.beyond(back))
            def _():
                self.take(-back, level)

            self.line(-back, level).start()

        self.levels(distance, send)

    def drain_line(self):
        z = self.place.z

        def sent(level, carry):
            @pl.when(z > level)
            def _():
                self.line(-1, level).wait_send()

            @pl.when(z < level)
            def _():
                self.line(1, level).wait_send()

            return carry

        lax.fori_loop(0, DEPTH, sent, 0)

    def drain(self):
        self.drain_line()

        def sent(level, carry):
            for stage in range(self.before):
                self.staged(stage, level).wait_send()
            return carry

        lax.fori_loop(0, DEPTH, sent, 0)
        for stage in range(self.before, len(self.stages)):
            self.staged(stage, self.place.z).wait_send()


class PairReduce(Reduce):
    def __init__(self, links, ref, slot, line_slots):
        super().__init__(links, lambda z, y, c, x: ref.at[z, y], ["y"], None, line_slots)
        self.ref, self.last_slot = ref, slot

    def block(self, stage, level, theirs=False):
        return self.ref.at[level]

    def final(self):
        place = self.place
        return self.links.copy(
            self.ref.at[place.z, 1 - place.y], self.last_slot, self.rows["y"], "y"
        )

    def finish(self):
        self.final().wait_recv()
        add_into(self.ref.at[self.place.z, self.place.y], self.last_slot)

    def drain(self):
        self.drain_line()
        self.final().wait_send()


class Plan:
    def __init__(self):
        self.steps = []

    def add(self, needs, action, *args, busy=False):
        self.steps.append((tuple(needs), functools.partial(action, *args), busy))
        return len(self.steps) - 1

    def run(self, order):
        seen = set()
        assert sorted(order) == list(range(len(self.steps)))
        for index in order:
            needs, action, _ = self.steps[index]
            assert seen.issuperset(needs)
            action()
            seen.add(index)


def mean_of(values):
    return jnp.mean(values, axis=1, keepdims=True)


def layer_kernel(
    length_ref,
    x_ref,
    grad_ref,
    grad_rows_ref,
    vectors_ref,
    in_ref,
    out_ref,
    gate_ref,
    up_ref,
    down_ref,
    mixer_hbm,
    parts_hbm,
    middle_hbm,
    mixer_grad,
    small,
    result_ref,
    input_grad,
    gate_grad,
    up_grad,
    down_grad,
    wm,
    w0,
    w1,
    w2,
    w3,
    product,
    middle,
    tokens,
    grads,
    r0,
    r1,
    r2,
    r3,
    l0,
    l1,
    l2,
    l3,
    e0,
    e1,
    e2,
    e3,
    acts,
    out_sum,
    back_sum,
    keep_sem,
    send,
    recv,
):
    place = Place()
    links = Links(place, send, recv)
    plan = Plan()
    rows, depth = parts_hbm.shape[0] // 3, parts_hbm.shape[1]
    tile = rows // 2
    weights, edges = (w0, w1, w2, w3), (e0, e1, e2, e3)
    quarter = sum(PARTS)
    offsets = [sum(PARTS[:k]) for k in range(len(PARTS))]

    def columns(first, count):
        return lambda z, y, c, x: wm.at[z, y, c, x, :, pl.ds(first, count)]

    mixers = [
        Gather(links, columns(depth * j, depth), stages)
        for j, stages in MIXER
    ]
    gathers, reduces = [], []
    for number, (w, r, l) in enumerate(zip(weights, (r0, r1, r2, r3), (l0, l1, l2, l3))):
        view = lambda z, y, c, x, w=w: w.at[z, y]
        if KINDS[number] == "y":
            gathers.append(PairGather(links, w))
        else:
            gathers.append(Gather(links, view, ["y"]))
        if GRAD_KINDS[number] == "y":
            reduces.append(PairReduce(links, w, r, l))
        else:
            reduces.append(Reduce(links, view, ["y"], [r], l))

    def sides(number, quarter_index):
        width = PARTS[number]
        start = pl.multiple_of(quarter_index * quarter + offsets[number], 128)
        return [
            (ref.at[:, pl.ds(start, width)], pl.ds(side * width, width))
            for side, ref in enumerate((gate_ref, up_ref, down_ref))
        ]

    twins = [
        [
            links.copy(
                source,
                weights[number].at[place.z, place.y, place.c, :, where],
                links.take(1),
                "c",
            )
            for source, where in sides(number, 1 - place.c)
        ]
        for number in range(len(PARTS))
    ]


    def share(ref):
        first = links.take(3)
        return (
            links.copy(ref[0], ref[1], first, "c"),
            links.copy(ref[0], ref[2], first + 1, "x"),
            links.copy(ref[2], ref[3], first + 2, "c"),
        )

    shared_grads = [
        share([grads.at[i // 2, 2 * (i % 2) + h, q] for i in range(4)])
        for h in range(2)
        for q in range(2)
    ]
    shared_tokens = [
        share([tokens.at[i // 2, 2 * (i % 2) + h] for i in range(4)]) for h in range(2)
    ]
    edge = links.copy(
        product.at[pl.ds(rows, 8)], product.at[pl.ds(0, 8)], links.take(1), "next"
    )
    back_edge = links.copy(
        middle.at[pl.ds(0, 8)], middle.at[pl.ds(rows, 8)], links.take(1), "prev"
    )
    has_next, has_prev = place.s < place.last, place.s > 0
    slots = [
        wm.at[pl.ds(2 * (i // 4), 2), :, :, :, :, pl.ds(depth * (i % 4), depth)]
        for i in range(6)
    ]

    def give_back(total, slots):
        first = links.take(3)
        return (
            links.copy(total.at[3], slots[2], first, "c"),
            links.copy(total.at[2], slots[1], first + 1, "x"),
            links.copy(total.at[1], slots[0], first + 2, "c"),
        )

    returned = [give_back(back_sum, slots[:3]), give_back(out_sum, slots[3:])]
    trades = [
        links.copy(w.at[place.z, place.y, 1 - place.c], e, links.take(1), "c")
        for w, e in zip(weights, edges)
    ]

    count = iter(range(keep_sem.shape[0]))

    def local(source, target):
        return pltpu.make_async_copy(source, target, keep_sem.at[next(count)])

    parts = acts.at[pl.ds(0, 3 * rows), pl.ds(0, depth)]
    save_mixer = local(wm, mixer_hbm)
    save_parts = local(parts, parts_hbm)
    save_middle = local(middle.at[pl.ds(0, rows)], middle_hbm)
    fills = [
        [
            local(source, weights[number].at[place.z, place.y, place.c, :, where])
            for source, where in sides(number, place.c)
        ]
        for number in range(len(PARTS))
    ]
    mine = wm.at[place.z, place.y, place.c, place.x]
    fill_in = local(in_ref, mine.at[:, pl.ds(0, 3 * depth)])
    fill_out = local(out_ref, mine.at[:, pl.ds(3 * depth, depth)])
    inner = pl.ds(0, rows)
    low_x, high_x = out_sum.at[1], back_sum.at[0]
    view = (2,) + tokens.shape[2:]
    load_x = [local(x_ref, x) for x in (low_x, high_x)]
    load_grad = local(grad_ref, grads.at[0, pl.ds(0, 2)])
    load_grad_rows = local(grad_rows_ref, acts.at[pl.ds(3 * rows, rows), pl.ds(0, depth)])
    save_result = local(back_sum.at[1], result_ref)
    blocks = [tokens.at[0], tokens.at[1], grads.at[0], grads.at[1]]
    load_mixer = [
        local(mixer_hbm.at[:, :, :, :, :, pl.ds(depth * j, depth)], block)
        for j, block in enumerate(blocks)
    ]
    load_parts = local(parts_hbm, parts)
    load_middle = local(middle_hbm, product.at[pl.ds(8, rows)])
    staging = [acts.at[pl.ds(2 * rows * i, 2 * rows), pl.ds(depth, 2 * tile)] for i in range(2)]
    stores = [
        local(staging[j % 2], mixer_grad.at[:, pl.ds(2 * tile * ((j + 6) % 8), 2 * tile)])
        for j in range(8)
    ]
    save_grad, save_inputs = (
        local(middle.at[pl.ds(0, rows)], input_grad) for _ in range(2)
    )
    load_back = local(input_grad, middle.at[pl.ds(0, rows)])

    def hear(*copies):
        for copy in copies:
            copy.wait_recv()

    def begin(*copies):
        for copy in copies:
            copy.start()

    def done(*copies):
        for copy in copies:
            copy.wait()

    def valid_rows(first, count):
        position = place.s * rows + first + lax.broadcasted_iota(
            jnp.int32, (count, 1), 0
        )
        return (position < length_ref[0]).astype(F32)

    def open_all():
        for copy in [fill_in, fill_out, load_x[0], load_grad] + sum(fills, []):
            copy.start()
        place.greet(["c", "y", "x", "up", "down", "next", "prev"])
        fill_in.wait()
        fill_out.wait()

    def clear():
        @pl.when(place.s == 0)
        def _():
            product[pl.ds(0, 8)] = jnp.zeros((8, depth), F32)

        @pl.when(place.s == place.last)
        def _():
            middle[pl.ds(rows, 8)] = jnp.zeros((8, depth), F32)

    def first_norm(source, target):
        x = source[...].reshape(rows, depth).astype(F32)
        scale = lax.rsqrt(mean_of(x * x) + epsilon)
        normed = (x * scale * vectors_ref[0:1]).astype(BF16)
        target[...] = normed.reshape(view)

    def mask_grads():
        masked = grads[0, pl.ds(0, 2)].reshape(rows, depth).astype(F32)
        masked *= valid_rows(0, rows)
        grads[0, pl.ds(0, 2)] = masked.astype(BF16).reshape(view)

    def project(index):
        weight = wm[..., depth * index : depth * (index + 1)].reshape(depth, depth)
        acts[rows * index : rows * (index + 1), :depth] = dot(
            out_sum[0].reshape(rows, depth), weight
        ).astype(BF16)

    def multiply():
        b_part = acts[:rows, :depth].astype(F32)
        v_part = acts[2 * rows : 3 * rows, :depth].astype(F32)
        product[pl.ds(8, rows)] = (b_part * v_part).astype(BF16).astype(F32)

    def conv_rows(start):
        total = 0.0
        for tap in range(3):
            first = start + 6 + tap
            total += vectors_ref[1 + tap : 2 + tap] * product[first : first + tile]
        return total

    def mix(index):
        start = tile * index
        where = slice(start, start + tile)
        c_part = acts[rows + start : rows + start + tile, :depth].astype(F32)
        gated = (c_part * conv_rows(start)).astype(BF16)
        weight = wm[..., 3 * depth :].reshape(depth, depth)
        x = low_x[index].reshape(tile, depth).astype(F32)
        total = x + valid_rows(start, tile) * dot(gated, weight)
        middle[where] = total
        scale = lax.rsqrt(mean_of(total * total) + epsilon)
        new = (total * scale * vectors_ref[4:5]).astype(BF16)
        tokens[0, index] = new.reshape(tokens.shape[2:])

    begun = set()

    def one_block(number, pair, i, carry):
        weight, width, spot = weights[number], PARTS[number], SPOTS[number]
        where = pl.ds(pl.multiple_of(rows * (2 * pair + i), rows), rows)
        gate_up = weight[..., : 2 * width].reshape(depth, 2 * width)
        both = dot(tokens[pair, pl.ds(2 * i, 2)].reshape(rows, depth), gate_up)
        gate, up = both[:, :width], both[:, width:]
        sigmoid = jax.nn.sigmoid(gate)
        silu = gate * sigmoid
        slope = sigmoid + silu * (1.0 - sigmoid)
        kept = (silu * up).astype(BF16)
        down = weight[..., 2 * width :].reshape(depth, width)
        grad_hidden = dot(grads[pair, pl.ds(2 * i, 2)].reshape(rows, depth), down)
        acts[where, spot : spot + width] = (grad_hidden * up * slope).astype(BF16)
        acts[where, spot + width : spot + 2 * width] = (grad_hidden * silu).astype(BF16)
        acts[where, spot + 2 * width : spot + 3 * width] = kept
        out_part = by_rows(kept, down)
        back_part = by_rows(acts[where, spot : spot + 2 * width], gate_up)
        shape = out_sum.shape[1:]
        index = 2 * pair + i
        if pair in begun:
            out_part += out_sum[index].reshape(rows, depth).astype(F32)
            back_part += back_sum[index].reshape(rows, depth).astype(F32)
        out_sum[index] = out_part.astype(BF16).reshape(shape)
        back_sum[index] = back_part.astype(BF16).reshape(shape)
        return carry

    def block(number, pair):
        lax.fori_loop(0, 2, functools.partial(one_block, number, pair), 0)
        begun.add(pair)

    def weigh(number):
        weight, width, spot = weights[number], PARTS[number], SPOTS[number]
        for source, first, size in ((tokens, 0, 2 * width), (grads, 2 * width, width)):
            step = size if size <= 512 else size // 2

            def column(i, carry):
                factor = acts[:, pl.ds(pl.multiple_of(spot + first + i * step, 128), step)]
                part = over_rows(source[...].reshape(4 * rows, depth), factor)
                where = pl.ds(pl.multiple_of(first + i * step, 128), step)
                weight[..., where] = part.astype(BF16).reshape(
                    weight.shape[:-1] + (step,)
                )
                return carry

            lax.fori_loop(0, size // step, column, 0)

    def lift(index):
        hear(returned[index][0])
        add_into((back_sum, out_sum)[index].at[2], slots[3 * index + 2])
        begin(returned[index][1])

    def returned_rows(index, start):
        total = (back_sum, out_sum)[index]
        i = start // tile
        found = total[0, i].reshape(tile, depth).astype(F32)
        for slot in slots[3 * index : 3 * index + 2]:
            found += slot[i].reshape(tile, depth).astype(F32)
        return found

    def note(row, values):
        total = jnp.sum(values, axis=0, keepdims=True)
        if ("row", row) in begun:
            total += small[row : row + 1]
        small[row : row + 1] = total
        begun.add(("row", row))

    def turn(index):
        start = tile * index
        where = slice(start, start + tile)
        part = returned_rows(0, start)
        total = middle[where]
        scale = lax.rsqrt(mean_of(total * total) + epsilon)
        hat = total * scale
        note(4, part * hat)
        scaled = part * vectors_ref[4:5]
        spot = slice(3 * rows + start, 3 * rows + start + tile)
        grad = acts[spot, :depth].astype(F32) + scale * (
            scaled - hat * mean_of(scaled * hat)
        )
        middle[where] = grad
        acts[spot, :depth] = (valid_rows(start, tile) * grad).astype(BF16)

    def unmix(index):
        start = tile * index
        spot = slice(rows + start, rows + start + tile)
        weight = grads[1].reshape(depth, depth)
        gated_grad = by_rows(
            acts[3 * rows + start : 3 * rows + start + tile, :depth], weight
        )
        c_part = acts[spot, :depth].astype(F32)
        conv = conv_rows(start)
        back_sum[3, index] = (c_part * conv).astype(BF16).reshape(tokens.shape[2:])
        acts[spot, :depth] = (gated_grad * conv).astype(BF16)
        conv_grad = gated_grad * c_part
        middle[start : start + tile] = conv_grad
        for tap in range(3):
            first = start + 6 + tap
            note(1 + tap, conv_grad * product[first : first + tile])

    def unconv(index):
        start = tile * index
        grad = 0.0
        for tap in range(3):
            first = start + 2 - tap
            grad += vectors_ref[1 + tap : 2 + tap] * middle[first : first + tile]
        b_spot = slice(start, start + tile)
        v_spot = slice(2 * rows + start, 2 * rows + start + tile)
        b_part = acts[b_spot, :depth].astype(F32)
        v_part = acts[v_spot, :depth].astype(F32)
        acts[b_spot, :depth] = (grad * v_part).astype(BF16)
        acts[v_spot, :depth] = (grad * b_part).astype(BF16)

    def project_back(index):
        start = tile * index
        where = slice(start, start + tile)
        part = 0.0
        for j in range(3):
            spot = slice(rows * j + start, rows * j + start + tile)
            part += by_rows(acts[spot, :depth], blocks[j][...].reshape(depth, depth))
        x = high_x[index].reshape(tile, depth).astype(F32)
        scale = lax.rsqrt(mean_of(x * x) + epsilon)
        hat = x * scale
        note(0, part * hat)
        scaled = part * vectors_ref[0:1]
        middle[where] = middle[where] + scale * (scaled - hat * mean_of(scaled * hat))

    def weigh_mixer(j):
        if j >= 2:
            stores[j - 2].wait()
        wide = 2 * tile
        if j >= 2:
            first = rows * (j // 2 - 1)
            left = back_sum[2].reshape(rows, depth)
        else:
            first = 3 * rows
            left = back_sum[3].reshape(rows, depth)
        start = wide * (j % 2)
        part = over_rows(left, acts[first : first + rows, start : start + wide])
        staging[j % 2][...] = part.astype(BF16)
        stores[j].start()

    def close_result():
        for index in range(2):
            start = tile * index
            total = product[8 + start : 8 + start + tile] + valid_rows(
                start, tile
            ) * returned_rows(1, start)
            back_sum[1, index] = total.astype(BF16).reshape(tokens.shape[2:])
        save_result.start()

    def own(number):
        width = PARTS[number]
        for side, target in enumerate((gate_grad, up_grad, down_grad)):
            spot = pl.ds(side * width, width)
            mine = pl.multiple_of(place.c * quarter + offsets[number], 128)
            twin = pl.multiple_of((1 - place.c) * quarter + offsets[number], 128)
            target[:, pl.ds(mine, width)] = weights[number][
                place.z, place.y, place.c, :, spot
            ]
            target[:, pl.ds(twin, width)] = edges[number][:, spot]

    def work_on(needs, action, *args):
        return plan.add(needs, action, *args, busy=True)

    start = plan.add([], open_all)
    for part in mixers:
        plan.add([start], part.along, 0)
        plan.add([start], part.depart, 0)
    for twin in twins:
        plan.add([start], begin, *twin)
    cleared = plan.add([start], clear)
    masked = plan.add([start], load_grad.wait)
    masked = work_on([masked], mask_grads)
    plan.add([masked], begin, *[group[0] for group in shared_grads])
    early = [plan.add([masked], begin, group[1]) for group in shared_grads[:EARLY]]
    norm = plan.add([start], load_x[0].wait)
    norm = work_on([norm], first_norm, low_x, out_sum.at[0])
    filled = [plan.add([start], done, *copies) for copies in fills]
    arrived = [
        plan.add([filled[number]], hear, *twins[number]) for number in range(len(PARTS))
    ]

    gone, whole, passed = [], {}, []
    for number, part in enumerate(mixers):
        last = {(0, 0): start}
        for distance in range(1, DEPTH):
            step = plan.add([start], part.along, distance)
            last[0, distance] = plan.add([step], part.depart, distance)
            passed += [step] * (distance == Z_GATE)
        for stage in range(3):
            for distance in range(DEPTH):
                last[stage + 1, distance] = plan.add(
                    [last[stage, distance]], part.across, stage, distance
                )
        gone += [last[stage, d] for stage in (0, 1) for d in range(DEPTH)]
        whole[MIXER[number][0]] = list(last.values())

    ready = {}
    z_gate, y_gate = [start] + passed, list(gone)
    pair_opening = passed if PAIR_EARLY else gone
    pair_gate = {}
    for number in PAIRS:
        pair_gate[number] = [plan.add([arrived[number]] + pair_opening, gathers[number].begin)]
    for number in ORDER:
        part = gathers[number]
        opening = part.join if KINDS[number] == "y" else functools.partial(part.along, 0)
        found = [plan.add([arrived[number]] + z_gate + pair_gate.get(number, []), opening)]
        for distance in range(1, DEPTH):
            found.append(plan.add(found[-1:], part.along, distance))
        z_gate = found[1:2]
        if KINDS[number] == "z":
            sends = [
                plan.add([found[distance]] + y_gate, part.depart, distance)
                for distance in range(DEPTH)
            ]
            y_gate = sends[2:3]
            last_sends = sends
            found += sends
            found += [
                plan.add([sends[distance]], part.across, 0, distance)
                for distance in range(DEPTH)
            ]
        ready[number] = found

    y_gate = last_sends

    x_free = early + [
        plan.add(gone, begin, group[1]) for group in shared_grads[EARLY:]
    ]
    b_step = work_on(whole[0] + [norm], project, 0)
    v_step = work_on(whole[2] + [norm], project, 2)
    times = work_on([b_step, v_step], multiply)

    def send_edge():
        pl.when(has_next)(edge.start)

    def take_edge():
        pl.when(has_prev)(edge.wait_recv)

    def edge_sent():
        pl.when(has_next)(edge.wait_send)

    sent = plan.add([times], send_edge)
    c_step = work_on(whole[1] + [times], project, 1)
    saving = plan.add([c_step], begin, save_parts)
    late_mix = work_on(whole[3] + [c_step, sent], mix, 1)
    drained = plan.add([late_mix], lambda: [part.drain() for part in mixers])
    saved = plan.add([drained], begin, save_mixer)
    token_sends = {}
    token_sends[1] = plan.add([late_mix] + x_free, begin, *shared_tokens[1][1::-1])
    edge_in = plan.add([sent, cleared], take_edge)
    mixed = work_on([edge_in, late_mix], mix, 0)
    kept = plan.add([mixed, saved], lambda: (save_middle.start(), save_mixer.wait()))
    token_sends[0] = plan.add([kept, token_sends[1]], begin, *shared_tokens[0][1::-1])

    grads_x, tokens_x = [], []

    def pass_grads(group):
        hear(group[1])
        begin(group[2])

    for step, group in zip(x_free, shared_grads):
        grads_x.append(plan.add([step], pass_grads, group))
    for h in (1, 0):
        group = shared_tokens[h]

        def pass_on(group=group):
            hear(group[1])
            begin(group[2])

        tokens_x.append(plan.add([token_sends[h]], pass_on))
    near = plan.add(
        [token_sends[0], masked],
        hear,
        *[group[0] for group in shared_grads + shared_tokens],
    )
    far = plan.add(
        tokens_x + grads_x, hear, *[group[2] for group in shared_grads + shared_tokens]
    )
    def flush():
        done(save_parts, save_middle)
        edge_sent()

    flushed = plan.add([kept, mixed, saving], flush)
    own_side, other_side = [near, flushed], [near, far, flushed]
    blocks_done = {}
    weighed = {}
    reduced = {}
    previous = []

    def reduce_steps(number, needs):
        part = reduces[number]
        if GRAD_KINDS[number] == "y":
            chain = list(needs)
            steps = []
            for distance in (3, 2, 1, 0):
                chain = [plan.add(chain, part.along, distance)]
                steps += chain
            chain = [plan.add(chain, lambda: part.final().start())]
            steps.append(plan.add(chain, part.finish))
            return steps
        steps = []
        opened = {
            distance: plan.add(needs + y_gate, part.begin, distance)
            for distance in (3, 2, 1, 0)
        }
        chain = []
        for distance in (3, 2, 1, 0):
            step = plan.add([opened[distance]], part.across, 0, distance)
            chain = [plan.add([step] + chain, part.along, distance)]
            steps += [step] + chain
        return steps

    def drain_and_weigh(number, needs):
        drain = plan.add(needs, gathers[number].drain)
        weighed[number] = work_on([drain], weigh, number)
        reduced[number] = reduce_steps(number, [weighed[number]])

    def columns_of(number):
        return set(range(SPOTS[number], SPOTS[number] + 3 * PARTS[number], 128))

    def run_block(number, pair):
        needs = [
            weighed[other]
            for other in ORDER[: ORDER.index(number)]
            if columns_of(other) & columns_of(number)
        ]
        blocks_done[number, pair] = work_on(
            ready[number] + (other_side if pair else own_side) + needs, block, number, pair
        )

    def finish_part(number):
        drain_and_weigh(number, [blocks_done[number, 0], blocks_done[number, 1]])

    first, second, third, fourth = ORDER
    for number in (first, second):
        if not columns_of(first) & columns_of(second):
            run_block(number, 0)
    for number in (first, second):
        if columns_of(first) & columns_of(second):
            run_block(number, 0)
        run_block(number, 1)
        finish_part(number)
    run_block(third, 1)
    run_block(fourth, 1)
    last_far = [blocks_done[third, 1], blocks_done[fourth, 1]]
    back_up = plan.add(last_far, begin, returned[0][0])
    out_up = plan.add([back_up], begin, returned[1][0])
    back_over = plan.add([back_up], lift, 0)
    run_block(third, 0)
    run_block(fourth, 0)
    near_done = [blocks_done[third, 0], blocks_done[fourth, 0]]
    back_near = plan.add(near_done + [back_over], begin, returned[0][2])
    out_over = plan.add([out_up, back_over], lift, 1)
    out_near = plan.add([back_near, out_over], begin, returned[1][2])
    finish_part(third)
    finish_part(fourth)

    def sent_tokens():
        for group in shared_grads + shared_tokens:
            for copy in group:
                copy.wait_send()

    freed = plan.add([weighed[number] for number in ORDER], sent_tokens)
    loads = plan.add(
        [freed], begin, load_parts, load_grad_rows, *load_mixer
    )
    back_in = plan.add([back_near], hear, returned[0][1], returned[0][2])
    loaded = plan.add([loads], done, load_parts, load_grad_rows, *load_mixer)
    turned = [work_on([back_in, loaded], turn, index) for index in range(2)]

    def free_sums():
        done(save_grad)
        for copy in returned[0]:
            copy.wait_send()
        load_x[1].start()

    freed = plan.add(turned, save_grad.start)
    freed = plan.add([freed], free_sums)
    unmixed = [work_on([freed], unmix, index) for index in range(2)]
    again = plan.add([freed], load_x[1].wait)
    again = work_on([again], first_norm, high_x, back_sum.at[2])

    def send_back():
        pl.when(has_prev)(back_edge.start)

    def take_back():
        pl.when(has_next)(back_edge.wait_recv)

    def back_sent():
        pl.when(has_prev)(back_edge.wait_send)

    back_edge_sent = plan.add([unmixed[0]], send_back)
    weigh_steps = [work_on(unmixed, weigh_mixer, 0)]
    weigh_steps.append(work_on(unmixed + weigh_steps, weigh_mixer, 1))
    low = work_on([unmixed[1], back_edge_sent], unconv, 0)
    taken = plan.add([back_edge_sent], take_back)
    high = work_on([taken, low], unconv, 1)
    fetched = plan.add([low, high] + [edge_in], begin, load_middle)
    for j in range(2, 8):
        weigh_steps.append(work_on([again, low, high, weigh_steps[-1]], weigh_mixer, j))
    revived = plan.add([low, high], lambda: (back_sent(), load_back.start()))
    revived = plan.add([revived, weigh_steps[-1]], load_back.wait)
    projected = [work_on([revived], project_back, index) for index in range(2)]
    stored = plan.add(projected, begin, save_inputs)
    def finish_result():
        load_middle.wait()
        close_result()

    out_in = plan.add([out_near, fetched], hear, returned[1][1], returned[1][2])
    finished = work_on([out_in, fetched] + weigh_steps, finish_result)

    finals = []
    for number in ORDER:
        trade = plan.add(reduced[number], begin, trades[number])
        heard = plan.add([trade], hear, trades[number])
        finals.append(work_on([heard], own, number))

    def close():
        small[pl.ds(5, 3)] = jnp.zeros((3, depth), F32)
        done(save_inputs, save_result, *stores[6:8])
        for reduce in reduces:
            reduce.drain()
        for group in returned[1:] + twins + [trades]:
            for copy in group:
                copy.wait_send()

    plan.add(finals + weigh_steps + projected + [stored, finished], close)
    plan.run(STEPS or list(range(len(plan.steps))))


def layer(lengths, inputs, cotangent, vectors, shards):
    rows, depth = inputs.shape
    ffn_columns = shards[2].shape[1]
    vmem = pl.BlockSpec(memory_space=pltpu.VMEM)
    hbm = pl.BlockSpec(memory_space=pl.ANY)
    shape = jax.ShapeDtypeStruct
    blocks = (DEPTH, 2, 2, 2, depth // (8 * DEPTH))
    half = (2, 2, 2, 2, rows // 16, depth)
    out_shape = [
        shape(blocks + (4 * depth,), BF16),
        shape((3 * rows, depth), BF16),
        shape((rows, depth), F32),
        shape((depth, 4 * depth), BF16),
        shape((8, depth), F32),
        shape(half, BF16),
        shape((rows, depth), F32),
    ] + [shape((64, ffn_columns), BF16)] * 3
    pair = (2, 64)
    widths = [3 * w for w in PARTS]

    def slots(lead, width, kind):
        if kind == "y":
            return (lead, 2) if lead > DEPTH else ()
        return (lead,)

    token = (2, 4, 2, 2, 2, 32, depth)
    total = (4, 2, 2, 2, 2, 32, depth)
    scratch = (
        [pltpu.VMEM(blocks + (4 * depth,), BF16)]
        + [pltpu.VMEM((DEPTH, 2) + pair + (w,), BF16) for w in widths]
        + [
            pltpu.VMEM((rows + 8, depth), F32),
            pltpu.VMEM((rows + 8, depth), F32),
        ]
        + [pltpu.VMEM(token, BF16)] * 2
        + [
            pltpu.VMEM(slots(lead, w, kind) + pair + (w,), BF16)
            for lead in (DEPTH, DEPTH + 1)
            for w, kind in zip(widths, GRAD_KINDS)
        ]
        + [pltpu.VMEM((64, w), BF16) for w in widths]
        + [pltpu.VMEM((4 * rows, ACTS), BF16)]
        + [pltpu.VMEM(total, BF16)] * 2
        + [
            pltpu.SemaphoreType.DMA((40,)),
            pltpu.SemaphoreType.DMA((240,)),
            pltpu.SemaphoreType.DMA((240,)),
        ]
    )
    smem = pl.BlockSpec(memory_space=pltpu.SMEM)
    return pl.pallas_call(
        layer_kernel,
        out_shape=out_shape,
        in_specs=[smem] + [hbm] * 3 + [vmem] + [hbm] * 5,
        out_specs=[hbm] * 4 + [vmem, hbm, hbm] + [vmem] * 3,
        scratch_shapes=scratch,
        compiler_params=pltpu.CompilerParams(
            collective_id=0, has_side_effects=True, vmem_limit_bytes=63 * 2**20
        ),
    )(
        lengths,
        inputs.reshape(half),
        cotangent.reshape(half),
        cotangent,
        vectors,
        *shards
    )


def reduce_kernel(grad_ref, small_ref, in_grad, out_grad, sum_ref, work, small, *rest):
    slots, (load_sem, send, recv) = rest[:-3], rest[-3:]
    place = Place()
    links = Links(place, send, recv)
    plan = Plan()
    depth = in_grad.shape[1] // 3
    parts = []
    remaining = list(slots)
    for j, before, after in MIXER_GRADS:
        where = pl.ds(depth * j, depth)
        count = len(before) + 1 + len(after)
        mine, remaining = remaining[:count], remaining[count:]
        parts.append(
            Reduce(
                links,
                lambda z, y, c, x, where=where: work.at[z, y, x, :, where],
                before,
                mine[: len(before)] + mine[len(before) + 1 :],
                mine[len(before)],
                after,
                lambda z, y, c, x, where=where: grad_ref.at[z, y, c, x, :, where],
            )
        )
    loads = [
        pltpu.make_async_copy(
            grad_ref.at[:, :, place.c, :, :, pl.ds(depth * j, depth)],
            work.at[:, :, :, :, pl.ds(depth * j, depth)],
            load_sem.at[number],
        )
        for number, (j, _, _) in enumerate(MIXER_GRADS)
    ]
    ring = ("c", "x", "y", "pair", "far")
    first = links.take(len(ring))
    rounds = [
        links.copy(small.at[i], small.at[len(ring) + 1 + i], first + i, name)
        for i, name in enumerate(ring)
    ]

    def open_all():
        for load in loads:
            load.start()
        place.greet(["c", "y", "x", "up", "down", "far"])
        small[0] = small_ref[...]

    start = plan.add([], open_all)
    opened = [
        [plan.add([start], part.begin, distance) for distance in (3, 2, 1, 0)]
        for part in parts
    ]
    ends = []
    for part, load, begun in zip(parts, loads, opened):
        loaded = plan.add([start], load.wait)
        line = []
        for number, distance in enumerate((3, 2, 1, 0)):
            step = plan.add([loaded, begun[number]], part.across, 0, distance)
            for stage in range(1, part.before):
                step = plan.add([step], part.across, stage, distance)
            line = [plan.add([step] + line, part.along, distance)]
        for stage in range(part.before, len(part.stages)):
            line = [plan.add(line, part.late_start, stage)]
            line = [plan.add(line, part.late_take, stage)]
        ends += line

    def add_round(number):
        rounds[number].wait_recv()
        small[number + 1] = small[number] + small[len(ring) + 1 + number]

    step = plan.add(sum(opened, []), rounds[0].start)
    for number in range(len(ring)):
        step = plan.add([step], add_round, number)
        if number + 1 < len(ring):
            step = plan.add([step], rounds[number + 1].start)

    def close():
        sum_ref[...] = small[len(ring)]
        own = work[place.z, place.y, place.x].astype(F32)
        in_grad[...] = own[:, : 3 * depth]
        out_grad[...] = own[:, 3 * depth :]
        for part in parts:
            part.drain()
        for copy in rounds:
            copy.wait_send()

    plan.add(ends + [step], close)
    plan.run(LAST_STEPS or list(range(len(plan.steps))))


def reduce_all(grad, small):
    columns = grad.shape[-1]
    depth = columns // 4
    block = (grad.shape[-2], depth)
    slots = []
    for _, before, after in MIXER_GRADS:
        left = len(before) + len(after)
        for _ in before:
            left -= 1
            slots.append((DEPTH,) + (2,) * left + block)
        slots.append((DEPTH + 1,) + (2,) * left + block)
        for _ in after:
            left -= 1
            slots.append((2,) * left + block)
    vmem = pl.BlockSpec(memory_space=pltpu.VMEM)
    hbm = pl.BlockSpec(memory_space=pl.ANY)
    return pl.pallas_call(
        reduce_kernel,
        out_shape=[
            jax.ShapeDtypeStruct((block[0], 3 * depth), F32),
            jax.ShapeDtypeStruct((block[0], depth), F32),
            jax.ShapeDtypeStruct(small.shape, F32),
        ],
        in_specs=[hbm, vmem],
        out_specs=[vmem] * 3,
        scratch_shapes=[
            pltpu.VMEM((DEPTH, 2, 2) + block[:1] + (columns,), BF16),
            pltpu.VMEM((11,) + small.shape, F32),
        ]
        + [pltpu.VMEM(slot, BF16) for slot in slots]
        + [
            pltpu.SemaphoreType.DMA((len(MIXER_GRADS),)),
            pltpu.SemaphoreType.DMA((96,)),
            pltpu.SemaphoreType.DMA((96,)),
        ],
        compiler_params=pltpu.CompilerParams(
            collective_id=2, has_side_effects=True, vmem_limit_bytes=58 * 2**20
        ),
    )(grad, small)


def shifted(block, axis, distance):
    devices = range(lax.axis_size(axis))
    route = [(i - distance, i) for i in devices if i - distance in devices]
    return lax.ppermute(block, axis, route)


def mixer_forward(inputs, lengths, norm_one_gain, conv_weight, norm_two_gain, in_all, out_all):
    tok_rows, feat_width = inputs.shape[1:]
    kept = {}
    x_float = inputs[0].astype(F32)
    kernel = conv_weight.astype(F32)
    position = lax.axis_index("seq") * tok_rows + lax.iota(jnp.int32, tok_rows)
    valid_mask = (position < lengths[0]).astype(F32)[:, None]
    scale_one = lax.rsqrt(jnp.mean(x_float * x_float, axis=1, keepdims=True) + epsilon)
    hat_one = x_float * scale_one
    normed_one = (hat_one * norm_one_gain.astype(F32)).astype(BF16)
    projected = rounded_dot(normed_one, in_all)
    b_part = projected[:, :feat_width]
    c_part = projected[:, feat_width : 2 * feat_width]
    v_part = projected[:, 2 * feat_width :]
    product = (b_part * v_part).astype(BF16)
    carried = shifted(product[tok_rows - 2 :], "seq", 1)
    extended = jnp.concatenate([carried, product], axis=0).astype(F32)
    conv_out = (
        kernel[0] * extended[:tok_rows]
        + kernel[1] * extended[1 : tok_rows + 1]
        + kernel[2] * extended[2:]
    )
    gated_mix = (c_part * conv_out).astype(BF16)
    mixer_out = rounded_dot(gated_mix, out_all)
    middle = x_float + valid_mask * mixer_out
    scale_two = lax.rsqrt(jnp.mean(middle * middle, axis=1, keepdims=True) + epsilon)
    hat_two = middle * scale_two
    normed_two = (hat_two * norm_two_gain.astype(F32)).astype(BF16)
    kept.update(locals())
    return kept


def mixer_backward(kept, grad_out, normed_part, norm_one_gain, norm_two_gain, in_all, out_all):
    tok_rows, feat_width = grad_out.shape
    kernel = kept["kernel"]
    extended, conv_out = kept["extended"], kept["conv_out"]
    hat_one, hat_two = kept["hat_one"], kept["hat_two"]
    grad_gain_two = jnp.sum(normed_part * hat_two, axis=0)
    scaled_two = normed_part * norm_two_gain.astype(F32)
    grad_middle = grad_out + kept["scale_two"] * (
        scaled_two - hat_two * jnp.mean(scaled_two * hat_two, axis=1, keepdims=True)
    )
    grad_mix = (kept["valid_mask"] * grad_middle).astype(BF16)
    grad_out_w = over_rows(kept["gated_mix"], grad_mix)
    grad_gated = by_rows(grad_mix, out_all)
    grad_c = grad_gated * conv_out
    grad_conv_in = grad_gated * kept["c_part"]
    grad_kernel = jnp.stack(
        [
            jnp.sum(grad_conv_in * extended[:tok_rows], axis=0),
            jnp.sum(grad_conv_in * extended[1 : tok_rows + 1], axis=0),
            jnp.sum(grad_conv_in * extended[2:], axis=0),
        ]
    )
    padded_grad = jnp.pad(grad_conv_in, ((2, 2), (0, 0)))
    grad_extended = (
        kernel[0] * padded_grad[2 : tok_rows + 4]
        + kernel[1] * padded_grad[1 : tok_rows + 3]
        + kernel[2] * padded_grad[: tok_rows + 2]
    )
    returned = shifted(grad_extended[:2], "seq", -1)
    grad_product = grad_extended[2:] + jnp.concatenate(
        [jnp.zeros((tok_rows - 2, feat_width), F32), returned], axis=0
    )
    grad_projected = jnp.concatenate(
        [grad_product * kept["v_part"], grad_c, grad_product * kept["b_part"]], axis=1
    ).astype(BF16)
    grad_in_w = over_rows(kept["normed_one"], grad_projected)
    grad_normed_one = by_rows(grad_projected, in_all)
    grad_gain_one = jnp.sum(grad_normed_one * hat_one, axis=0)
    scaled_one = grad_normed_one * norm_one_gain.astype(F32)
    grad_inputs = grad_middle + kept["scale_one"] * (
        scaled_one - hat_one * jnp.mean(scaled_one * hat_one, axis=1, keepdims=True)
    )
    return grad_inputs, grad_in_w, grad_out_w, grad_gain_one, grad_kernel, grad_gain_two


def in_blocks(
    inputs,
    lengths,
    norm_one_gain,
    w_in,
    conv_weight,
    w_out,
    norm_two_gain,
    w_gate,
    w_up,
    w_down,
    cotangent,
):
    width = inputs.shape[2]
    vectors = jnp.concatenate([norm_one_gain[None], conv_weight, norm_two_gain[None]])
    found = layer(
        lengths,
        inputs[0],
        cotangent[0],
        vectors.astype(F32),
        (w_in, w_out, w_gate, w_up, w_down.T),
    )
    mixer_grad, small, result, grad_inputs, gate, up, down = found[3:]
    in_grad, out_grad, total = reduce_all(
        mixer_grad.reshape(DEPTH, 2, 2, 2, 32, 4 * width), small
    )
    return (
        result.reshape(inputs.shape),
        grad_inputs[None],
        total[0],
        in_grad,
        total[1:4],
        out_grad,
        total[4],
        gate.astype(F32),
        up.astype(F32),
        down.T.astype(F32),
    )


def anywhere(
    inputs,
    lengths,
    norm_one_gain,
    w_in,
    conv_weight,
    w_out,
    norm_two_gain,
    w_gate,
    w_up,
    w_down,
    cotangent,
):
    both = ("seq", "batch")
    in_all = lax.all_gather(w_in, both, axis=0, tiled=True)
    out_all = lax.all_gather(w_out, both, axis=0, tiled=True)
    gate_use, up_use = (
        lax.all_gather(
            lax.all_gather(w, "seq", axis=0, tiled=True), "batch", axis=1, tiled=True
        )
        for w in (w_gate, w_up)
    )
    down_use = lax.all_gather(
        lax.all_gather(w_down, "seq", axis=1, tiled=True), "batch", axis=0, tiled=True
    )
    kept = mixer_forward(
        inputs, lengths, norm_one_gain, conv_weight, norm_two_gain, in_all, out_all
    )
    rows_norm = kept["normed_two"]
    grad_out = cotangent[0].astype(F32)
    rows_grad = (kept["valid_mask"] * grad_out).astype(BF16)
    gate_val = rounded_dot(rows_norm, gate_use)
    up_val = rounded_dot(rows_norm, up_use)
    hidden = (jax.nn.silu(gate_val) * up_val).astype(BF16)
    ffn_out = rounded_dot(hidden, down_use)
    result = (kept["middle"] + kept["valid_mask"] * ffn_out).astype(BF16)
    grad_down = over_rows(hidden, rows_grad)
    grad_hidden = by_rows(rows_grad, down_use)
    sigmoid_gate = jax.nn.sigmoid(gate_val)
    slope_gate = sigmoid_gate * (1.0 + gate_val * (1.0 - sigmoid_gate))
    grad_gate = (grad_hidden * up_val * slope_gate).astype(BF16)
    grad_up = (grad_hidden * gate_val * sigmoid_gate).astype(BF16)
    grad_gate_w = over_rows(rows_norm, grad_gate)
    grad_up_w = over_rows(rows_norm, grad_up)
    normed_part = by_rows(grad_gate, gate_use) + by_rows(grad_up, up_use)

    def owned(grad, axis):
        half = lax.psum_scatter(
            grad.astype(BF16), "batch", scatter_dimension=axis, tiled=True
        ).astype(F32)
        return lax.psum_scatter(half, "seq", scatter_dimension=1 - axis, tiled=True)

    shards = owned(grad_gate_w, 1), owned(grad_up_w, 1), owned(grad_down, 0)
    grad_inputs, grad_in_w, grad_out_w, gain_one, taps, gain_two = mixer_backward(
        kept, grad_out, normed_part, norm_one_gain, norm_two_gain, in_all, out_all
    )
    shard_in, shard_out = (
        lax.psum_scatter(grad, both, scatter_dimension=0, tiled=True)
        for grad in (grad_in_w, grad_out_w)
    )
    total_one, total_two, total_kernel = lax.psum((gain_one, gain_two, taps), both)
    return (
        result[None],
        grad_inputs[None],
        total_one,
        shard_in,
        total_kernel,
        shard_out,
        total_two,
    ) + shards


def solution(mesh):
    in_specs = (
        P("batch", "seq", None),
        P("batch"),
        P(),
        P(("seq", "batch"), None),
        P(),
        P(("seq", "batch"), None),
        P(),
        P("seq", "batch"),
        P("seq", "batch"),
        P("batch", "seq"),
        P("batch", "seq", None),
    )
    out_specs = (
        P("batch", "seq", None),
        P("batch", "seq", None),
        P(),
        P(("seq", "batch"), None),
        P(),
        P(("seq", "batch"), None),
        P(),
        P("seq", "batch"),
        P("seq", "batch"),
        P("batch", "seq"),
    )
    by_blocks = mesh.shape["seq"] == 4 * DEPTH and mesh.shape["batch"] == 2
    return jax.shard_map(
        in_blocks if by_blocks else anywhere,
        mesh=mesh,
        in_specs=in_specs,
        out_specs=out_specs,
        check_vma=False,
    )
```

```python
import functools

import jax
import jax.numpy as jnp
from jax import lax
from jax.experimental import pallas as pl
from jax.experimental.pallas import tpu as pltpu
from jax.sharding import PartitionSpec as P

epsilon = 1e-05
MESH = pl.DeviceIdType.MESH
F32, BF16 = jnp.float32, jnp.bfloat16
DEPTH = 4
PARTS = [384, 256, 256, 256]
KINDS = ("z", "y", "z", "z")
GRAD_KINDS = ("y", "z", "z", "z")
ORDER = (0, 1, 2, 3)
SPOTS = [0, 1152, 0, 768]
PAIRS = tuple(k for k, kind in enumerate(KINDS) if kind == "y")
PAIR_EARLY = 1
MIXER = (
    (2, ["x", "y", "c"]),
    (0, ["y", "x", "c"]),
    (1, ["y", "x", "c"]),
    (3, ["x", "y", "c"]),
)
MIXER_GRADS = (
    (0, ["c", "x", "y"], []),
    (2, ["c", "y", "x"], []),
    (3, ["c"], ["x", "y"]),
    (1, ["c", "y", "x"], []),
)
LAST_STEPS = (
    0, 15, 17, 1, 64, 34, 51, 9, 7, 13, 11, 5, 73, 18, 52, 53, 2, 12, 3, 35, 6, 10, 22,
    65, 14, 8, 54, 4, 19, 16, 43, 74, 81, 58, 55, 39, 36, 82, 83, 66, 26, 37, 84, 20,
    21, 69, 38, 67, 56, 68, 85, 30, 23, 57, 77, 40, 75, 70, 27, 86, 87, 47, 31, 24, 44,
    25, 71, 41, 72, 42, 59, 60, 78, 28, 29, 45, 88, 76, 48, 46, 89, 61, 62, 32, 79, 33,
    80, 49, 50, 63, 90, 91,
)
Z_GATE = 1
ACTS = 1920
EARLY = 1
STEPS = (
    0, 8, 14, 7, 15, 17, 4, 10, 6, 3, 21, 5, 82, 88, 9, 83, 1, 64, 84, 2, 20, 65, 85,
    28, 29, 52, 25, 46, 47, 66, 70, 24, 100, 67, 12, 34, 30, 101, 48, 35, 49, 86, 31,
    87, 13, 53, 91, 18, 72, 56, 50, 102, 32, 68, 22, 51, 69, 113, 89, 33, 11, 54, 95,
    71, 73, 36, 16, 37, 90, 57, 93, 55, 103, 141, 58, 77, 38, 99, 39, 42, 40, 74, 76,
    142, 62, 41, 97, 61, 44, 114, 105, 59, 19, 158, 94, 80, 60, 92, 23, 45, 143, 81, 96,
    26, 75, 104, 107, 78, 43, 63, 98, 144, 159, 108, 145, 79, 109, 146, 147, 148, 149,
    150, 117, 153, 106, 27, 121, 151, 154, 115, 160, 161, 152, 155, 118, 156, 157, 166,
    111, 129, 164, 122, 112, 110, 116, 167, 119, 162, 123, 133, 168, 130, 163, 120, 124,
    126, 134, 165, 169, 131, 170, 171, 172, 135, 178, 132, 179, 125, 136, 127, 137, 180,
    183, 139, 128, 138, 193, 173, 181, 140, 194, 195, 196, 184, 185, 197, 198, 182, 186,
    203, 204, 206, 207, 174, 199, 217, 205, 218, 231, 187, 201, 188, 200, 219, 191, 209,
    208, 220, 210, 232, 202, 221, 211, 213, 234, 223, 224, 189, 233, 236, 235, 222, 237,
    238, 241, 175, 239, 243, 212, 240, 190, 246, 242, 247, 248, 244, 225, 245, 250, 215,
    176, 249, 226, 251, 227, 252, 214, 253, 192, 256, 266, 254, 255, 267, 261, 228, 257,
    259, 177, 229, 263, 258, 268, 216, 269, 264, 260, 265, 230, 272, 262, 270, 271, 273,
    274, 275,
)


def over_rows(left, right):
    return lax.dot_general(
        left, right, (((0,), (0,)), ((), ())), preferred_element_type=F32
    )


def by_rows(left, right):
    return lax.dot_general(
        left, right, (((1,), (1,)), ((), ())), preferred_element_type=F32
    )


def dot(left, right):
    return jnp.dot(left, right, preferred_element_type=F32)


def rounded_dot(left, right):
    return dot(left, right).astype(BF16).astype(F32)


class Place:
    def __init__(self):
        self.s = lax.axis_index("seq")
        self.x = lax.axis_index("batch")
        self.z = self.s // 4
        self.y = (self.s // 2) % 2
        self.c = self.s % 2
        self.last = lax.axis_size("seq") - 1
        self.own = {"y": self.y, "c": self.c, "x": self.x}
        self.device = {
            "c": (self.s + 1 - 2 * self.c, self.x),
            "y": (self.s + 2 - 4 * self.y, self.x),
            "x": (self.s, 1 - self.x),
            "up": (self.s + 4, self.x),
            "down": (self.s - 4, self.x),
            "next": (self.s + 1, self.x),
            "prev": (self.s - 1, self.x),
            "pair": (self.s + 4 - 8 * (self.z % 2), self.x),
            "far": (self.s + 8 - 16 * (self.z // 2), self.x),
        }

    def greet(self, names):
        barrier = pltpu.get_barrier_semaphore()
        ends = {
            "up": self.z < DEPTH - 1,
            "down": self.z > 0,
            "next": self.s < self.last,
            "prev": self.s > 0,
        }

        def signal(name):
            pl.semaphore_signal(
                barrier, inc=1, device_id=self.device[name], device_id_type=MESH
            )

        expected = 0
        for name in names:
            if name in ends:
                pl.when(ends[name])(functools.partial(signal, name))
                expected = expected + ends[name].astype(jnp.int32)
            else:
                signal(name)
                expected = expected + 1
        pl.semaphore_wait(barrier, expected)


class Links:
    def __init__(self, place, send, recv):
        self.place, self.send, self.recv = place, send, recv
        self.used = 0

    def take(self, count):
        first = self.used
        self.used += count
        assert self.used <= self.send.shape[0]
        return first

    def copy(self, source, target, index, name):
        return pltpu.make_async_remote_copy(
            src_ref=source,
            dst_ref=target,
            send_sem=self.send.at[index],
            recv_sem=self.recv.at[index],
            device_id=self.place.device[name],
            device_id_type=MESH,
        )


def way(direction):
    return (1 - direction) // 2


class Line:
    def take_line(self):
        self.first = self.links.take(2 * DEPTH)

    def hop(self, source, target, direction, level):
        place = self.place
        index = self.first + DEPTH * way(direction) + level
        return pltpu.make_async_remote_copy(
            src_ref=source,
            dst_ref=target,
            send_sem=self.links.send.at[index],
            recv_sem=self.links.recv.at[index],
            device_id=(place.s + 4 * direction, place.x),
            device_id_type=MESH,
        )

    def levels(self, distance, action):
        z = self.place.z
        if distance == 0:
            action(z, None)
            return

        def side(i, carry):
            direction = 1 - 2 * i
            level = z - direction * distance

            @pl.when((level >= 0) & (level < DEPTH))
            def _():
                action(level, direction)

            return carry

        lax.fori_loop(0, 2, side, 0)

    def beyond(self, direction):
        further = self.place.z + direction
        return (further >= 0) & (further < DEPTH)


class Gather(Line):
    def __init__(self, links, view, stages):
        self.links, self.view, self.stages = links, view, stages
        self.place = links.place
        self.take_line()
        self.rows = {name: links.take(DEPTH) for name in stages}

    def block(self, stage, level, theirs=False):
        where = dict(self.place.own)
        if stage is not None:
            for name in self.stages[:stage]:
                where[name] = slice(None)
            if theirs:
                where[self.stages[stage]] = 1 - where[self.stages[stage]]
        return self.view(level, where["y"], where["c"], where["x"])

    def line(self, direction, level):
        ref = self.block(None, level)
        return self.hop(ref, ref, direction, level)

    def staged(self, stage, level, theirs=False):
        name = self.stages[stage]
        ref = self.block(stage, level, theirs)
        return self.links.copy(ref, ref, self.rows[name] + level, name)

    def along(self, distance):
        def hand_on(level, direction):
            if distance:
                self.line(direction, level).wait_recv()

            @pl.when(self.beyond(direction))
            def _():
                self.line(direction, level).start()

        if distance == 0:
            hand_on(self.place.z, 1)
            hand_on(self.place.z, -1)
        else:
            self.levels(distance, hand_on)

    def depart(self, distance):
        self.levels(distance, lambda level, _: self.staged(0, level).start())

    def across(self, stage, distance):
        def pass_on(level, _):
            self.staged(stage, level, True).wait_recv()
            if stage + 1 < len(self.stages):
                self.staged(stage + 1, level).start()

        self.levels(distance, pass_on)

    def drain_line(self):
        z = self.place.z

        def sent(level, carry):
            @pl.when((z >= level) & (z < DEPTH - 1))
            def _():
                self.line(1, level).wait_send()

            @pl.when((z <= level) & (z > 0))
            def _():
                self.line(-1, level).wait_send()

            return carry

        lax.fori_loop(0, DEPTH, sent, 0)

    def drain(self):
        self.drain_line()

        def sent(level, carry):
            for stage in range(len(self.stages)):
                self.staged(stage, level).wait_send()
            return carry

        lax.fori_loop(0, DEPTH, sent, 0)


class PairGather(Gather):
    def __init__(self, links, ref):
        super().__init__(links, lambda z, y, c, x: ref.at[z, y], ["y"])
        self.ref = ref

    def line(self, direction, level):
        ref = self.ref.at[level]
        return self.hop(ref, ref, direction, level)

    def begin(self):
        self.staged(0, self.place.z).start()

    def join(self):
        self.staged(0, self.place.z, True).wait_recv()
        self.along(0)

    def drain(self):
        self.staged(0, self.place.z).wait_send()
        self.drain_line()


def add_into(target, source):
    def add(i, carry):
        target[i] = (target[i].astype(F32) + source[i].astype(F32)).astype(BF16)
        return carry

    if len(target.shape) > 2:
        lax.fori_loop(0, target.shape[0], add, 0)
    else:
        add(Ellipsis, 0)


class Reduce(Line):
    def __init__(self, links, view, stages, slots, line_slots, after=(), source=None):
        self.links, self.view, self.stages = links, view, list(stages) + list(after)
        self.slots, self.line_slots = slots, line_slots
        self.source = source or view
        self.before = len(stages)
        self.place = links.place
        self.take_line()
        self.rows = {name: links.take(DEPTH) for name in stages}
        self.rows.update({name: links.take(1) for name in after})

    def block(self, stage, level, theirs=False):
        where = dict(self.place.own)
        for name in self.stages[stage + 1 :]:
            where[name] = slice(None)
        if theirs:
            where[self.stages[stage]] = 1 - where[self.stages[stage]]
        view = self.source if theirs and stage == 0 else self.view
        return view(level, where["y"], where["c"], where["x"])

    def staged(self, stage, level):
        name = self.stages[stage]
        late = stage >= self.before
        return self.links.copy(
            self.block(stage, level, True),
            self.slots[stage] if late else self.slots[stage].at[level],
            self.rows[name] + (0 if late else level),
            name,
        )

    def late_start(self, stage):
        self.staged(stage, self.place.z).start()

    def late_take(self, stage):
        z = self.place.z
        self.staged(stage, z).wait_recv()
        add_into(self.block(stage, z), self.slots[stage])

    def slot(self, direction, level):
        return self.line_slots.at[level + 1 - way(direction)]

    def line(self, direction, level):
        ref = self.block(self.before - 1, level)
        return self.hop(ref, self.slot(direction, level), direction, level)

    def begin(self, distance):
        self.levels(distance, lambda level, _: self.staged(0, level).start())

    def across(self, stage, distance):
        def take(level, _):
            self.staged(stage, level).wait_recv()
            add_into(self.block(stage, level), self.slots[stage].at[level])
            if stage + 1 < self.before:
                self.staged(stage + 1, level).start()

        self.levels(distance, take)

    def take(self, direction, level):
        self.line(direction, level).wait_recv()
        add_into(self.block(self.before - 1, level), self.slot(direction, level))

    def along(self, distance):
        if distance == 0:

            def side(i, carry):
                direction = 1 - 2 * i

                @pl.when(self.beyond(-direction))
                def _():
                    self.take(direction, self.place.z)

                return carry

            lax.fori_loop(0, 2, side, 0)
            return

        def send(level, back):
            @pl.when(self.beyond(back))
            def _():
                self.take(-back, level)

            self.line(-back, level).start()

        self.levels(distance, send)

    def drain_line(self):
        z = self.place.z

        def sent(level, carry):
            @pl.when(z > level)
            def _():
                self.line(-1, level).wait_send()

            @pl.when(z < level)
            def _():
                self.line(1, level).wait_send()

            return carry

        lax.fori_loop(0, DEPTH, sent, 0)

    def drain(self):
        self.drain_line()

        def sent(level, carry):
            for stage in range(self.before):
                self.staged(stage, level).wait_send()
            return carry

        lax.fori_loop(0, DEPTH, sent, 0)
        for stage in range(self.before, len(self.stages)):
            self.staged(stage, self.place.z).wait_send()


class PairReduce(Reduce):
    def __init__(self, links, ref, slot, line_slots):
        super().__init__(links, lambda z, y, c, x: ref.at[z, y], ["y"], None, line_slots)
        self.ref, self.last_slot = ref, slot

    def block(self, stage, level, theirs=False):
        return self.ref.at[level]

    def final(self):
        place = self.place
        return self.links.copy(
            self.ref.at[place.z, 1 - place.y], self.last_slot, self.rows["y"], "y"
        )

    def finish(self):
        self.final().wait_recv()
        add_into(self.ref.at[self.place.z, self.place.y], self.last_slot)

    def drain(self):
        self.drain_line()
        self.final().wait_send()


class Plan:
    def __init__(self):
        self.steps = []

    def add(self, needs, action, *args, busy=False):
        self.steps.append((tuple(needs), functools.partial(action, *args), busy))
        return len(self.steps) - 1

    def run(self, order):
        seen = set()
        assert sorted(order) == list(range(len(self.steps)))
        for index in order:
            needs, action, _ = self.steps[index]
            assert seen.issuperset(needs)
            action()
            seen.add(index)


def mean_of(values):
    return jnp.mean(values, axis=1, keepdims=True)


def layer_kernel(
    length_ref,
    x_ref,
    grad_ref,
    grad_rows_ref,
    vectors_ref,
    in_ref,
    out_ref,
    gate_ref,
    up_ref,
    down_ref,
    mixer_hbm,
    parts_hbm,
    middle_hbm,
    mixer_grad,
    small,
    result_ref,
    input_grad,
    gate_grad,
    up_grad,
    down_grad,
    wm,
    w0,
    w1,
    w2,
    w3,
    product,
    middle,
    tokens,
    grads,
    r0,
    r1,
    r2,
    r3,
    l0,
    l1,
    l2,
    l3,
    e0,
    e1,
    e2,
    e3,
    acts,
    out_sum,
    back_sum,
    keep_sem,
    send,
    recv,
):
    place = Place()
    links = Links(place, send, recv)
    plan = Plan()
    rows, depth = parts_hbm.shape[0] // 3, parts_hbm.shape[1]
    tile = rows // 2
    weights, edges = (w0, w1, w2, w3), (e0, e1, e2, e3)
    quarter = sum(PARTS)
    offsets = [sum(PARTS[:k]) for k in range(len(PARTS))]

    def columns(first, count):
        return lambda z, y, c, x: wm.at[z, y, c, x, :, pl.ds(first, count)]

    mixers = [
        Gather(links, columns(depth * j, depth), stages)
        for j, stages in MIXER
    ]
    gathers, reduces = [], []
    for number, (w, r, l) in enumerate(zip(weights, (r0, r1, r2, r3), (l0, l1, l2, l3))):
        view = lambda z, y, c, x, w=w: w.at[z, y]
        if KINDS[number] == "y":
            gathers.append(PairGather(links, w))
        else:
            gathers.append(Gather(links, view, ["y"]))
        if GRAD_KINDS[number] == "y":
            reduces.append(PairReduce(links, w, r, l))
        else:
            reduces.append(Reduce(links, view, ["y"], [r], l))

    def sides(number, quarter_index):
        width = PARTS[number]
        start = pl.multiple_of(quarter_index * quarter + offsets[number], 128)
        return [
            (ref.at[:, pl.ds(start, width)], pl.ds(side * width, width))
            for side, ref in enumerate((gate_ref, up_ref, down_ref))
        ]

    twins = [
        [
            links.copy(
                source,
                weights[number].at[place.z, place.y, place.c, :, where],
                links.take(1),
                "c",
            )
            for source, where in sides(number, 1 - place.c)
        ]
        for number in range(len(PARTS))
    ]


    def share(ref):
        first = links.take(3)
        return (
            links.copy(ref[0], ref[1], first, "c"),
            links.copy(ref[0], ref[2], first + 1, "x"),
            links.copy(ref[2], ref[3], first + 2, "c"),
        )

    shared_grads = [
        share([grads.at[i // 2, 2 * (i % 2) + h, q] for i in range(4)])
        for h in range(2)
        for q in range(2)
    ]
    shared_tokens = [
        share([tokens.at[i // 2, 2 * (i % 2) + h] for i in range(4)]) for h in range(2)
    ]
    edge = links.copy(
        product.at[pl.ds(rows, 8)], product.at[pl.ds(0, 8)], links.take(1), "next"
    )
    back_edge = links.copy(
        middle.at[pl.ds(0, 8)], middle.at[pl.ds(rows, 8)], links.take(1), "prev"
    )
    has_next, has_prev = place.s < place.last, place.s > 0
    slots = [
        wm.at[pl.ds(2 * (i // 4), 2), :, :, :, :, pl.ds(depth * (i % 4), depth)]
        for i in range(6)
    ]

    def give_back(total, slots):
        first = links.take(3)
        return (
            links.copy(total.at[3], slots[2], first, "c"),
            links.copy(total.at[2], slots[1], first + 1, "x"),
            links.copy(total.at[1], slots[0], first + 2, "c"),
        )

    returned = [give_back(back_sum, slots[:3]), give_back(out_sum, slots[3:])]
    trades = [
        links.copy(w.at[place.z, place.y, 1 - place.c], e, links.take(1), "c")
        for w, e in zip(weights, edges)
    ]

    count = iter(range(keep_sem.shape[0]))

    def local(source, target):
        return pltpu.make_async_copy(source, target, keep_sem.at[next(count)])

    parts = acts.at[pl.ds(0, 3 * rows), pl.ds(0, depth)]
    save_mixer = local(wm, mixer_hbm)
    save_parts = local(parts, parts_hbm)
    save_middle = local(middle.at[pl.ds(0, rows)], middle_hbm)
    fills = [
        [
            local(source, weights[number].at[place.z, place.y, place.c, :, where])
            for source, where in sides(number, place.c)
        ]
        for number in range(len(PARTS))
    ]
    mine = wm.at[place.z, place.y, place.c, place.x]
    fill_in = local(in_ref, mine.at[:, pl.ds(0, 3 * depth)])
    fill_out = local(out_ref, mine.at[:, pl.ds(3 * depth, depth)])
    inner = pl.ds(0, rows)
    low_x, high_x = out_sum.at[1], back_sum.at[0]
    view = (2,) + tokens.shape[2:]
    load_x = [local(x_ref, x) for x in (low_x, high_x)]
    load_grad = local(grad_ref, grads.at[0, pl.ds(0, 2)])
    load_grad_rows = local(grad_rows_ref, acts.at[pl.ds(3 * rows, rows), pl.ds(0, depth)])
    save_result = local(back_sum.at[1], result_ref)
    blocks = [tokens.at[0], tokens.at[1], grads.at[0], grads.at[1]]
    load_mixer = [
        local(mixer_hbm.at[:, :, :, :, :, pl.ds(depth * j, depth)], block)
        for j, block in enumerate(blocks)
    ]
    load_parts = local(parts_hbm, parts)
    load_middle = local(middle_hbm, product.at[pl.ds(8, rows)])
    staging = [acts.at[pl.ds(2 * rows * i, 2 * rows), pl.ds(depth, 2 * tile)] for i in range(2)]
    stores = [
        local(staging[j % 2], mixer_grad.at[:, pl.ds(2 * tile * ((j + 6) % 8), 2 * tile)])
        for j in range(8)
    ]
    save_grad, save_inputs = (
        local(middle.at[pl.ds(0, rows)], input_grad) for _ in range(2)
    )
    load_back = local(input_grad, middle.at[pl.ds(0, rows)])

    def hear(*copies):
        for copy in copies:
            copy.wait_recv()

    def begin(*copies):
        for copy in copies:
            copy.start()

    def done(*copies):
        for copy in copies:
            copy.wait()

    def valid_rows(first, count):
        position = place.s * rows + first + lax.broadcasted_iota(
            jnp.int32, (count, 1), 0
        )
        return (position < length_ref[0]).astype(F32)

    def open_all():
        for copy in [fill_in, fill_out, load_x[0], load_grad] + sum(fills, []):
            copy.start()
        place.greet(["c", "y", "x", "up", "down", "next", "prev"])
        fill_in.wait()
        fill_out.wait()

    def clear():
        @pl.when(place.s == 0)
        def _():
            product[pl.ds(0, 8)] = jnp.zeros((8, depth), F32)

        @pl.when(place.s == place.last)
        def _():
            middle[pl.ds(rows, 8)] = jnp.zeros((8, depth), F32)

    def first_norm(source, target):
        x = source[...].reshape(rows, depth).astype(F32)
        scale = lax.rsqrt(mean_of(x * x) + epsilon)
        normed = (x * scale * vectors_ref[0:1]).astype(BF16)
        target[...] = normed.reshape(view)

    def mask_grads():
        masked = grads[0, pl.ds(0, 2)].reshape(rows, depth).astype(F32)
        masked *= valid_rows(0, rows)
        grads[0, pl.ds(0, 2)] = masked.astype(BF16).reshape(view)

    def project(index):
        weight = wm[..., depth * index : depth * (index + 1)].reshape(depth, depth)
        acts[rows * index : rows * (index + 1), :depth] = dot(
            out_sum[0].reshape(rows, depth), weight
        ).astype(BF16)

    def multiply():
        b_part = acts[:rows, :depth].astype(F32)
        v_part = acts[2 * rows : 3 * rows, :depth].astype(F32)
        product[pl.ds(8, rows)] = (b_part * v_part).astype(BF16).astype(F32)

    def conv_rows(start):
        total = 0.0
        for tap in range(3):
            first = start + 6 + tap
            total += vectors_ref[1 + tap : 2 + tap] * product[first : first + tile]
        return total

    def mix(index):
        start = tile * index
        where = slice(start, start + tile)
        c_part = acts[rows + start : rows + start + tile, :depth].astype(F32)
        gated = (c_part * conv_rows(start)).astype(BF16)
        weight = wm[..., 3 * depth :].reshape(depth, depth)
        x = low_x[index].reshape(tile, depth).astype(F32)
        total = x + valid_rows(start, tile) * dot(gated, weight)
        middle[where] = total
        scale = lax.rsqrt(mean_of(total * total) + epsilon)
        new = (total * scale * vectors_ref[4:5]).astype(BF16)
        tokens[0, index] = new.reshape(tokens.shape[2:])

    begun = set()

    def one_block(number, pair, i, carry):
        weight, width, spot = weights[number], PARTS[number], SPOTS[number]
        where = pl.ds(pl.multiple_of(rows * (2 * pair + i), rows), rows)
        gate_up = weight[..., : 2 * width].reshape(depth, 2 * width)
        both = dot(tokens[pair, pl.ds(2 * i, 2)].reshape(rows, depth), gate_up)
        gate, up = both[:, :width], both[:, width:]
        sigmoid = jax.nn.sigmoid(gate)
        silu = gate * sigmoid
        slope = sigmoid + silu * (1.0 - sigmoid)
        kept = (silu * up).astype(BF16)
        down = weight[..., 2 * width :].reshape(depth, width)
        grad_hidden = dot(grads[pair, pl.ds(2 * i, 2)].reshape(rows, depth), down)
        acts[where, spot : spot + width] = (grad_hidden * up * slope).astype(BF16)
        acts[where, spot + width : spot + 2 * width] = (grad_hidden * silu).astype(BF16)
        acts[where, spot + 2 * width : spot + 3 * width] = kept
        out_part = by_rows(kept, down)
        back_part = by_rows(acts[where, spot : spot + 2 * width], gate_up)
        shape = out_sum.shape[1:]
        index = 2 * pair + i
        if pair in begun:
            out_part += out_sum[index].reshape(rows, depth).astype(F32)
            back_part += back_sum[index].reshape(rows, depth).astype(F32)
        out_sum[index] = out_part.astype(BF16).reshape(shape)
        back_sum[index] = back_part.astype(BF16).reshape(shape)
        return carry

    def block(number, pair):
        lax.fori_loop(0, 2, functools.partial(one_block, number, pair), 0)
        begun.add(pair)

    def weigh(number):
        weight, width, spot = weights[number], PARTS[number], SPOTS[number]
        for source, first, size in ((tokens, 0, 2 * width), (grads, 2 * width, width)):
            step = size if size <= 512 else size // 2

            def column(i, carry):
                factor = acts[:, pl.ds(pl.multiple_of(spot + first + i * step, 128), step)]
                part = over_rows(source[...].reshape(4 * rows, depth), factor)
                where = pl.ds(pl.multiple_of(first + i * step, 128), step)
                weight[..., where] = part.astype(BF16).reshape(
                    weight.shape[:-1] + (step,)
                )
                return carry

            lax.fori_loop(0, size // step, column, 0)

    def lift(index):
        hear(returned[index][0])
        add_into((back_sum, out_sum)[index].at[2], slots[3 * index + 2])
        begin(returned[index][1])

    def returned_rows(index, start):
        total = (back_sum, out_sum)[index]
        i = start // tile
        found = total[0, i].reshape(tile, depth).astype(F32)
        for slot in slots[3 * index : 3 * index + 2]:
            found += slot[i].reshape(tile, depth).astype(F32)
        return found

    def note(row, values):
        total = jnp.sum(values, axis=0, keepdims=True)
        if ("row", row) in begun:
            total += small[row : row + 1]
        small[row : row + 1] = total
        begun.add(("row", row))

    def turn(index):
        start = tile * index
        where = slice(start, start + tile)
        part = returned_rows(0, start)
        total = middle[where]
        scale = lax.rsqrt(mean_of(total * total) + epsilon)
        hat = total * scale
        note(4, part * hat)
        scaled = part * vectors_ref[4:5]
        spot = slice(3 * rows + start, 3 * rows + start + tile)
        grad = acts[spot, :depth].astype(F32) + scale * (
            scaled - hat * mean_of(scaled * hat)
        )
        middle[where] = grad
        acts[spot, :depth] = (valid_rows(start, tile) * grad).astype(BF16)

    def unmix(index):
        start = tile * index
        spot = slice(rows + start, rows + start + tile)
        weight = grads[1].reshape(depth, depth)
        gated_grad = by_rows(
            acts[3 * rows + start : 3 * rows + start + tile, :depth], weight
        )
        c_part = acts[spot, :depth].astype(F32)
        conv = conv_rows(start)
        back_sum[3, index] = (c_part * conv).astype(BF16).reshape(tokens.shape[2:])
        acts[spot, :depth] = (gated_grad * conv).astype(BF16)
        conv_grad = gated_grad * c_part
        middle[start : start + tile] = conv_grad
        for tap in range(3):
            first = start + 6 + tap
            note(1 + tap, conv_grad * product[first : first + tile])

    def unconv(index):
        start = tile * index
        grad = 0.0
        for tap in range(3):
            first = start + 2 - tap
            grad += vectors_ref[1 + tap : 2 + tap] * middle[first : first + tile]
        b_spot = slice(start, start + tile)
        v_spot = slice(2 * rows + start, 2 * rows + start + tile)
        b_part = acts[b_spot, :depth].astype(F32)
        v_part = acts[v_spot, :depth].astype(F32)
        acts[b_spot, :depth] = (grad * v_part).astype(BF16)
        acts[v_spot, :depth] = (grad * b_part).astype(BF16)

    def project_back(index):
        start = tile * index
        where = slice(start, start + tile)
        part = 0.0
        for j in range(3):
            spot = slice(rows * j + start, rows * j + start + tile)
            part += by_rows(acts[spot, :depth], blocks[j][...].reshape(depth, depth))
        x = high_x[index].reshape(tile, depth).astype(F32)
        scale = lax.rsqrt(mean_of(x * x) + epsilon)
        hat = x * scale
        note(0, part * hat)
        scaled = part * vectors_ref[0:1]
        middle[where] = middle[where] + scale * (scaled - hat * mean_of(scaled * hat))

    def weigh_mixer(j):
        if j >= 2:
            stores[j - 2].wait()
        wide = 2 * tile
        if j >= 2:
            first = rows * (j // 2 - 1)
            left = back_sum[2].reshape(rows, depth)
        else:
            first = 3 * rows
            left = back_sum[3].reshape(rows, depth)
        start = wide * (j % 2)
        part = over_rows(left, acts[first : first + rows, start : start + wide])
        staging[j % 2][...] = part.astype(BF16)
        stores[j].start()

    def close_result():
        for index in range(2):
            start = tile * index
            total = product[8 + start : 8 + start + tile] + valid_rows(
                start, tile
            ) * returned_rows(1, start)
            back_sum[1, index] = total.astype(BF16).reshape(tokens.shape[2:])
        save_result.start()

    def own(number):
        width = PARTS[number]
        for side, target in enumerate((gate_grad, up_grad, down_grad)):
            spot = pl.ds(side * width, width)
            mine = pl.multiple_of(place.c * quarter + offsets[number], 128)
            twin = pl.multiple_of((1 - place.c) * quarter + offsets[number], 128)
            target[:, pl.ds(mine, width)] = weights[number][
                place.z, place.y, place.c, :, spot
            ]
            target[:, pl.ds(twin, width)] = edges[number][:, spot]

    def work_on(needs, action, *args):
        return plan.add(needs, action, *args, busy=True)

    start = plan.add([], open_all)
    for part in mixers:
        plan.add([start], part.along, 0)
        plan.add([start], part.depart, 0)
    for twin in twins:
        plan.add([start], begin, *twin)
    cleared = plan.add([start], clear)
    masked = plan.add([start], load_grad.wait)
    masked = work_on([masked], mask_grads)
    plan.add([masked], begin, *[group[0] for group in shared_grads])
    early = [plan.add([masked], begin, group[1]) for group in shared_grads[:EARLY]]
    norm = plan.add([start], load_x[0].wait)
    norm = work_on([norm], first_norm, low_x, out_sum.at[0])
    filled = [plan.add([start], done, *copies) for copies in fills]
    arrived = [
        plan.add([filled[number]], hear, *twins[number]) for number in range(len(PARTS))
    ]

    gone, whole, passed = [], {}, []
    for number, part in enumerate(mixers):
        last = {(0, 0): start}
        for distance in range(1, DEPTH):
            step = plan.add([start], part.along, distance)
            last[0, distance] = plan.add([step], part.depart, distance)
            passed += [step] * (distance == Z_GATE)
        for stage in range(3):
            for distance in range(DEPTH):
                last[stage + 1, distance] = plan.add(
                    [last[stage, distance]], part.across, stage, distance
                )
        gone += [last[stage, d] for stage in (0, 1) for d in range(DEPTH)]
        whole[MIXER[number][0]] = list(last.values())

    ready = {}
    z_gate, y_gate = [start] + passed, list(gone)
    pair_opening = passed if PAIR_EARLY else gone
    pair_gate = {}
    for number in PAIRS:
        pair_gate[number] = [plan.add([arrived[number]] + pair_opening, gathers[number].begin)]
    for number in ORDER:
        part = gathers[number]
        opening = part.join if KINDS[number] == "y" else functools.partial(part.along, 0)
        found = [plan.add([arrived[number]] + z_gate + pair_gate.get(number, []), opening)]
        for distance in range(1, DEPTH):
            found.append(plan.add(found[-1:], part.along, distance))
        z_gate = found[1:2]
        if KINDS[number] == "z":
            sends = [
                plan.add([found[distance]] + y_gate, part.depart, distance)
                for distance in range(DEPTH)
            ]
            y_gate = sends[2:3]
            last_sends = sends
            found += sends
            found += [
                plan.add([sends[distance]], part.across, 0, distance)
                for distance in range(DEPTH)
            ]
        ready[number] = found

    y_gate = last_sends

    x_free = early + [
        plan.add(gone, begin, group[1]) for group in shared_grads[EARLY:]
    ]
    b_step = work_on(whole[0] + [norm], project, 0)
    v_step = work_on(whole[2] + [norm], project, 2)
    times = work_on([b_step, v_step], multiply)

    def send_edge():
        pl.when(has_next)(edge.start)

    def take_edge():
        pl.when(has_prev)(edge.wait_recv)

    def edge_sent():
        pl.when(has_next)(edge.wait_send)

    sent = plan.add([times], send_edge)
    c_step = work_on(whole[1] + [times], project, 1)
    saving = plan.add([c_step], begin, save_parts)
    late_mix = work_on(whole[3] + [c_step, sent], mix, 1)
    drained = plan.add([late_mix], lambda: [part.drain() for part in mixers])
    saved = plan.add([drained], begin, save_mixer)
    token_sends = {}
    token_sends[1] = plan.add([late_mix] + x_free, begin, *shared_tokens[1][1::-1])
    edge_in = plan.add([sent, cleared], take_edge)
    mixed = work_on([edge_in, late_mix], mix, 0)
    kept = plan.add([mixed, saved], lambda: (save_middle.start(), save_mixer.wait()))
    token_sends[0] = plan.add([kept, token_sends[1]], begin, *shared_tokens[0][1::-1])

    grads_x, tokens_x = [], []

    def pass_grads(group):
        hear(group[1])
        begin(group[2])

    for step, group in zip(x_free, shared_grads):
        grads_x.append(plan.add([step], pass_grads, group))
    for h in (1, 0):
        group = shared_tokens[h]

        def pass_on(group=group):
            hear(group[1])
            begin(group[2])

        tokens_x.append(plan.add([token_sends[h]], pass_on))
    near = plan.add(
        [token_sends[0], masked],
        hear,
        *[group[0] for group in shared_grads + shared_tokens],
    )
    far = plan.add(
        tokens_x + grads_x, hear, *[group[2] for group in shared_grads + shared_tokens]
    )
    def flush():
        done(save_parts, save_middle)
        edge_sent()

    flushed = plan.add([kept, mixed, saving], flush)
    own_side, other_side = [near, flushed], [near, far, flushed]
    blocks_done = {}
    weighed = {}
    reduced = {}
    previous = []

    def reduce_steps(number, needs):
        part = reduces[number]
        if GRAD_KINDS[number] == "y":
            chain = list(needs)
            steps = []
            for distance in (3, 2, 1, 0):
                chain = [plan.add(chain, part.along, distance)]
                steps += chain
            chain = [plan.add(chain, lambda: part.final().start())]
            steps.append(plan.add(chain, part.finish))
            return steps
        steps = []
        opened = {
            distance: plan.add(needs + y_gate, part.begin, distance)
            for distance in (3, 2, 1, 0)
        }
        chain = []
        for distance in (3, 2, 1, 0):
            step = plan.add([opened[distance]], part.across, 0, distance)
            chain = [plan.add([step] + chain, part.along, distance)]
            steps += [step] + chain
        return steps

    def drain_and_weigh(number, needs):
        drain = plan.add(needs, gathers[number].drain)
        weighed[number] = work_on([drain], weigh, number)
        reduced[number] = reduce_steps(number, [weighed[number]])

    def columns_of(number):
        return set(range(SPOTS[number], SPOTS[number] + 3 * PARTS[number], 128))

    def run_block(number, pair):
        needs = [
            weighed[other]
            for other in ORDER[: ORDER.index(number)]
            if columns_of(other) & columns_of(number)
        ]
        blocks_done[number, pair] = work_on(
            ready[number] + (other_side if pair else own_side) + needs, block, number, pair
        )

    def finish_part(number):
        drain_and_weigh(number, [blocks_done[number, 0], blocks_done[number, 1]])

    first, second, third, fourth = ORDER
    for number in (first, second):
        if not columns_of(first) & columns_of(second):
            run_block(number, 0)
    for number in (first, second):
        if columns_of(first) & columns_of(second):
            run_block(number, 0)
        run_block(number, 1)
        finish_part(number)
    run_block(third, 1)
    run_block(fourth, 1)
    last_far = [blocks_done[third, 1], blocks_done[fourth, 1]]
    back_up = plan.add(last_far, begin, returned[0][0])
    out_up = plan.add([back_up], begin, returned[1][0])
    back_over = plan.add([back_up], lift, 0)
    run_block(third, 0)
    run_block(fourth, 0)
    near_done = [blocks_done[third, 0], blocks_done[fourth, 0]]
    back_near = plan.add(near_done + [back_over], begin, returned[0][2])
    out_over = plan.add([out_up, back_over], lift, 1)
    out_near = plan.add([back_near, out_over], begin, returned[1][2])
    finish_part(third)
    finish_part(fourth)

    def sent_tokens():
        for group in shared_grads + shared_tokens:
            for copy in group:
                copy.wait_send()

    freed = plan.add([weighed[number] for number in ORDER], sent_tokens)
    loads = plan.add(
        [freed], begin, load_parts, load_grad_rows, *load_mixer
    )
    back_in = plan.add([back_near], hear, returned[0][1], returned[0][2])
    loaded = plan.add([loads], done, load_parts, load_grad_rows, *load_mixer)
    turned = [work_on([back_in, loaded], turn, index) for index in range(2)]

    def free_sums():
        done(save_grad)
        for copy in returned[0]:
            copy.wait_send()
        load_x[1].start()

    freed = plan.add(turned, save_grad.start)
    freed = plan.add([freed], free_sums)
    unmixed = [work_on([freed], unmix, index) for index in range(2)]
    again = plan.add([freed], load_x[1].wait)
    again = work_on([again], first_norm, high_x, back_sum.at[2])

    def send_back():
        pl.when(has_prev)(back_edge.start)

    def take_back():
        pl.when(has_next)(back_edge.wait_recv)

    def back_sent():
        pl.when(has_prev)(back_edge.wait_send)

    back_edge_sent = plan.add([unmixed[0]], send_back)
    weigh_steps = [work_on(unmixed, weigh_mixer, 0)]
    weigh_steps.append(work_on(unmixed + weigh_steps, weigh_mixer, 1))
    low = work_on([unmixed[1], back_edge_sent], unconv, 0)
    taken = plan.add([back_edge_sent], take_back)
    high = work_on([taken, low], unconv, 1)
    fetched = plan.add([low, high] + [edge_in], begin, load_middle)
    for j in range(2, 8):
        weigh_steps.append(work_on([again, low, high, weigh_steps[-1]], weigh_mixer, j))
    revived = plan.add([low, high], lambda: (back_sent(), load_back.start()))
    revived = plan.add([revived, weigh_steps[-1]], load_back.wait)
    projected = [work_on([revived], project_back, index) for index in range(2)]
    stored = plan.add(projected, begin, save_inputs)
    def finish_result():
        load_middle.wait()
        close_result()

    out_in = plan.add([out_near, fetched], hear, returned[1][1], returned[1][2])
    finished = work_on([out_in, fetched] + weigh_steps, finish_result)

    finals = []
    for number in ORDER:
        trade = plan.add(reduced[number], begin, trades[number])
        heard = plan.add([trade], hear, trades[number])
        finals.append(work_on([heard], own, number))

    def close():
        small[pl.ds(5, 3)] = jnp.zeros((3, depth), F32)
        done(save_inputs, save_result, *stores[6:8])
        for reduce in reduces:
            reduce.drain()
        for group in returned[1:] + twins + [trades]:
            for copy in group:
                copy.wait_send()

    plan.add(finals + weigh_steps + projected + [stored, finished], close)
    plan.run(STEPS or list(range(len(plan.steps))))


def layer(lengths, inputs, cotangent, vectors, shards):
    rows, depth = inputs.shape
    ffn_columns = shards[2].shape[1]
    vmem = pl.BlockSpec(memory_space=pltpu.VMEM)
    hbm = pl.BlockSpec(memory_space=pl.ANY)
    shape = jax.ShapeDtypeStruct
    blocks = (DEPTH, 2, 2, 2, depth // (8 * DEPTH))
    half = (2, 2, 2, 2, rows // 16, depth)
    out_shape = [
        shape(blocks + (4 * depth,), BF16),
        shape((3 * rows, depth), BF16),
        shape((rows, depth), F32),
        shape((depth, 4 * depth), BF16),
        shape((8, depth), F32),
        shape(half, BF16),
        shape((rows, depth), F32),
    ] + [shape((64, ffn_columns), BF16)] * 3
    pair = (2, 64)
    widths = [3 * w for w in PARTS]

    def slots(lead, width, kind):
        if kind == "y":
            return (lead, 2) if lead > DEPTH else ()
        return (lead,)

    token = (2, 4, 2, 2, 2, 32, depth)
    total = (4, 2, 2, 2, 2, 32, depth)
    scratch = (
        [pltpu.VMEM(blocks + (4 * depth,), BF16)]
        + [pltpu.VMEM((DEPTH, 2) + pair + (w,), BF16) for w in widths]
        + [
            pltpu.VMEM((rows + 8, depth), F32),
            pltpu.VMEM((rows + 8, depth), F32),
        ]
        + [pltpu.VMEM(token, BF16)] * 2
        + [
            pltpu.VMEM(slots(lead, w, kind) + pair + (w,), BF16)
            for lead in (DEPTH, DEPTH + 1)
            for w, kind in zip(widths, GRAD_KINDS)
        ]
        + [pltpu.VMEM((64, w), BF16) for w in widths]
        + [pltpu.VMEM((4 * rows, ACTS), BF16)]
        + [pltpu.VMEM(total, BF16)] * 2
        + [
            pltpu.SemaphoreType.DMA((40,)),
            pltpu.SemaphoreType.DMA((240,)),
            pltpu.SemaphoreType.DMA((240,)),
        ]
    )
    smem = pl.BlockSpec(memory_space=pltpu.SMEM)
    return pl.pallas_call(
        layer_kernel,
        out_shape=out_shape,
        in_specs=[smem] + [hbm] * 3 + [vmem] + [hbm] * 5,
        out_specs=[hbm] * 4 + [vmem, hbm, hbm] + [vmem] * 3,
        scratch_shapes=scratch,
        compiler_params=pltpu.CompilerParams(
            collective_id=0, has_side_effects=True, vmem_limit_bytes=63 * 2**20
        ),
    )(
        lengths,
        inputs.reshape(half),
        cotangent.reshape(half),
        cotangent,
        vectors,
        *shards
    )


def reduce_kernel(
    grad_ref, small_ref, in_grad, out_grad, one_ref, taps_ref, two_ref, work, small, *rest
):
    slots, (load_sem, send, recv) = rest[:-3], rest[-3:]
    place = Place()
    links = Links(place, send, recv)
    plan = Plan()
    depth = in_grad.shape[1] // 3
    parts = []
    remaining = list(slots)
    for j, before, after in MIXER_GRADS:
        where = pl.ds(depth * j, depth)
        count = len(before) + 1 + len(after)
        mine, remaining = remaining[:count], remaining[count:]
        parts.append(
            Reduce(
                links,
                lambda z, y, c, x, where=where: work.at[z, y, x, :, where],
                before,
                mine[: len(before)] + mine[len(before) + 1 :],
                mine[len(before)],
                after,
                lambda z, y, c, x, where=where: grad_ref.at[z, y, c, x, :, where],
            )
        )
    loads = [
        pltpu.make_async_copy(
            grad_ref.at[:, :, place.c, :, :, pl.ds(depth * j, depth)],
            work.at[:, :, :, :, pl.ds(depth * j, depth)],
            load_sem.at[number],
        )
        for number, (j, _, _) in enumerate(MIXER_GRADS)
    ]
    ring = ("c", "x", "y", "pair", "far")
    first = links.take(len(ring))
    rounds = [
        links.copy(small.at[i], small.at[len(ring) + 1 + i], first + i, name)
        for i, name in enumerate(ring)
    ]

    def open_all():
        for load in loads:
            load.start()
        place.greet(["c", "y", "x", "up", "down", "far"])
        small[0] = small_ref[...]

    start = plan.add([], open_all)
    opened = [
        [plan.add([start], part.begin, distance) for distance in (3, 2, 1, 0)]
        for part in parts
    ]
    ends = []
    for part, load, begun in zip(parts, loads, opened):
        loaded = plan.add([start], load.wait)
        line = []
        for number, distance in enumerate((3, 2, 1, 0)):
            step = plan.add([loaded, begun[number]], part.across, 0, distance)
            for stage in range(1, part.before):
                step = plan.add([step], part.across, stage, distance)
            line = [plan.add([step] + line, part.along, distance)]
        for stage in range(part.before, len(part.stages)):
            line = [plan.add(line, part.late_start, stage)]
            line = [plan.add(line, part.late_take, stage)]
        ends += line

    def add_round(number):
        rounds[number].wait_recv()
        small[number + 1] = small[number] + small[len(ring) + 1 + number]

    step = plan.add(sum(opened, []), rounds[0].start)
    for number in range(len(ring)):
        step = plan.add([step], add_round, number)
        if number + 1 < len(ring):
            step = plan.add([step], rounds[number + 1].start)

    def close():
        one_ref[...] = small[len(ring), 0:1]
        taps_ref[...] = small[len(ring), 1:4]
        two_ref[...] = small[len(ring), 4:5]
        own = work[place.z, place.y, place.x].astype(F32)
        in_grad[...] = own[:, : 3 * depth]
        out_grad[...] = own[:, 3 * depth :]
        for part in parts:
            part.drain()
        for copy in rounds:
            copy.wait_send()

    plan.add(ends + [step], close)
    plan.run(LAST_STEPS or list(range(len(plan.steps))))


def reduce_all(grad, small):
    columns = grad.shape[-1]
    depth = columns // 4
    block = (grad.shape[-2], depth)
    slots = []
    for _, before, after in MIXER_GRADS:
        left = len(before) + len(after)
        for _ in before:
            left -= 1
            slots.append((DEPTH,) + (2,) * left + block)
        slots.append((DEPTH + 1,) + (2,) * left + block)
        for _ in after:
            left -= 1
            slots.append((2,) * left + block)
    vmem = pl.BlockSpec(memory_space=pltpu.VMEM)
    hbm = pl.BlockSpec(memory_space=pl.ANY)
    return pl.pallas_call(
        reduce_kernel,
        out_shape=[
            jax.ShapeDtypeStruct((block[0], 3 * depth), F32),
            jax.ShapeDtypeStruct((block[0], depth), F32),
        ]
        + [jax.ShapeDtypeStruct((rows, depth), F32) for rows in (1, 3, 1)],
        in_specs=[hbm, vmem],
        out_specs=[vmem] * 5,
        scratch_shapes=[
            pltpu.VMEM((DEPTH, 2, 2) + block[:1] + (columns,), BF16),
            pltpu.VMEM((11,) + small.shape, F32),
        ]
        + [pltpu.VMEM(slot, BF16) for slot in slots]
        + [
            pltpu.SemaphoreType.DMA((len(MIXER_GRADS),)),
            pltpu.SemaphoreType.DMA((96,)),
            pltpu.SemaphoreType.DMA((96,)),
        ],
        compiler_params=pltpu.CompilerParams(
            collective_id=2, has_side_effects=True, vmem_limit_bytes=58 * 2**20
        ),
    )(grad, small)


def shifted(block, axis, distance):
    devices = range(lax.axis_size(axis))
    route = [(i - distance, i) for i in devices if i - distance in devices]
    return lax.ppermute(block, axis, route)


def mixer_forward(inputs, lengths, norm_one_gain, conv_weight, norm_two_gain, in_all, out_all):
    tok_rows, feat_width = inputs.shape[1:]
    kept = {}
    x_float = inputs[0].astype(F32)
    kernel = conv_weight.astype(F32)
    position = lax.axis_index("seq") * tok_rows + lax.iota(jnp.int32, tok_rows)
    valid_mask = (position < lengths[0]).astype(F32)[:, None]
    scale_one = lax.rsqrt(jnp.mean(x_float * x_float, axis=1, keepdims=True) + epsilon)
    hat_one = x_float * scale_one
    normed_one = (hat_one * norm_one_gain.astype(F32)).astype(BF16)
    projected = rounded_dot(normed_one, in_all)
    b_part = projected[:, :feat_width]
    c_part = projected[:, feat_width : 2 * feat_width]
    v_part = projected[:, 2 * feat_width :]
    product = (b_part * v_part).astype(BF16)
    carried = shifted(product[tok_rows - 2 :], "seq", 1)
    extended = jnp.concatenate([carried, product], axis=0).astype(F32)
    conv_out = (
        kernel[0] * extended[:tok_rows]
        + kernel[1] * extended[1 : tok_rows + 1]
        + kernel[2] * extended[2:]
    )
    gated_mix = (c_part * conv_out).astype(BF16)
    mixer_out = rounded_dot(gated_mix, out_all)
    middle = x_float + valid_mask * mixer_out
    scale_two = lax.rsqrt(jnp.mean(middle * middle, axis=1, keepdims=True) + epsilon)
    hat_two = middle * scale_two
    normed_two = (hat_two * norm_two_gain.astype(F32)).astype(BF16)
    kept.update(locals())
    return kept


def mixer_backward(kept, grad_out, normed_part, norm_one_gain, norm_two_gain, in_all, out_all):
    tok_rows, feat_width = grad_out.shape
    kernel = kept["kernel"]
    extended, conv_out = kept["extended"], kept["conv_out"]
    hat_one, hat_two = kept["hat_one"], kept["hat_two"]
    grad_gain_two = jnp.sum(normed_part * hat_two, axis=0)
    scaled_two = normed_part * norm_two_gain.astype(F32)
    grad_middle = grad_out + kept["scale_two"] * (
        scaled_two - hat_two * jnp.mean(scaled_two * hat_two, axis=1, keepdims=True)
    )
    grad_mix = (kept["valid_mask"] * grad_middle).astype(BF16)
    grad_out_w = over_rows(kept["gated_mix"], grad_mix)
    grad_gated = by_rows(grad_mix, out_all)
    grad_c = grad_gated * conv_out
    grad_conv_in = grad_gated * kept["c_part"]
    grad_kernel = jnp.stack(
        [
            jnp.sum(grad_conv_in * extended[:tok_rows], axis=0),
            jnp.sum(grad_conv_in * extended[1 : tok_rows + 1], axis=0),
            jnp.sum(grad_conv_in * extended[2:], axis=0),
        ]
    )
    padded_grad = jnp.pad(grad_conv_in, ((2, 2), (0, 0)))
    grad_extended = (
        kernel[0] * padded_grad[2 : tok_rows + 4]
        + kernel[1] * padded_grad[1 : tok_rows + 3]
        + kernel[2] * padded_grad[: tok_rows + 2]
    )
    returned = shifted(grad_extended[:2], "seq", -1)
    grad_product = grad_extended[2:] + jnp.concatenate(
        [jnp.zeros((tok_rows - 2, feat_width), F32), returned], axis=0
    )
    grad_projected = jnp.concatenate(
        [grad_product * kept["v_part"], grad_c, grad_product * kept["b_part"]], axis=1
    ).astype(BF16)
    grad_in_w = over_rows(kept["normed_one"], grad_projected)
    grad_normed_one = by_rows(grad_projected, in_all)
    grad_gain_one = jnp.sum(grad_normed_one * hat_one, axis=0)
    scaled_one = grad_normed_one * norm_one_gain.astype(F32)
    grad_inputs = grad_middle + kept["scale_one"] * (
        scaled_one - hat_one * jnp.mean(scaled_one * hat_one, axis=1, keepdims=True)
    )
    return grad_inputs, grad_in_w, grad_out_w, grad_gain_one, grad_kernel, grad_gain_two


def in_blocks(
    inputs,
    lengths,
    norm_one_gain,
    w_in,
    conv_weight,
    w_out,
    norm_two_gain,
    w_gate,
    w_up,
    w_down,
    cotangent,
):
    width = inputs.shape[2]
    vectors = jnp.concatenate(
        [
            norm_one_gain.astype(F32)[None],
            conv_weight.astype(F32),
            norm_two_gain.astype(F32)[None],
        ]
    )
    found = layer(
        lengths,
        inputs[0],
        cotangent[0],
        vectors,
        (w_in, w_out, w_gate, w_up, w_down.T),
    )
    mixer_grad, small, result, grad_inputs, gate, up, down = found[3:]
    in_grad, out_grad, one, taps, two = reduce_all(
        mixer_grad.reshape(DEPTH, 2, 2, 2, 32, 4 * width), small
    )
    return (
        result.reshape(inputs.shape),
        grad_inputs[None],
        one[0],
        in_grad,
        taps,
        out_grad,
        two[0],
        gate.astype(F32),
        up.astype(F32),
        down.T.astype(F32),
    )


def anywhere(
    inputs,
    lengths,
    norm_one_gain,
    w_in,
    conv_weight,
    w_out,
    norm_two_gain,
    w_gate,
    w_up,
    w_down,
    cotangent,
):
    both = ("seq", "batch")
    in_all = lax.all_gather(w_in, both, axis=0, tiled=True)
    out_all = lax.all_gather(w_out, both, axis=0, tiled=True)
    gate_use, up_use = (
        lax.all_gather(
            lax.all_gather(w, "seq", axis=0, tiled=True), "batch", axis=1, tiled=True
        )
        for w in (w_gate, w_up)
    )
    down_use = lax.all_gather(
        lax.all_gather(w_down, "seq", axis=1, tiled=True), "batch", axis=0, tiled=True
    )
    kept = mixer_forward(
        inputs, lengths, norm_one_gain, conv_weight, norm_two_gain, in_all, out_all
    )
    rows_norm = kept["normed_two"]
    grad_out = cotangent[0].astype(F32)
    rows_grad = (kept["valid_mask"] * grad_out).astype(BF16)
    gate_val = rounded_dot(rows_norm, gate_use)
    up_val = rounded_dot(rows_norm, up_use)
    hidden = (jax.nn.silu(gate_val) * up_val).astype(BF16)
    ffn_out = rounded_dot(hidden, down_use)
    result = (kept["middle"] + kept["valid_mask"] * ffn_out).astype(BF16)
    grad_down = over_rows(hidden, rows_grad)
    grad_hidden = by_rows(rows_grad, down_use)
    sigmoid_gate = jax.nn.sigmoid(gate_val)
    slope_gate = sigmoid_gate * (1.0 + gate_val * (1.0 - sigmoid_gate))
    grad_gate = (grad_hidden * up_val * slope_gate).astype(BF16)
    grad_up = (grad_hidden * gate_val * sigmoid_gate).astype(BF16)
    grad_gate_w = over_rows(rows_norm, grad_gate)
    grad_up_w = over_rows(rows_norm, grad_up)
    normed_part = by_rows(grad_gate, gate_use) + by_rows(grad_up, up_use)

    def owned(grad, axis):
        half = lax.psum_scatter(
            grad.astype(BF16), "batch", scatter_dimension=axis, tiled=True
        ).astype(F32)
        return lax.psum_scatter(half, "seq", scatter_dimension=1 - axis, tiled=True)

    shards = owned(grad_gate_w, 1), owned(grad_up_w, 1), owned(grad_down, 0)
    grad_inputs, grad_in_w, grad_out_w, gain_one, taps, gain_two = mixer_backward(
        kept, grad_out, normed_part, norm_one_gain, norm_two_gain, in_all, out_all
    )
    shard_in, shard_out = (
        lax.psum_scatter(grad, both, scatter_dimension=0, tiled=True)
        for grad in (grad_in_w, grad_out_w)
    )
    total_one, total_two, total_kernel = lax.psum((gain_one, gain_two, taps), both)
    return (
        result[None],
        grad_inputs[None],
        total_one,
        shard_in,
        total_kernel,
        shard_out,
        total_two,
    ) + shards


def solution(mesh):
    in_specs = (
        P("batch", "seq", None),
        P("batch"),
        P(),
        P(("seq", "batch"), None),
        P(),
        P(("seq", "batch"), None),
        P(),
        P("seq", "batch"),
        P("seq", "batch"),
        P("batch", "seq"),
        P("batch", "seq", None),
    )
    out_specs = (
        P("batch", "seq", None),
        P("batch", "seq", None),
        P(),
        P(("seq", "batch"), None),
        P(),
        P(("seq", "batch"), None),
        P(),
        P("seq", "batch"),
        P("seq", "batch"),
        P("batch", "seq"),
    )
    by_blocks = mesh.shape["seq"] == 4 * DEPTH and mesh.shape["batch"] == 2
    return jax.shard_map(
        in_blocks if by_blocks else anywhere,
        mesh=mesh,
        in_specs=in_specs,
        out_specs=out_specs,
        check_vma=False,
    )
```
